32 devices in a mesh: dp: 8 (over z, x), seq: 4 (over y, core).
Axes of the slice: x: 2, y: 2, z: 4, core: 2. Of those that a mesh axis runs over, the one named last changes fastest.
Arguments:
- layer_in: float32 [16, 512, 768], P('dp', 'seq'), may hold values from -6 to 6
- lengths: int32 [16], P('dp'), may hold values from 64 to 512, as said below
- op_ids: int32 [8, 2], P('dp'), may hold values from 0 to 2, as said below
- kernel_ids: int32 [8, 2], P('dp'), may hold values from 0 to 2, as said below
- attn_proj: bfloat16 [2, 3, 768, 768], replicated, may hold values from -0.21875 to 0.21875
- attn_out: bfloat16 [2, 768, 768], replicated, may hold values from -0.625 to 0.625
- ffn_in: bfloat16 [2, 768, 3072], replicated, may hold values from -0.21875 to 0.21875
- ffn_out: bfloat16 [2, 3072, 768], replicated, may hold values from -0.109375 to 0.109375
- point_weights: bfloat16 [2, 768, 768], replicated, may hold values from -0.21875 to 0.21875
- depth_weights: float32 [2, 7, 768], replicated, may hold values from -3 to 3
- norm_gains: float32 [2, 768], replicated, may hold values from 0.5 to 1.5
- norm_shifts: float32 [2, 768], replicated, may hold values from -2 to 2
- cotangent: float32 [16, 512, 768], P('dp', 'seq'), may hold values from -6 to 6
Outputs:
- layer_out: float32 [16, 512, 768], P('dp', 'seq')
- input_grad: float32 [16, 512, 768], P('dp', 'seq')
- attn_proj_grad: float32 [2, 3, 768, 768], P(None, None, 'seq', 'dp')
- attn_out_grad: float32 [2, 768, 768], P(None, 'seq', 'dp')
- ffn_in_grad: float32 [2, 768, 3072], P(None, 'seq', 'dp')
- ffn_out_grad: float32 [2, 3072, 768], P(None, 'seq', 'dp')
- point_grad: float32 [2, 768, 768], P(None, 'seq', 'dp')
- depth_grad: float32 [2, 7, 768], replicated
- gain_grad: float32 [2, 768], replicated
- shift_grad: float32 [2, 768], replicated
The draws below stay inside these ranges and needn't reach their ends.
Inputs may be any that keep to these rules, and one draw needn't show every extreme that they name: `lengths`: each data group holds one slot of length 512; other slots are mostly short. `op_ids`: 0 is attention, 1 separable convolution, 2 feed-forward; in every block each op is taken by some data group. `kernel_ids`: the kernel has 3 + 2 * value taps and matters where the op is 1; in every block some group with op 1 has value 2.
All inputs are finite; a program needn't handle non-finite values.
Results may differ from the reference program's by a relative error of at most 0.017.
Values may be sent and summed in bfloat16 or wider, within the bound.
No kernel may reach another device: no remote copies, remote signals or barrier semaphores. Data moves between devices by JAX's collectives and lax.ppermute only.
A program may use at most 320 MiB of HBM per device.

```python
import jax
import jax.numpy as jnp
from jax import lax

D = 768
HEADS = 12
HEAD = 64
FF = 3072
TAPS = 7
BLOCKS = 2
LEN = 512
SHORT = 64
SLOT_DEV = 2
GROUPS = 8
SLOTS = 16


def path_draw(key):
    op_key = jax.random.fold_in(key, 17)
    choose = jax.random.randint(jax.random.fold_in(op_key, 1), (GROUPS, BLOCKS), 0, 3)
    kernel = jax.random.randint(jax.random.fold_in(op_key, 2), (GROUPS, BLOCKS), 0, 3)
    for block_index in range(BLOCKS):
        order = jax.random.permutation(jax.random.fold_in(op_key, 10 + block_index), GROUPS)
        choose = choose.at[order[:3], block_index].set(jnp.arange(3, dtype=jnp.int32))
        kernel = kernel.at[order[1], block_index].set(2)
    return (choose.astype(jnp.int32), kernel.astype(jnp.int32))


def draw_op_ids(key, part):
    choose, kernel = path_draw(key)
    return choose


def draw_kernel_ids(key, part):
    choose, kernel = path_draw(key)
    return kernel


def draw_lengths(key, part):
    key = jax.random.fold_in(key, 5)
    span_size = LEN - SHORT + 1
    draw_one = jax.random.randint(jax.random.fold_in(key, 1), (SLOTS,), 0, span_size)
    draw_two = jax.random.randint(jax.random.fold_in(key, 2), (SLOTS,), 0, span_size)
    slot_lengths = SHORT + draw_one * draw_two // span_size
    longest = jax.random.randint(jax.random.fold_in(key, 3), (GROUPS,), 0, SLOT_DEV)
    long_rows = jnp.arange(GROUPS, dtype=jnp.int32) * SLOT_DEV + longest
    return slot_lengths.at[long_rows].set(LEN).astype(jnp.int32)


def shard_levels(rng, shape, pieces, low, largest):
    def one(axis_at, shards_of):
        steps = jax.random.uniform(jax.random.fold_in(jax.random.fold_in(rng, 6), axis_at), (shards_of,), jnp.float32, low / len(pieces), largest / len(pieces))
        return jnp.repeat(jnp.exp(steps), shape[axis_at] // shards_of).reshape((-1,) + (1,) * (len(shape) - axis_at - 1))

    gain = one(*pieces[0])
    for cut in pieces[1:]:
        gain = gain * one(*cut)
    return gain


def scatter_about(own_key, shape, width, bound, shards=(), kind=jnp.bfloat16):
    loudness = shard_levels(own_key, shape, shards, -0.22, 0.18) if shards else 1.0
    array = jax.random.normal(own_key, shape, jnp.float32) * width * loudness
    return jnp.minimum(jnp.maximum(array, -bound), bound).astype(kind)


def setup_inputs(seed: int = 0) -> dict:
    keys = jax.random.split(jax.random.key(seed), 14)
    return {
        "layer_in": scatter_about(keys[0], (SLOTS, LEN, D), 1.0, 6.0, ((0, 8), (1, 4)), jnp.float32),
        "lengths": draw_lengths(jax.random.fold_in(keys[13], 71), 0),
        "op_ids": draw_op_ids(jax.random.fold_in(keys[13], 71), 0),
        "kernel_ids": draw_kernel_ids(jax.random.fold_in(keys[13], 71), 0),
        "attn_proj": scatter_about(keys[4], (BLOCKS, 3, D, D), D ** -0.5, 0.21875),
        "attn_out": scatter_about(keys[5], (BLOCKS, D, D), (D // 8) ** -0.5, 0.625),
        "ffn_in": scatter_about(keys[6], (BLOCKS, D, FF), D ** -0.5, 0.21875),
        "ffn_out": scatter_about(keys[7], (BLOCKS, FF, D), FF ** -0.5, 0.109375),
        "point_weights": scatter_about(keys[8], (BLOCKS, D, D), D ** -0.5, 0.21875),
        "depth_weights": scatter_about(keys[9], (BLOCKS, TAPS, D), 0.4, 3.0, (), jnp.float32),
        "norm_gains": jnp.clip(1.0 + 0.1 * jax.random.normal(keys[10], (BLOCKS, D), jnp.float32), 0.5, 1.5),
        "norm_shifts": scatter_about(keys[11], (BLOCKS, D), 0.3, 2.0, (), jnp.float32),
        "cotangent": scatter_about(keys[12], (SLOTS, LEN, D), 1.0, 6.0, ((0, 8), (1, 4)), jnp.float32),
    }


highest = lax.Precision.HIGHEST

@jax.custom_vjp
def low(v):
    return lax.optimization_barrier(v.astype(jnp.bfloat16)).astype(jnp.float32)

@jax.custom_vjp
def low_back(v):
    return v

def low_keep(v):
    return (low(v), None)

def low_pass(kept, grad):
    return (grad,)

def back_keep(v):
    return (v, None)

def back_low(kept, grad):
    return (low(grad),)
low.defvjp(low_keep, low_pass)
low_back.defvjp(back_keep, back_low)

def split_heads(tensor):
    return tensor.reshape(tensor.shape[0], tensor.shape[1], HEADS, HEAD)

def layer_norm(summed, gain_row, shift_row):
    center = summed - lax.optimization_barrier(jnp.mean(summed, axis=-1, keepdims=True))
    spread = lax.optimization_barrier(jnp.mean(center * center, axis=-1, keepdims=True))
    return center * lax.rsqrt(spread + 1e-05) * gain_row + shift_row

def attention_path(inputs, proj, out_weight, key_live):
    rounded = low(inputs)
    queries = low(low_back(jnp.dot(rounded, proj[0], precision=highest)))
    keys_all = low(low_back(jnp.dot(rounded, proj[1], precision=highest)))
    values_all = low(low_back(jnp.dot(rounded, proj[2], precision=highest)))
    scores = jnp.einsum('sqhd,skhd->shqk', split_heads(queries), split_heads(keys_all), precision=highest) * HEAD ** (-0.5)
    scores = jnp.where(key_live[:, None, None, :], low_back(scores), -1000000000.0)
    soft_weights = jax.nn.softmax(scores, axis=-1)
    head_mix = jnp.einsum('shqk,skhd->sqhd', low(soft_weights), split_heads(values_all), precision=highest)
    head_mix = low(low_back(head_mix.reshape(inputs.shape)))
    return jnp.dot(head_mix, out_weight, precision=highest)

def conv_path(inputs, depth, point, kernel_id):
    rounded = low(inputs)
    half_width = TAPS // 2
    padded = jnp.pad(rounded, ((0, 0), (half_width, half_width), (0, 0)))
    length = inputs.shape[1]
    tap_used = jnp.abs(jnp.arange(TAPS, dtype=jnp.int32) - half_width) <= kernel_id + 1
    running = jnp.zeros_like(inputs)
    for offset in range(TAPS):
        running = running + padded[:, offset:offset + length] * jnp.where(tap_used[offset], depth[offset], 0.0)
    conv_mixed = low(low_back(running))
    return jnp.dot(conv_mixed, point, precision=highest)

def ffn_path(inputs, weight_in, weight_out):
    hidden = low_back(jnp.dot(low(inputs), weight_in, precision=highest))
    active = low(low_back(jax.nn.gelu(hidden, approximate=False)))
    return jnp.dot(active, weight_out, precision=highest)

def block_forward(values, slot_live, key_live, op_id, kernel_id, block_index, params):
    attn_proj, attn_out, ffn_in, ffn_out, point_weights, depth_weights, norm_gains, norm_shifts = params

    def run_attention(inputs):
        return attention_path(inputs, attn_proj[block_index], attn_out[block_index], key_live)

    def run_conv(inputs):
        return conv_path(inputs, depth_weights[block_index], point_weights[block_index], kernel_id)

    def run_ffn(inputs):
        return ffn_path(inputs, ffn_in[block_index], ffn_out[block_index])
    update = low_back(lax.switch(op_id, [run_attention, run_conv, run_ffn], values))
    return layer_norm(values + update, norm_gains[block_index], norm_shifts[block_index]) * slot_live[..., None]

def reference(layer_in, lengths, op_ids, kernel_ids, attn_proj, attn_out, ffn_in, ffn_out, point_weights, depth_weights, norm_gains, norm_shifts, cotangent):
    weights = tuple((item.astype(jnp.float32) for item in (attn_proj, attn_out, ffn_in, ffn_out, point_weights, depth_weights, norm_gains, norm_shifts)))
    positions = jnp.arange(LEN, dtype=jnp.int32)
    key_live = positions[None, :] < lengths[:, None]
    live_rows = key_live.astype(jnp.float32)
    group_live = live_rows.reshape(GROUPS, SLOT_DEV, LEN)
    group_keys = key_live.reshape(GROUPS, SLOT_DEV, LEN)

    def one_group(packed, params):
        values, slot_live, slot_keys, group_ops, group_kernels = packed
        for block_index in range(BLOCKS):
            values = block_forward(values, slot_live, slot_keys, group_ops[block_index], group_kernels[block_index], block_index, params)
        return values

    def forward(inputs, params):
        grouped = (inputs * live_rows[..., None]).reshape(GROUPS, SLOT_DEV, LEN, D)
        checked = jax.checkpoint(one_group)

        def run_group(packed):
            return checked(packed, params)
        result = lax.map(run_group, (grouped, group_live, group_keys, op_ids, kernel_ids))
        return result.reshape(SLOTS, LEN, D)
    layer_out, pullback = jax.vjp(forward, layer_in.astype(jnp.float32), weights)
    input_grad, grads = pullback(cotangent.astype(jnp.float32))
    counts = jnp.stack([lax.optimization_barrier(jnp.sum((op_ids == op_index).astype(jnp.float32), axis=0)) for op_index in range(3)])
    attn_count, conv_count, ffn_count = (counts[0], counts[1], counts[2])
    return (layer_out, input_grad, grads[0] / attn_count[:, None, None, None], grads[1] / attn_count[:, None, None], grads[2] / ffn_count[:, None, None], grads[3] / ffn_count[:, None, None], grads[4] / conv_count[:, None, None], grads[5] / conv_count[:, None, None], grads[6] / GROUPS, grads[7] / GROUPS)
```

```python
import jax
import jax.numpy as jnp
from jax import lax
from jax.sharding import PartitionSpec as P

HEADS = 12
HEAD = 64
TAPS = 7
BLOCKS = 2
EXTRA = 16
norm_eps = 1e-05
low = jnp.bfloat16


def mm(left, right):
    return jnp.dot(left, right, preferred_element_type=jnp.float32)


def ein(spec, left, right):
    return jnp.einsum(spec, left, right, preferred_element_type=jnp.float32)


def gather_group(piece, place, peers):
    parts = {0: piece}
    step = 1
    while step < peers:
        reach = peers // (2 * step)
        moved = {}
        for key, part in parts.items():
            moved[key ^ reach] = lax.ppermute(part, "seq", [(i, i ^ reach) for i in range(peers)])
        parts.update(moved)
        step *= 2
    stacked = jnp.stack([parts[key] for key in range(peers)])
    order = [lax.dynamic_index_in_dim(stacked, place ^ j, 0, False) for j in range(peers)]
    return jnp.concatenate(order, axis=1)


def heads_of(tensor):
    return tensor.reshape(tensor.shape[0], tensor.shape[1], HEADS, HEAD)


def soft_of(queries, keys, key_live):
    scores = ein("sqhd,skhd->shqk", heads_of(queries), heads_of(keys)) * HEAD**-0.5
    scores = jnp.where(key_live[:, None, None, :], scores, -1000000000.0)
    return jax.nn.softmax(scores, axis=-1)


def gelu_exact(hidden):
    return jax.nn.gelu(hidden, approximate=False)


def conv_of(a, taps, length):
    half = TAPS // 2
    padded = jnp.pad(a, ((0, 0), (half, half), (0, 0)))
    running = jnp.zeros(a.shape, jnp.float32)
    for offset in range(TAPS):
        running = running + padded[:, offset : offset + length] * taps[offset]
    return padded, running.astype(low)


def local(
    layer_in,
    lengths,
    op_ids,
    kernel_ids,
    attn_proj,
    attn_out,
    ffn_in,
    ffn_out,
    point_weights,
    depth_weights,
    norm_gains,
    norm_shifts,
    cotangent,
):
    slots, span, width = layer_in.shape
    hidden_width = ffn_in.shape[2]
    peers = lax.axis_size("seq")
    groups = lax.axis_size("dp")
    place = lax.axis_index("seq")
    length = span * peers
    rows = width // peers
    hidden_rows = hidden_width // peers
    cols = width // groups
    hidden_cols = hidden_width // groups
    key_live = jnp.arange(length, dtype=jnp.int32)[None, :] < lengths[:, None]
    live = key_live.astype(jnp.float32)[..., None]
    half = TAPS // 2

    x = gather_group(layer_in.astype(low), place, peers).astype(jnp.float32) * live
    cot = gather_group(cotangent.astype(low), place, peers).astype(jnp.float32)

    def own(full, count):
        return lax.dynamic_slice_in_dim(full, place * count, count, axis=2)

    def taps_of(b):
        used = jnp.abs(jnp.arange(TAPS, dtype=jnp.int32) - half) <= kernel_ids[0, b] + 1
        return used, jnp.where(used[:, None], depth_weights[b], 0.0)

    def forward(b, a):
        def attention(a):
            q, k, v = (mm(a, attn_proj[b, j]).astype(low) for j in range(3))
            soft = soft_of(q, k, key_live)
            mix = ein("shqk,skhd->sqhd", soft.astype(low), heads_of(v))
            return mm(mix.reshape(a.shape).astype(low), attn_out[b])

        def conv(a):
            return mm(conv_of(a, taps_of(b)[1], length)[1], point_weights[b])

        def ffn(a):
            return mm(gelu_exact(mm(a, ffn_in[b])).astype(low), ffn_out[b])

        return lax.switch(op_ids[0, b], [attention, conv, ffn], a)

    def backward(b, a, du):
        none_in = jnp.zeros((groups, rows, hidden_cols), low)
        none_depth = jnp.zeros((TAPS, width), jnp.float32)

        def columns(full):
            return full.reshape(groups, cols, -1)

        def attention(a, du):
            q, k, v = (mm(a, attn_proj[b, j]).astype(low) for j in range(3))
            soft = soft_of(q, k, key_live)
            soft_low = soft.astype(low)
            mix = ein("shqk,skhd->sqhd", soft_low, heads_of(v)).reshape(a.shape).astype(low)
            grad_mix = ein("std,ed->ste", du, attn_out[b]).astype(low)
            grad_soft = ein("sqhd,skhd->shqk", heads_of(grad_mix), heads_of(v))
            inner = jnp.sum(soft * grad_soft, axis=-1, keepdims=True)
            grad_scores = (soft * (grad_soft - inner)).astype(low)
            dv = ein("shqk,sqhd->skhd", soft_low, heads_of(grad_mix)).reshape(a.shape).astype(low)
            dq = (ein("shqk,skhd->sqhd", grad_scores, heads_of(k)) * HEAD**-0.5).reshape(a.shape)
            dk = (ein("shqk,sqhd->skhd", grad_scores, heads_of(q)) * HEAD**-0.5).reshape(a.shape)
            triple = (dq.astype(low), dk.astype(low), dv)
            da = sum(ein("ste,de->std", part, attn_proj[b, j]) for j, part in enumerate(triple))
            mine = own(a, rows)
            terms = [ein("ste,std->ed", part, mine) for part in triple]
            terms.append(ein("std,ste->de", du, own(mix, rows)))
            return da, none_in, columns(jnp.concatenate(terms, axis=1).astype(low)), none_depth

        def conv(a, du):
            used, taps = taps_of(b)
            padded, mixed = conv_of(a, taps, length)
            dc = ein("std,ed->ste", du, point_weights[b]).astype(low)
            wide = jnp.pad(dc, ((0, 0), (half, half), (0, 0)))
            da = jnp.zeros(a.shape, jnp.float32)
            depth = []
            for offset in range(TAPS):
                start = TAPS - 1 - offset
                da = da + wide[:, start : start + length] * taps[offset]
                moved = padded[:, offset : offset + length].astype(jnp.float32)
                depth.append(jnp.sum(moved * dc.astype(jnp.float32), axis=(0, 1)))
            term = ein("std,ste->de", du, own(mixed, rows)).astype(low)
            term = jnp.pad(term, ((0, 0), (0, width - rows)))
            return da, none_in, columns(term), jnp.where(used[:, None], jnp.stack(depth), 0.0)

        def ffn(a, du):
            hidden = mm(a, ffn_in[b])
            active, pull = jax.vjp(gelu_exact, hidden)
            df = ein("std,ed->ste", du, ffn_out[b]).astype(low)
            dh = pull(df.astype(jnp.float32))[0].astype(low)
            da = ein("ste,de->std", dh, ffn_in[b])
            term_in = ein("std,ste->de", own(a, rows), dh).astype(low)
            term_out = ein("std,ste->de", du, own(active.astype(low), hidden_rows)).astype(low)
            term_in = term_in.reshape(rows, groups, hidden_cols).transpose(1, 0, 2)
            return da, term_in, columns(term_out), none_depth

        return lax.switch(op_ids[0, b], [attention, conv, ffn], a, du)

    kept = []
    for b in range(BLOCKS):
        a = x.astype(low)
        z = x + forward(b, a)
        center = z - jnp.mean(z, axis=-1, keepdims=True)
        scale = lax.rsqrt(jnp.mean(center * center, axis=-1, keepdims=True) + norm_eps)
        unit = center * scale
        kept.append((a, unit, scale))
        x = (unit * norm_gains[b] + norm_shifts[b]) * live
    layer_out = lax.dynamic_slice_in_dim(x, place * span, span, axis=1)

    g = cot
    sums = [None] * BLOCKS
    for b in reversed(range(BLOCKS)):
        a, unit, scale = kept[b]
        g = g * live
        gain_term = jnp.sum(g * unit, axis=(0, 1))
        shift_term = jnp.sum(g, axis=(0, 1))
        gy = g * norm_gains[b]
        dz = scale * (
            gy
            - jnp.mean(gy, axis=-1, keepdims=True)
            - unit * jnp.mean(gy * unit, axis=-1, keepdims=True)
        )
        da, term_in, term_out, depth_term = backward(b, a, dz.astype(low))
        g = dz + da
        op_row = jnp.full((1, width), op_ids[0, b], jnp.float32)
        extra = jnp.concatenate([depth_term, gain_term[None], shift_term[None], op_row])
        extra = jnp.pad(extra, ((0, EXTRA - extra.shape[0]), (0, 0))).astype(low)
        extra = jnp.broadcast_to(extra[None], (groups, EXTRA, width))
        got_in = lax.all_to_all(term_in, "dp", 0, 0, tiled=True)
        got_out = lax.all_to_all(
            jnp.concatenate([term_out, extra], axis=1), "dp", 0, 0, tiled=True
        )
        sums[b] = (got_in, got_out)
    input_grad = lax.dynamic_slice_in_dim(g * live, place * span, span, axis=1)

    outs = [[] for _ in range(8)]
    for b in range(BLOCKS):
        got_in, got_out = (part.astype(jnp.float32) for part in sums[b])
        taken = got_out[:, cols + TAPS + 2, 0]
        picks = [(taken == op).astype(jnp.float32) for op in range(3)]
        counts = [jnp.sum(pick) for pick in picks]
        matrix = got_out[:, :cols]

        def picked(op, values):
            return jnp.sum(values * picks[op][:, None, None], axis=0) / counts[op]

        attn = picked(0, matrix).reshape(cols, 4, rows).transpose(1, 2, 0)
        outs[0].append(attn[:3])
        outs[1].append(attn[3])
        outs[2].append(picked(2, got_in))
        outs[3].append(picked(2, matrix).T)
        outs[4].append(picked(1, matrix[:, :, :rows]).T)
        small = got_out[:, cols:]
        outs[5].append(jnp.sum(small[:, :TAPS], axis=0) / counts[1])
        outs[6].append(jnp.sum(small[:, TAPS], axis=0) / groups)
        outs[7].append(jnp.sum(small[:, TAPS + 1], axis=0) / groups)
    return (layer_out, input_grad) + tuple(jnp.stack(part) for part in outs)


def solution(mesh):
    placed = (
        P("dp", "seq", None),
        P("dp"),
        P("dp", None),
        P("dp", None),
        P(),
        P(),
        P(),
        P(),
        P(),
        P(),
        P(),
        P(),
        P("dp", "seq", None),
    )
    return jax.shard_map(
        local,
        mesh=mesh,
        in_specs=placed,
        out_specs=(
            P("dp", "seq", None),
            P("dp", "seq", None),
            P(None, None, "seq", "dp"),
            P(None, "seq", "dp"),
            P(None, "seq", "dp"),
            P(None, "seq", "dp"),
            P(None, "seq", "dp"),
            P(),
            P(),
            P(),
        ),
        check_vma=False,
    )
```

```python
import functools

import jax
import jax.numpy as jnp
from jax import lax
from jax.experimental import pallas as pl
from jax.experimental.pallas import tpu as pltpu
from jax.sharding import PartitionSpec as P

HEADS = 12
HEAD = 64
TAPS = 7
BLOCKS = 2
EXTRA = 16
PAD = 8
norm_eps = 1e-05
low = jnp.bfloat16
wide = jnp.float32
VMEM_LIMIT = 60 * 1024 * 1024


def nn(left, right):
    return lax.dot_general(left, right, (((1,), (0,)), ((), ())), preferred_element_type=wide)


def nt(left, right):
    return lax.dot_general(left, right, (((1,), (1,)), ((), ())), preferred_element_type=wide)


def tn(left, right):
    return lax.dot_general(left, right, (((0,), (0,)), ((), ())), preferred_element_type=wide)


def live_of(scalars, slot, start, count, width):
    at = lax.broadcasted_iota(jnp.int32, (count, width), 0) + start
    return at < scalars[slot]


def used_tap(scalars, offset):
    return (abs(offset - TAPS // 2) <= scalars[3] + 1).astype(wide)


def fill_padded(padded, a_of, slots, length):
    width = padded.shape[2]
    for slot in range(slots):
        padded[slot, 0:PAD, :] = jnp.zeros((PAD, width), wide)
        padded[slot, PAD + length : PAD + length + PAD, :] = jnp.zeros((PAD, width), wide)
        padded[slot, PAD : PAD + length, :] = a_of(slot)


TILE = 256


def forward_kernel(
    b, slots, length, first, scalars, *refs
):
    pieces = refs[: (4 if first else 1)]
    refs = refs[len(pieces) :]
    (proj_h, out_h, fin_h, fout_h, point_h, depth, gain, shift) = refs[:8]
    (x_next, a_out, unit_out, scale_out, qkv_h, mix_h, lse_out, act_h, slope_h) = refs[8:17]
    (x_now, update, w_attn, w_in, w_out, qkv, mix, act, slope, padded, w_sem, s_sem) = refs[17:]
    width = x_next.shape[1]
    hidden = w_in.shape[1]
    chunks = hidden // width
    share = act_h.shape[1]
    tiles = length // TILE
    op = scalars[2]
    place = scalars[4]

    def attn_copies():
        return [
            pltpu.make_async_copy(proj_h.at[b, j], w_attn.at[j], w_sem.at[j]) for j in range(3)
        ] + [pltpu.make_async_copy(out_h.at[b], w_attn.at[3], w_sem.at[3])]

    def ffn_copies():
        cut = [pl.ds(j * width, width) for j in range(chunks)]
        return [
            pltpu.make_async_copy(fin_h.at[b, :, cut[j]], w_in.at[:, cut[j]], w_sem.at[j])
            for j in range(chunks)
        ] + [
            pltpu.make_async_copy(fout_h.at[b, cut[j]], w_out.at[cut[j]], w_sem.at[chunks + j])
            for j in range(chunks)
        ]

    def point_copy():
        return pltpu.make_async_copy(point_h.at[b], w_attn.at[0], w_sem.at[0])

    @pl.when(op == 0)
    def _():
        for copy in attn_copies():
            copy.start()

    @pl.when(op == 1)
    def _():
        point_copy().start()

    @pl.when(op == 2)
    def _():
        for copy in ffn_copies():
            copy.start()

    if first:
        span = pieces[0].shape[1]
        for key, piece in enumerate(pieces):
            origin = jnp.bitwise_xor(place, key) * span
            for slot in range(slots):
                rows = pl.ds(pl.multiple_of(slot * length + origin, span), span)
                keep = live_of(scalars, slot, origin, span, width)
                value = jnp.where(keep, piece[slot].astype(wide), 0.0)
                x_now[rows, :] = value
                a_out[rows, :] = value.astype(low)
    else:
        x_now = pieces[0]
        for t in range(slots * tiles):
            rows = pl.ds(t * TILE, TILE)
            a_out[rows, :] = x_now[rows, :].astype(low)

    @pl.when(op == 0)
    def _():
        copies = attn_copies()
        for j in range(3):
            copies[j].wait()

            @pl.loop(0, slots * tiles)
            def _(t):
                rows = pl.ds(pl.multiple_of(t * TILE, TILE), TILE)
                qkv[j, rows, :] = nn(a_out[rows, :], w_attn[j]).astype(low)

        saves = [pltpu.make_async_copy(qkv.at[j], qkv_h.at[j], s_sem.at[j]) for j in range(3)]
        for save in saves:
            save.start()
        for slot in range(slots):
            key_at = lax.broadcasted_iota(jnp.int32, (1, length), 1)
            bias = jnp.where(key_at < scalars[slot], 0.0, -1000000000.0).astype(wide)
            base = slot * length

            @pl.loop(0, HEADS // 2)
            def _(pair):
                lanes = pl.ds(pl.multiple_of(pair * 2 * HEAD, 2 * HEAD), 2 * HEAD)
                keys = qkv[1, pl.ds(base, length), lanes]
                values = qkv[2, pl.ds(base, length), lanes]
                for t in range(tiles):
                    rows = pl.ds(base + t * TILE, TILE)
                    queries = qkv[0, rows, lanes]
                    mixed = []
                    lane = lax.broadcasted_iota(jnp.int32, (TILE, 2 * HEAD), 1)
                    for head in range(2):
                        mine = (lane >= HEAD) == (head == 1)
                        one = jnp.where(mine, queries * jnp.asarray(HEAD**-0.5, low), jnp.zeros((), low))
                        scores = nt(one, keys) + bias
                        top = jnp.max(scores, axis=-1, keepdims=True)
                        exponent = jnp.exp(scores - top)
                        total = jnp.sum(exponent, axis=-1, keepdims=True)
                        soft = (exponent * (1.0 / total)).astype(low)
                        mixed.append(nn(soft, values))
                        stat = top + jnp.log(total)
                        lse_out[rows, :] = jnp.where(lane == pair * 2 + head, stat, lse_out[rows, :])
                    both = jnp.where(lane < HEAD, mixed[0], mixed[1])
                    mix[rows, lanes] = both.astype(low)

        save_mix = pltpu.make_async_copy(mix, mix_h, s_sem.at[3])
        save_mix.start()
        copies[3].wait()

        @pl.loop(0, slots * tiles)
        def _(t):
            rows = pl.ds(pl.multiple_of(t * TILE, TILE), TILE)
            update[rows, :] = nn(mix[rows, :], w_attn[3])

        for save in saves:
            save.wait()
        save_mix.wait()

    @pl.when(op == 1)
    def _():
        def rounded(slot):
            return a_out[pl.ds(slot * length, length), :].astype(wide)

        fill_padded(padded, rounded, slots, length)
        point_copy().wait()
        half = TAPS // 2
        for slot in range(slots):
            for t in range(tiles):
                running = jnp.zeros((TILE, width), wide)
                for offset in range(TAPS):
                    start = PAD + t * TILE + offset - half
                    tap = depth[offset : offset + 1, :] * used_tap(scalars, offset)
                    running = running + padded[slot, start : start + TILE, :] * tap
                rows = pl.ds(slot * length + t * TILE, TILE)
                mix[rows, :] = running.astype(low)
                update[rows, :] = nn(running.astype(low), w_attn[0])
        save_mix = pltpu.make_async_copy(mix, mix_h, s_sem.at[0])
        save_mix.start()
        save_mix.wait()

    @pl.when(op == 2)
    def _():
        copies = ffn_copies()
        for copy in copies:
            copy.wait()

        @pl.loop(0, slots * tiles)
        def _(t):
            rows = pl.ds(pl.multiple_of(t * TILE, TILE), TILE)
            a = a_out[rows, :]
            for j in range(chunks):
                cut = pl.ds(j * width, width)
                h = nn(a, w_in[:, cut])
                cdf = 0.5 * (1.0 + lax.erf(h * (0.5**0.5)))
                density = jnp.exp(-0.5 * h * h) * 0.3989422804014327
                act[rows, cut] = (h * cdf).astype(low)
                slope[rows, cut] = (cdf + h * density).astype(low)
            update[rows, :] = nn(act[rows, :], w_out[...])

        mine = pl.ds(pl.multiple_of(place * share, 128), share)
        saves = [
            pltpu.make_async_copy(act.at[:, mine], act_h, s_sem.at[0]),
            pltpu.make_async_copy(slope, slope_h, s_sem.at[1]),
        ]
        for save in saves:
            save.start()
        for save in saves:
            save.wait()

    for slot in range(slots):

        @pl.loop(0, tiles)
        def _(t):
            start = pl.multiple_of(t * TILE, TILE)
            rows = pl.ds(pl.multiple_of(slot * length + t * TILE, TILE), TILE)
            z = x_now[rows, :] + update[rows, :]
            center = z - jnp.mean(z, axis=-1, keepdims=True)
            scale = lax.rsqrt(jnp.mean(center * center, axis=-1, keepdims=True) + norm_eps)
            unit = center * scale
            unit_out[rows, :] = unit
            scale_out[rows, :] = scale
            keep = live_of(scalars, slot, start, TILE, width)
            x_next[rows, :] = jnp.where(keep, unit * gain[...] + shift[...], 0.0)


def any_spec():
    return pl.BlockSpec(memory_space=pl.ANY)


def vmem_spec():
    return pl.BlockSpec(memory_space=pltpu.VMEM)


def forward_call(b, slots, length, peers, scalars, pieces, weights, depth, gain, shift):
    width = gain.shape[-1]
    hidden = weights[2].shape[2]
    rows = slots * length
    first = len(pieces) > 1
    shapes = [
        ((rows, width), wide),
        ((rows, width), low),
        ((rows, width), wide),
        ((rows, 1), wide),
        ((3, rows, width), low),
        ((rows, width), low),
        ((rows, 2 * HEAD), wide),
        ((rows, hidden // peers), low),
        ((rows, hidden), low),
    ]
    in_any = (False, False, False, False, True, True, False, True, True)
    return pl.pallas_call(
        functools.partial(forward_kernel, b, slots, length, first),
        out_shape=[jax.ShapeDtypeStruct(*s) for s in shapes],
        in_specs=[pl.BlockSpec(memory_space=pltpu.SMEM)]
        + [vmem_spec()] * len(pieces)
        + [any_spec()] * 5
        + [vmem_spec()] * 3,
        out_specs=[any_spec() if flag else vmem_spec() for flag in in_any],
        scratch_shapes=[
            pltpu.VMEM((rows, width) if first else (8, 128), wide),
            pltpu.VMEM((rows, width), wide),
            pltpu.VMEM((4, width, width), low),
            pltpu.VMEM((width, hidden), low),
            pltpu.VMEM((hidden, width), low),
            pltpu.VMEM((3, rows, width), low),
            pltpu.VMEM((rows, width), low),
            pltpu.VMEM((rows, hidden), low),
            pltpu.VMEM((rows, hidden), low),
            pltpu.VMEM((slots, length + 2 * PAD, width), wide),
            pltpu.SemaphoreType.DMA((8,)),
            pltpu.SemaphoreType.DMA((4,)),
        ],
        compiler_params=pltpu.CompilerParams(vmem_limit_bytes=VMEM_LIMIT),
        name="forward_block",
    )(scalars, *pieces, *weights, depth, gain, shift)


def backward_kernel(b, slots, length, peers, groups, first, last, scalars, *refs):
    pieces = refs[: (peers if first else 1)]
    refs = refs[len(pieces) :]
    (unit_in, scale_in, a_in, lse_in, qkv_h, mix_h, act_h, slope_h) = refs[:8]
    (proj_h, out_h, fin_h, fout_h, point_h, depth, gain) = refs[8:15]
    (g_out, term_in, term_out) = refs[15:18]
    (gn, du, w_attn, w_in, w_out, qkv, mix, act, slope, padded, lse_t, turned, w_sem, s_sem) = refs[18:]
    width = a_in.shape[1]
    hidden = w_in.shape[1]
    chunks = hidden // width
    tiles = length // TILE
    rows_all = slots * length
    own = width // peers
    cols = width // groups
    hidden_cols = hidden // groups
    op = scalars[2]
    place = scalars[4]
    span = length // peers

    def attn_copies():
        return (
            [pltpu.make_async_copy(qkv_h.at[j], qkv.at[j], s_sem.at[j]) for j in range(3)]
            + [pltpu.make_async_copy(mix_h, mix, s_sem.at[3])]
            + [pltpu.make_async_copy(proj_h.at[b, j], w_attn.at[j], w_sem.at[j]) for j in range(3)]
            + [pltpu.make_async_copy(out_h.at[b], w_attn.at[3], w_sem.at[3])]
        )

    def conv_copies():
        return [
            pltpu.make_async_copy(mix_h, mix, s_sem.at[0]),
            pltpu.make_async_copy(point_h.at[b], w_attn.at[0], w_sem.at[0]),
        ]

    def ffn_copies():
        cut = [pl.ds(j * width, width) for j in range(chunks)]
        return [
            pltpu.make_async_copy(fout_h.at[b], w_out, w_sem.at[0]),
            pltpu.make_async_copy(slope_h, slope, s_sem.at[0]),
            pltpu.make_async_copy(fin_h.at[b], w_in, w_sem.at[1]),
            pltpu.make_async_copy(act_h, act, s_sem.at[1]),
        ]

    for index, copies in enumerate((attn_copies, conv_copies, ffn_copies)):

        @pl.when(op == index)
        def _():
            for copy in copies():
                copy.start()

    gain_term = jnp.zeros((1, width), wide)
    shift_term = jnp.zeros((1, width), wide)

    def norm_back(slot, start, g, rows, count):
        keep = live_of(scalars, slot, start, count, width)
        g = jnp.where(keep, g, 0.0)
        unit = unit_in[rows, :]
        gu = g * unit
        gy = g * gain[...]
        first_mean = jnp.mean(gy, axis=-1, keepdims=True)
        second_mean = jnp.mean(gu * gain[...], axis=-1, keepdims=True)
        dz = scale_in[rows, :] * (gy - first_mean - unit * second_mean)
        gn[rows, :] = dz
        du[rows, :] = dz.astype(low)
        return jnp.sum(gu, axis=0, keepdims=True), jnp.sum(g, axis=0, keepdims=True)

    for slot in range(slots):
        if first:
            for j in range(peers):
                rows = pl.ds(slot * length + j * span, span)
                for key in range(peers):

                    @pl.when(jnp.bitwise_xor(place, key) == j)
                    def _():
                        gn[rows, :] = pieces[key][slot].astype(wide)

                one, two = norm_back(slot, j * span, gn[rows, :], rows, span)
                gain_term, shift_term = gain_term + one, shift_term + two
        else:
            for t in range(tiles):
                rows = pl.ds(slot * length + t * TILE, TILE)
                one, two = norm_back(slot, t * TILE, pieces[0][rows, :], rows, TILE)
                gain_term, shift_term = gain_term + one, shift_term + two

    def spread(start, values):
        for d in range(groups):
            term_out[d, cols + start : cols + start + values.shape[0], :] = values.astype(low)

    spread(TAPS, gain_term)
    spread(TAPS + 1, shift_term)
    spread(TAPS + 2, jnp.full((1, width), op.astype(wide), wide))

    def turn_own(source):
        for s in range(peers):

            @pl.when(place == s)
            def _():
                turned[...] = source[:, s * own : (s + 1) * own].T

    def put_out(start, values):
        for d in range(groups):
            piece = values[d * cols : (d + 1) * cols].astype(low)
            term_out[d, 0:cols, start : start + values.shape[1]] = piece

    def add_back(grad):
        if last:
            for slot in range(slots):
                rows = pl.ds(pl.multiple_of(slot * length + place * span, span), span)
                keep = live_of(scalars, slot, place * span, span, width)
                g_out[slot] = jnp.where(keep, gn[rows, :] + grad(rows), 0.0)
        else:

            @pl.loop(0, slots * tiles)
            def _(t):
                rows = pl.ds(pl.multiple_of(t * TILE, TILE), TILE)
                g_out[rows, :] = gn[rows, :] + grad(rows)

    @pl.when(op == 0)
    def _():
        copies = attn_copies()
        copies[7].wait()
        for copy in copies[:4]:
            copy.wait()
        turn_own(mix)
        put_out(3 * own, nn(turned[...], du[...]).T)

        @pl.loop(0, slots * tiles)
        def _(t):
            rows = pl.ds(pl.multiple_of(t * TILE, TILE), TILE)
            mix[rows, :] = nt(du[rows, :], w_attn[3]).astype(low)

        for slot in range(slots):
            lse_t[slot] = lse_in[slot * length : (slot + 1) * length, :].T
        for slot in range(slots):
            base = slot * length

            @pl.loop(0, HEADS // 2)
            def _(pair):
                lanes = pl.ds(pl.multiple_of(pair * 2 * HEAD, 2 * HEAD), 2 * HEAD)
                every = pl.ds(base, length)
                keys = qkv[1, every, lanes]
                values = qkv[2, every, lanes]
                dk = jnp.zeros((length, 2 * HEAD), wide)
                dv = jnp.zeros((length, 2 * HEAD), wide)
                lane = lax.broadcasted_iota(jnp.int32, (TILE, 2 * HEAD), 1)
                lane_all = lax.broadcasted_iota(jnp.int32, (length, 2 * HEAD), 1)
                factor = jnp.asarray(HEAD**-0.5, low)
                none = jnp.zeros((), low)
                for t in range(tiles):
                    rows = pl.ds(base + t * TILE, TILE)
                    queries = qkv[0, rows, lanes] * factor
                    grads = mix[rows, lanes]
                    dq = jnp.zeros((2 * HEAD, TILE), wide)
                    for head in range(2):
                        mine = (lane >= HEAD) == (head == 1)
                        mine_all = (lane_all >= HEAD) == (head == 1)
                        q_one = jnp.where(mine, queries, none)
                        g_one = jnp.where(mine, grads, none)
                        k_one = jnp.where(mine_all, keys * factor, none)
                        stat = lse_t[slot, pl.ds(pair * 2 + head, 1), t * TILE : (t + 1) * TILE]
                        soft = jnp.exp(jnp.minimum(nt(keys, q_one) - stat, 0.0))
                        product = soft * nt(values, g_one)
                        inner = jnp.sum(product, axis=0, keepdims=True)
                        grad_scores = (product - soft * inner).astype(low)
                        dv = dv + nn(soft.astype(low), g_one)
                        dk = dk + nn(grad_scores, q_one)
                        dq = dq + tn(k_one, grad_scores)
                    qkv[0, rows, lanes] = dq.T.astype(low)
                qkv[1, every, lanes] = dk.astype(low)
                qkv[2, every, lanes] = dv.astype(low)

        for j in range(3):
            copies[4 + j].wait()
        add_back(
            lambda rows: nt(qkv[0, rows, :], w_attn[0])
            + nt(qkv[1, rows, :], w_attn[1])
            + nt(qkv[2, rows, :], w_attn[2])
        )
        turn_own(a_in)
        for j in range(3):
            put_out(j * own, nn(turned[...], qkv[j]).T)

    @pl.when(op == 1)
    def _():
        copies = conv_copies()
        for copy in copies:
            copy.wait()
        turn_own(mix)
        put_out(0, nn(turned[...], du[...]).T)

        @pl.loop(0, slots * tiles)
        def _(t):
            rows = pl.ds(pl.multiple_of(t * TILE, TILE), TILE)
            mix[rows, :] = nt(du[rows, :], w_attn[0]).astype(low)

        half = TAPS // 2
        depth_terms = [jnp.zeros((1, width), wide) for _ in range(TAPS)]
        fill_padded(padded, lambda slot: a_in[pl.ds(slot * length, length), :].astype(wide), slots, length)
        for slot in range(slots):
            for t in range(tiles):
                grads = mix[pl.ds(slot * length + t * TILE, TILE), :].astype(wide)
                for offset in range(TAPS):
                    start = PAD + t * TILE + offset - half
                    moved = padded[slot, start : start + TILE, :]
                    depth_terms[offset] += jnp.sum(moved * grads, axis=0, keepdims=True)
        for offset in range(TAPS):
            spread(offset, depth_terms[offset] * used_tap(scalars, offset))
        fill_padded(padded, lambda slot: mix[pl.ds(slot * length, length), :].astype(wide), slots, length)
        for slot in range(slots):
            for t in range(tiles):
                running = jnp.zeros((TILE, width), wide)
                for offset in range(TAPS):
                    start = PAD + t * TILE - offset + half
                    tap = depth[offset : offset + 1, :] * used_tap(scalars, offset)
                    running = running + padded[slot, start : start + TILE, :] * tap
                rows = pl.ds(slot * length + t * TILE, TILE)
                gn[rows, :] = gn[rows, :] + running
        add_back(lambda rows: 0.0)

    @pl.when(op == 2)
    def _():
        copies = ffn_copies()
        copies[0].wait()
        copies[1].wait()

        @pl.loop(0, slots * tiles)
        def _(t):
            rows = pl.ds(pl.multiple_of(t * TILE, TILE), TILE)
            upstream = du[rows, :]
            for j in range(chunks):
                cut = pl.ds(j * width, width)
                df = nt(upstream, w_out[cut, :]).astype(low).astype(wide)
                slope[rows, cut] = (df * slope[rows, cut].astype(wide)).astype(low)

        copies[2].wait()
        copies[3].wait()
        put_out(0, nn(du[...].T, act[...]))
        turn_own(a_in)
        for d in range(groups):
            piece = slope[:, d * hidden_cols : (d + 1) * hidden_cols]
            term_in[d] = nn(turned[...], piece).astype(low)
        add_back(lambda rows: nt(slope[rows, :], w_in[...]))


def backward_call(b, slots, length, peers, groups, last, scalars, pieces, kept, weights, depth, gain):
    width = gain.shape[-1]
    hidden = weights[2].shape[2]
    rows = slots * length
    first = len(pieces) > 1
    cols = width // groups
    (unit, scale, a, lse, qkv, mix, act, slope) = kept
    shapes = [
        ((slots, length // peers, width) if last else (rows, width), wide),
        ((groups, width // peers, hidden // groups), low),
        ((groups, cols + EXTRA, width), low),
    ]
    return pl.pallas_call(
        functools.partial(backward_kernel, b, slots, length, peers, groups, first, last),
        out_shape=[jax.ShapeDtypeStruct(*s) for s in shapes],
        in_specs=[pl.BlockSpec(memory_space=pltpu.SMEM)]
        + [vmem_spec()] * len(pieces)
        + [vmem_spec()] * 4
        + [any_spec()] * 9
        + [vmem_spec()] * 2,
        out_specs=[vmem_spec()] * 3,
        scratch_shapes=[
            pltpu.VMEM((rows, width), wide),
            pltpu.VMEM((rows, width), low),
            pltpu.VMEM((4, width, width), low),
            pltpu.VMEM((width, hidden), low),
            pltpu.VMEM((hidden, width), low),
            pltpu.VMEM((3, rows, width), low),
            pltpu.VMEM((rows, width), low),
            pltpu.VMEM((rows, hidden // peers), low),
            pltpu.VMEM((rows, hidden), low),
            pltpu.VMEM((slots, length + 2 * PAD, width), wide),
            pltpu.VMEM((slots, 2 * HEAD, length), wide),
            pltpu.VMEM((width // peers, rows), low),
            pltpu.SemaphoreType.DMA((8,)),
            pltpu.SemaphoreType.DMA((4,)),
        ],
        compiler_params=pltpu.CompilerParams(vmem_limit_bytes=VMEM_LIMIT),
        name="backward_block",
    )(scalars, *pieces, unit, scale, a, lse, qkv, mix, act, slope, *weights, depth, gain)


def exchange_group(piece, peers):
    parts = {0: piece}
    reach = peers // 2
    while reach:
        pairs = [(i, i ^ reach) for i in range(peers)]
        parts.update({key ^ reach: lax.ppermute(part, "seq", pairs) for key, part in parts.items()})
        reach //= 2
    return [parts[key] for key in range(peers)]


def local(
    layer_in,
    lengths,
    op_ids,
    kernel_ids,
    attn_proj,
    attn_out,
    ffn_in,
    ffn_out,
    point_weights,
    depth_weights,
    norm_gains,
    norm_shifts,
    cotangent,
):
    slots, span, width = layer_in.shape
    peers = lax.axis_size("seq")
    groups = lax.axis_size("dp")
    place = lax.axis_index("seq").astype(jnp.int32)
    length = span * peers
    rows = width // peers
    cols = width // groups
    weights = (attn_proj, attn_out, ffn_in, ffn_out, point_weights)

    x_parts = exchange_group(layer_in.astype(low), peers)
    later, x_parts = lax.optimization_barrier((cotangent.astype(low), x_parts))
    cot_parts = exchange_group(later, peers)

    scalars = [
        jnp.concatenate([lengths, jnp.stack([op_ids[0, b], kernel_ids[0, b], place])])
        for b in range(BLOCKS)
    ]
    kept = []
    pieces = x_parts
    for b in range(BLOCKS):
        outs = forward_call(
            b, slots, length, peers, scalars[b], pieces, weights,
            depth_weights[b], norm_gains[b][None], norm_shifts[b][None],
        )
        x, a, unit, scale, qkv, mix, lse, act, slope = outs
        kept.append((unit, scale, a, lse, qkv, mix, act, slope))
        pieces = [x]
    layer_out = lax.dynamic_slice_in_dim(
        x.reshape(slots, length, width), place * span, span, axis=1
    )

    pieces = cot_parts
    sums = [None] * BLOCKS
    for b in reversed(range(BLOCKS)):
        g, term_in, term_out = backward_call(
            b, slots, length, peers, groups, b == 0, scalars[b], pieces, kept[b], weights,
            depth_weights[b], norm_gains[b][None],
        )
        pieces = [g]
        sums[b] = (
            lax.all_to_all(term_in, "dp", 0, 0, tiled=True),
            lax.all_to_all(term_out, "dp", 0, 0, tiled=True),
        )

    outs = [[] for _ in range(8)]
    for b in range(BLOCKS):
        got_in, got_out = sums[b]
        taken = got_out[:, cols + TAPS + 2, 0]
        counts = [jnp.sum((taken == op).astype(wide)) for op in range(3)]
        matrix = got_out[:, :cols]

        def picked(op, values):
            kept_values = jnp.where((taken == op)[:, None, None], values.astype(wide), 0.0)
            return jnp.sum(kept_values, axis=0) / counts[op]

        attn = picked(0, matrix).reshape(cols, 4, rows).transpose(1, 2, 0)
        outs[0].append(attn[:3])
        outs[1].append(attn[3])
        outs[2].append(picked(2, got_in))
        outs[3].append(picked(2, matrix).T)
        outs[4].append(picked(1, matrix[:, :, :rows]).T)
        small = got_out[:, cols:].astype(wide)
        depth = jnp.where((taken == 1)[:, None, None], small[:, :TAPS], 0.0)
        outs[5].append(jnp.sum(depth, axis=0) / counts[1])
        outs[6].append(jnp.sum(small[:, TAPS], axis=0) / groups)
        outs[7].append(jnp.sum(small[:, TAPS + 1], axis=0) / groups)
    return (layer_out, g) + tuple(jnp.stack(part) for part in outs)


def solution(mesh):
    placed = (
        P("dp", "seq", None),
        P("dp"),
        P("dp", None),
        P("dp", None),
        P(),
        P(),
        P(),
        P(),
        P(),
        P(),
        P(),
        P(),
        P("dp", "seq", None),
    )
    return jax.shard_map(
        local,
        mesh=mesh,
        in_specs=placed,
        out_specs=(
            P("dp", "seq", None),
            P("dp", "seq", None),
            P(None, None, "seq", "dp"),
            P(None, "seq", "dp"),
            P(None, "seq", "dp"),
            P(None, "seq", "dp"),
            P(None, "seq", "dp"),
            P(),
            P(),
            P(),
        ),
        check_vma=False,
    )
```

```python
import functools

import jax
import jax.numpy as jnp
from jax import lax
from jax.experimental import pallas as pl
from jax.experimental.pallas import tpu as pltpu
from jax.sharding import PartitionSpec as P

HEADS = 12
HEAD = 64
TAPS = 7
BLOCKS = 2
EXTRA = 16
PAD = 8
norm_eps = 1e-05
low = jnp.bfloat16
wide = jnp.float32
VMEM_LIMIT = 60 * 1024 * 1024


def nn(left, right):
    return lax.dot_general(left, right, (((1,), (0,)), ((), ())), preferred_element_type=wide)


def nt(left, right):
    return lax.dot_general(left, right, (((1,), (1,)), ((), ())), preferred_element_type=wide)


def tn(left, right):
    return lax.dot_general(left, right, (((0,), (0,)), ((), ())), preferred_element_type=wide)


def live_of(scalars, slot, start, count, width):
    at = lax.broadcasted_iota(jnp.int32, (count, width), 0) + start
    return at < scalars[slot]


def used_tap(scalars, offset):
    return (abs(offset - TAPS // 2) <= scalars[3] + 1).astype(wide)


def fill_padded(padded, a_of, slots, length):
    width = padded.shape[2]
    for slot in range(slots):
        padded[slot, 0:PAD, :] = jnp.zeros((PAD, width), wide)
        padded[slot, PAD + length : PAD + length + PAD, :] = jnp.zeros((PAD, width), wide)
        padded[slot, PAD : PAD + length, :] = a_of(slot)


TILE = 256
QUERY_TILE = 256
GRAD_TILE = 512
FACTOR = HEAD**-0.5


def pair_rows(tensor):
    lane = lax.broadcasted_iota(jnp.int32, tensor.shape, 1)
    none = jnp.zeros((), tensor.dtype)
    return jnp.concatenate(
        [jnp.where(lane < HEAD, tensor, none), jnp.where(lane < HEAD, none, tensor)], axis=0
    )


def forward_kernel(
    b, slots, length, peers, first, last, scalars, *refs
):
    pieces = refs[: (4 if first else 1)]
    refs = refs[len(pieces) :]
    (proj_h, out_h, fin_h, fout_h, point_h, depth, gain, shift) = refs[:8]
    (x_next, a_out, unit_out, scale_out, qkv_h, mix_h, lse_out, act_h, slope_h) = refs[8:17]
    (x_now, update, w_in, w_out, mix, act, slope, padded, w_sem, s_sem) = refs[17:]
    width = w_out.shape[1]
    hidden = w_in.shape[1]
    span = length // peers
    chunks = hidden // width
    share = act_h.shape[1]
    tiles = length // TILE
    op = scalars[2]
    place = scalars[4]

    def part(j):
        return pl.ds(j * width, width)

    def heads(j, pair):
        return pl.ds(pl.multiple_of(j * width + pair * 2 * HEAD, 2 * HEAD), 2 * HEAD)

    def attn_copies():
        return [
            pltpu.make_async_copy(proj_h.at[b, j], w_out.at[part(j)], w_sem.at[j]) for j in range(3)
        ] + [pltpu.make_async_copy(out_h.at[b], w_out.at[part(3)], w_sem.at[3])]

    def ffn_copies():
        cut = [pl.ds(j * width, width) for j in range(chunks)]
        return [
            pltpu.make_async_copy(fin_h.at[b, :, cut[j]], w_in.at[:, cut[j]], w_sem.at[j])
            for j in range(chunks)
        ] + [
            pltpu.make_async_copy(fout_h.at[b, cut[j]], w_out.at[cut[j]], w_sem.at[chunks + j])
            for j in range(chunks)
        ]

    def attn_saves():
        return [pltpu.make_async_copy(slope.at[:, part(j)], qkv_h.at[j], s_sem.at[j]) for j in range(3)] + [
            pltpu.make_async_copy(mix, mix_h, s_sem.at[3])
        ]

    def conv_saves():
        return [pltpu.make_async_copy(mix, mix_h, s_sem.at[0])]

    def ffn_saves():
        mine = pl.ds(pl.multiple_of(place * share, 128), share)
        return [
            pltpu.make_async_copy(act.at[:, mine], act_h, s_sem.at[0]),
            pltpu.make_async_copy(slope, slope_h, s_sem.at[1]),
        ]

    def point_copy():
        return pltpu.make_async_copy(point_h.at[b], w_out.at[part(0)], w_sem.at[0])

    @pl.when(op == 0)
    def _():
        for copy in attn_copies():
            copy.start()

    @pl.when(op == 1)
    def _():
        point_copy().start()

    @pl.when(op == 2)
    def _():
        for copy in ffn_copies():
            copy.start()

    if first:
        for key, piece in enumerate(pieces):
            origin = jnp.bitwise_xor(place, key) * span
            for slot in range(slots):
                rows = pl.ds(pl.multiple_of(slot * length + origin, span), span)
                keep = live_of(scalars, slot, origin, span, width)
                value = jnp.where(keep, piece[slot].astype(wide), 0.0)
                x_now[rows, :] = value
                a_out[rows, :] = value.astype(low)
    else:
        x_now = pieces[0]
        for t in range(slots * tiles):
            rows = pl.ds(t * TILE, TILE)
            a_out[rows, :] = x_now[rows, :].astype(low)

    @pl.when(op == 0)
    def _():
        copies = attn_copies()
        for j in range(3):
            copies[j].wait()

            @pl.loop(0, slots * tiles)
            def _(t):
                rows = pl.ds(pl.multiple_of(t * TILE, TILE), TILE)
                slope[rows, part(j)] = nn(a_out[rows, :], w_out[part(j), :]).astype(low)

        for save in attn_saves()[:3]:
            save.start()
        for slot in range(slots):
            key_at = lax.broadcasted_iota(jnp.int32, (1, length), 1)
            bias = jnp.where(key_at < scalars[slot], 0.0, -1000000000.0).astype(wide)
            base = slot * length

            @pl.loop(0, HEADS // 2)
            def _(pair):
                lanes = pl.ds(pl.multiple_of(pair * 2 * HEAD, 2 * HEAD), 2 * HEAD)
                keys = slope[pl.ds(base, length), heads(1, pair)]
                values = slope[pl.ds(base, length), heads(2, pair)]
                lane = lax.broadcasted_iota(jnp.int32, (QUERY_TILE, 2 * HEAD), 1)
                for t in range(length // QUERY_TILE):
                    rows = pl.ds(base + t * QUERY_TILE, QUERY_TILE)
                    scores = nt(pair_rows(slope[rows, heads(0, pair)] * FACTOR), keys) + bias
                    top = jnp.max(scores, axis=-1, keepdims=True)
                    exponent = jnp.exp(scores - top)
                    total = jnp.sum(exponent, axis=-1, keepdims=True)
                    mixed = nn(exponent.astype(low), values) * (1.0 / total)
                    stat = top + jnp.log(total)
                    kept = jnp.where(lane == pair * 2, stat[:QUERY_TILE], lse_out[rows, :])
                    lse_out[rows, :] = jnp.where(lane == pair * 2 + 1, stat[QUERY_TILE:], kept)
                    both = jnp.where(lane < HEAD, mixed[:QUERY_TILE], mixed[QUERY_TILE:])
                    mix[rows, lanes] = both.astype(low)

        attn_saves()[3].start()
        copies[3].wait()

        @pl.loop(0, slots * tiles)
        def _(t):
            rows = pl.ds(pl.multiple_of(t * TILE, TILE), TILE)
            update[rows, :] = nn(mix[rows, :], w_out[part(3), :])

    @pl.when(op == 1)
    def _():
        def rounded(slot):
            return a_out[pl.ds(slot * length, length), :].astype(wide)

        fill_padded(padded, rounded, slots, length)
        point_copy().wait()
        half = TAPS // 2
        for slot in range(slots):
            for t in range(tiles):
                running = jnp.zeros((TILE, width), wide)
                for offset in range(TAPS):
                    start = PAD + t * TILE + offset - half
                    tap = depth[offset : offset + 1, :] * used_tap(scalars, offset)
                    running = running + padded[slot, start : start + TILE, :] * tap
                rows = pl.ds(slot * length + t * TILE, TILE)
                mix[rows, :] = running.astype(low)
                update[rows, :] = nn(running.astype(low), w_out[part(0), :])
        conv_saves()[0].start()

    @pl.when(op == 2)
    def _():
        copies = ffn_copies()

        @pl.loop(0, slots * tiles)
        def _(t):
            rows = pl.ds(pl.multiple_of(t * TILE, TILE), TILE)
            a = a_out[rows, :]
            for j in range(chunks):
                cut = pl.ds(j * width, width)

                @pl.when(t == 0)
                def _():
                    copies[j].wait()

                h = nn(a, w_in[:, cut])
                cdf = 0.5 * (1.0 + lax.erf(h * (0.5**0.5)))
                density = jnp.exp(-0.5 * h * h) * 0.3989422804014327
                act[rows, cut] = (h * cdf).astype(low)
                slope[rows, cut] = (cdf + h * density).astype(low)

            @pl.when(t == 0)
            def _():
                for copy in copies[chunks:]:
                    copy.wait()

            update[rows, :] = nn(act[rows, :], w_out[...])

        for save in ffn_saves():
            save.start()

    for slot in range(slots):

        @pl.loop(0, tiles)
        def _(t):
            start = pl.multiple_of(t * TILE, TILE)
            rows = pl.ds(pl.multiple_of(slot * length + t * TILE, TILE), TILE)
            z = x_now[rows, :] + update[rows, :]
            center = z - jnp.mean(z, axis=-1, keepdims=True)
            scale = lax.rsqrt(jnp.mean(center * center, axis=-1, keepdims=True) + norm_eps)
            unit = center * scale
            unit_out[rows, :] = unit
            scale_out[rows, :] = scale
            keep = live_of(scalars, slot, start, TILE, width)
            target = update if last else x_next
            target[rows, :] = jnp.where(keep, unit * gain[...] + shift[...], 0.0)

        if last:
            mine = pl.ds(pl.multiple_of(slot * length + place * span, span), span)
            x_next[slot] = update[mine, :]

    for index, saves in enumerate((attn_saves, conv_saves, ffn_saves)):

        @pl.when(op == index)
        def _():
            for save in saves():
                save.wait()


def any_spec():
    return pl.BlockSpec(memory_space=pl.ANY)


def vmem_spec():
    return pl.BlockSpec(memory_space=pltpu.VMEM)


def forward_call(b, slots, length, peers, last, scalars, pieces, weights, depth, gain, shift):
    width = gain.shape[-1]
    hidden = weights[2].shape[2]
    rows = slots * length
    first = len(pieces) > 1
    shapes = [
        ((slots, length // peers, width) if last else (rows, width), wide),
        ((rows, width), low),
        ((rows, width), wide),
        ((rows, 1), wide),
        ((3, rows, width), low),
        ((rows, width), low),
        ((rows, 2 * HEAD), wide),
        ((rows, hidden // peers), low),
        ((rows, hidden), low),
    ]
    in_any = (False, False, False, False, True, True, False, True, True)
    return pl.pallas_call(
        functools.partial(forward_kernel, b, slots, length, peers, first, last),
        out_shape=[jax.ShapeDtypeStruct(*s) for s in shapes],
        in_specs=[pl.BlockSpec(memory_space=pltpu.SMEM)]
        + [vmem_spec()] * len(pieces)
        + [any_spec()] * 5
        + [vmem_spec()] * 3,
        out_specs=[any_spec() if flag else vmem_spec() for flag in in_any],
        scratch_shapes=[
            pltpu.VMEM((rows, width) if first else (8, 128), wide),
            pltpu.VMEM((rows, width), wide),
            pltpu.VMEM((width, hidden), low),
            pltpu.VMEM((hidden, width), low),
            pltpu.VMEM((rows, width), low),
            pltpu.VMEM((rows, hidden), low),
            pltpu.VMEM((rows, hidden), low),
            pltpu.VMEM((slots, length + 2 * PAD, width), wide),
            pltpu.SemaphoreType.DMA((8,)),
            pltpu.SemaphoreType.DMA((4,)),
        ],
        compiler_params=pltpu.CompilerParams(vmem_limit_bytes=VMEM_LIMIT),
        name="forward_block",
    )(scalars, *pieces, *weights, depth, gain, shift)


def up16(count):
    return -(-count // 16) * 16


def payload_rows(width, groups):
    pitch = up16(width // groups)
    return pitch, 2 * pitch + EXTRA


def dense_rows(width, groups, peers):
    pitch = up16(width // groups)
    tail = up16(width // groups // peers)
    return pitch, 3 * pitch, 3 * pitch + tail, 3 * pitch + tail + EXTRA


def backward_kernel(b, slots, length, peers, groups, first, last, scalars, *refs):
    pieces = refs[: (peers if first else 1)]
    refs = refs[len(pieces) :]
    (unit_in, scale_in, a_in, lse_in, qkv_h, mix_h, act_h, slope_h) = refs[:8]
    (proj_h, out_h, fin_h, fout_h, point_h, depth, gain) = refs[8:15]
    g_out = refs[15]
    sent = refs[16 : 16 + groups]
    (payload, gn, du, w_in, w_out, mix, act, slope, padded, lse_t, turned, w_sem, s_sem, p_sem) = refs[16 + groups :]
    width = a_in.shape[1]
    hidden = w_in.shape[1]
    chunks = hidden // width
    tiles = length // TILE
    rows_all = slots * length
    own = width // peers
    cols = width // groups
    hidden_cols = hidden // groups
    op = scalars[2]
    place = scalars[4]
    span = length // peers
    me = scalars[5]
    pitch, _ = payload_rows(width, groups)

    def key_of(d):
        return jnp.bitwise_xor(me, d)

    def part(j):
        return pl.ds(j * width, width)

    def heads(j, pair):
        return pl.ds(pl.multiple_of(j * width + pair * 2 * HEAD, 2 * HEAD), 2 * HEAD)

    def attn_copies():
        return (
            [pltpu.make_async_copy(qkv_h.at[j], slope.at[:, part(j)], s_sem.at[j]) for j in range(3)]
            + [pltpu.make_async_copy(mix_h, mix, s_sem.at[3])]
            + [pltpu.make_async_copy(proj_h.at[b, j], w_out.at[part(j)], w_sem.at[j]) for j in range(3)]
            + [pltpu.make_async_copy(out_h.at[b], w_out.at[part(3)], w_sem.at[3])]
        )

    def conv_copies():
        return [
            pltpu.make_async_copy(mix_h, mix, s_sem.at[0]),
            pltpu.make_async_copy(point_h.at[b], w_out.at[part(0)], w_sem.at[0]),
        ]

    def ffn_copies():
        cut = [pl.ds(j * width, width) for j in range(chunks)]
        return [
            pltpu.make_async_copy(fout_h.at[b], w_out, w_sem.at[0]),
            pltpu.make_async_copy(slope_h, slope, s_sem.at[0]),
            pltpu.make_async_copy(fin_h.at[b], w_in, w_sem.at[1]),
            pltpu.make_async_copy(act_h, act, s_sem.at[1]),
        ]

    for index, copies in enumerate((attn_copies, conv_copies, ffn_copies)):

        @pl.when(op == index)
        def _():
            for copy in copies():
                copy.start()

    gain_term = jnp.zeros((1, width), wide)
    shift_term = jnp.zeros((1, width), wide)

    def norm_back(slot, start, g, rows, count):
        keep = live_of(scalars, slot, start, count, width)
        g = jnp.where(keep, g, 0.0)
        unit = unit_in[rows, :]
        gu = g * unit
        gy = g * gain[...]
        first_mean = jnp.mean(gy, axis=-1, keepdims=True)
        second_mean = jnp.mean(gu * gain[...], axis=-1, keepdims=True)
        dz = scale_in[rows, :] * (gy - first_mean - unit * second_mean)
        gn[rows, :] = dz
        du[rows, :] = dz.astype(low)
        return jnp.sum(gu, axis=0, keepdims=True), jnp.sum(g, axis=0, keepdims=True)

    for slot in range(slots):
        if first:
            for j in range(peers):
                rows = pl.ds(slot * length + j * span, span)
                for key in range(peers):

                    @pl.when(jnp.bitwise_xor(place, key) == j)
                    def _():
                        gn[rows, :] = pieces[key][slot].astype(wide)

                one, two = norm_back(slot, j * span, gn[rows, :], rows, span)
                gain_term, shift_term = gain_term + one, shift_term + two
        else:
            for t in range(tiles):
                rows = pl.ds(slot * length + t * TILE, TILE)
                one, two = norm_back(slot, t * TILE, pieces[0][rows, :], rows, TILE)
                gain_term, shift_term = gain_term + one, shift_term + two

    def spread(start, values):
        for d in range(groups):
            at = 2 * pitch + start
            payload[key_of(d), at : at + values.shape[0], :] = values.astype(low)

    spread(TAPS, gain_term)
    spread(TAPS + 1, shift_term)
    spread(TAPS + 2, jnp.full((1, width), op.astype(wide), wide))

    def turn_own(source):
        for s in range(peers):

            @pl.when(place == s)
            def _():
                turned[...] = source[:, s * own : (s + 1) * own].T

    def put_out(start, values):
        for d in range(groups):
            piece = values[d * cols : (d + 1) * cols].astype(low)
            payload[key_of(d), 0:cols, start : start + values.shape[1]] = piece

    def put_point(values):
        part = cols // peers
        for d in range(groups):
            for p in range(peers):
                piece = values[d * cols + p * part : d * cols + (p + 1) * part].astype(low)
                payload[key_of(d), 0:part, p * own : (p + 1) * own] = piece

    def put_in(d, values):
        for p in range(own // cols):
            at = slice(p * hidden_cols, (p + 1) * hidden_cols)
            payload[key_of(d), pitch : pitch + cols, at] = values[p * cols : (p + 1) * cols]

    def add_back(grad):
        if last:
            for slot in range(slots):
                rows = pl.ds(pl.multiple_of(slot * length + place * span, span), span)
                keep = live_of(scalars, slot, place * span, span, width)
                g_out[slot] = jnp.where(keep, gn[rows, :] + grad(rows), 0.0)
        else:

            @pl.loop(0, slots * tiles)
            def _(t):
                rows = pl.ds(pl.multiple_of(t * TILE, TILE), TILE)
                g_out[rows, :] = gn[rows, :] + grad(rows)

    @pl.when(op == 0)
    def _():
        copies = attn_copies()
        copies[7].wait()
        for copy in copies[:4]:
            copy.wait()
        turn_own(mix)
        put_out(3 * own, nn(turned[...], du[...]).T)

        @pl.loop(0, slots * tiles)
        def _(t):
            rows = pl.ds(pl.multiple_of(t * TILE, TILE), TILE)
            mix[rows, :] = nt(du[rows, :], w_out[part(3), :]).astype(low)

        for slot in range(slots):
            lse_t[slot] = lse_in[slot * length : (slot + 1) * length, :].T
        for slot in range(slots):
            base = slot * length

            @pl.loop(0, HEADS // 2)
            def _(pair):
                lanes = pl.ds(pl.multiple_of(pair * 2 * HEAD, 2 * HEAD), 2 * HEAD)
                every = pl.ds(base, length)
                keys = slope[every, heads(1, pair)]
                values = slope[every, heads(2, pair)]
                dk = jnp.zeros((length, 2 * HEAD), wide)
                dv = jnp.zeros((length, 2 * HEAD), wide)
                count = GRAD_TILE
                scaled_keys = keys * FACTOR
                upper = lax.broadcasted_iota(jnp.int32, (2 * HEAD, count), 0) < HEAD
                for t in range(length // count):
                    rows = pl.ds(base + t * count, count)
                    at = slice(t * count, (t + 1) * count)
                    queries = pair_rows(slope[rows, heads(0, pair)] * FACTOR)
                    grads = pair_rows(mix[rows, lanes])
                    stat = jnp.concatenate(
                        [lse_t[slot, pl.ds(pair * 2 + head, 1), at] for head in range(2)], axis=1
                    )
                    soft = jnp.exp(jnp.minimum(nt(keys, queries) - stat, 0.0))
                    product = soft * nt(values, grads)
                    inner = jnp.sum(product, axis=0, keepdims=True)
                    grad_scores = (product - soft * inner).astype(low)
                    dv = dv + nn(soft.astype(low), grads)
                    dk = dk + nn(grad_scores, queries)
                    dq = tn(scaled_keys, grad_scores)
                    dq = jnp.where(upper, dq[:, :count], dq[:, count:])
                    slope[rows, heads(0, pair)] = dq.T.astype(low)
                slope[every, heads(1, pair)] = dk.astype(low)
                slope[every, heads(2, pair)] = dv.astype(low)

        for j in range(3):
            copies[4 + j].wait()
        add_back(
            lambda rows: nt(slope[rows, part(0)], w_out[part(0), :])
            + nt(slope[rows, part(1)], w_out[part(1), :])
            + nt(slope[rows, part(2)], w_out[part(2), :])
        )
        turn_own(a_in)
        for j in range(3):
            put_out(j * own, nn(turned[...], slope[:, part(j)]).T)

    @pl.when(op == 1)
    def _():
        copies = conv_copies()
        for copy in copies:
            copy.wait()
        turn_own(mix)
        put_point(nn(turned[...], du[...]).T)

        @pl.loop(0, slots * tiles)
        def _(t):
            rows = pl.ds(pl.multiple_of(t * TILE, TILE), TILE)
            mix[rows, :] = nt(du[rows, :], w_out[part(0), :]).astype(low)

        half = TAPS // 2
        depth_terms = [jnp.zeros((1, width), wide) for _ in range(TAPS)]
        fill_padded(padded, lambda slot: a_in[pl.ds(slot * length, length), :].astype(wide), slots, length)
        for slot in range(slots):
            for t in range(tiles):
                grads = mix[pl.ds(slot * length + t * TILE, TILE), :].astype(wide)
                for offset in range(TAPS):
                    start = PAD + t * TILE + offset - half
                    moved = padded[slot, start : start + TILE, :]
                    depth_terms[offset] += jnp.sum(moved * grads, axis=0, keepdims=True)
        for offset in range(TAPS):
            spread(offset, depth_terms[offset] * used_tap(scalars, offset))
        fill_padded(padded, lambda slot: mix[pl.ds(slot * length, length), :].astype(wide), slots, length)
        for slot in range(slots):
            for t in range(tiles):
                running = jnp.zeros((TILE, width), wide)
                for offset in range(TAPS):
                    start = PAD + t * TILE - offset + half
                    tap = depth[offset : offset + 1, :] * used_tap(scalars, offset)
                    running = running + padded[slot, start : start + TILE, :] * tap
                rows = pl.ds(slot * length + t * TILE, TILE)
                gn[rows, :] = gn[rows, :] + running
        add_back(lambda rows: 0.0)

    @pl.when(op == 2)
    def _():
        copies = ffn_copies()
        copies[0].wait()
        copies[1].wait()

        @pl.loop(0, slots * tiles)
        def _(t):
            rows = pl.ds(pl.multiple_of(t * TILE, TILE), TILE)
            upstream = du[rows, :]
            for j in range(chunks):
                cut = pl.ds(j * width, width)
                df = nt(upstream, w_out[cut, :]).astype(low).astype(wide)
                slope[rows, cut] = (df * slope[rows, cut].astype(wide)).astype(low)

        copies[2].wait()
        copies[3].wait()
        put_out(0, nn(du[...].T, act[...]))
        turn_own(a_in)
        for d in range(groups):
            piece = slope[:, d * hidden_cols : (d + 1) * hidden_cols]
            put_in(d, nn(turned[...], piece).astype(low))
        add_back(lambda rows: nt(slope[rows, :], w_in[...]))

    order = sorted(range(groups), key=lambda key: key < groups // 2)
    leaving = [pltpu.make_async_copy(payload.at[key], sent[key], p_sem.at[key]) for key in order]
    for copy in leaving:
        copy.start()
    for copy in leaving:
        copy.wait()


def backward_call(b, slots, length, peers, groups, last, scalars, pieces, kept, weights, depth, gain):
    width = gain.shape[-1]
    hidden = weights[2].shape[2]
    rows = slots * length
    first = len(pieces) > 1
    _, count = payload_rows(width, groups)
    (unit, scale, a, lse, qkv, mix, act, slope) = kept
    shapes = [
        ((slots, length // peers, width) if last else (rows, width), wide),
    ] + [((count, width), low)] * groups
    return pl.pallas_call(
        functools.partial(backward_kernel, b, slots, length, peers, groups, first, last),
        out_shape=[jax.ShapeDtypeStruct(*s) for s in shapes],
        in_specs=[pl.BlockSpec(memory_space=pltpu.SMEM)]
        + [vmem_spec()] * len(pieces)
        + [vmem_spec()] * 4
        + [any_spec()] * 9
        + [vmem_spec()] * 2,
        out_specs=[vmem_spec()] + [any_spec()] * groups,
        scratch_shapes=[
            pltpu.VMEM((groups, count, width), low),
            pltpu.VMEM((rows, width), wide),
            pltpu.VMEM((rows, width), low),
            pltpu.VMEM((width, hidden), low),
            pltpu.VMEM((hidden, width), low),
            pltpu.VMEM((rows, width), low),
            pltpu.VMEM((rows, hidden // peers), low),
            pltpu.VMEM((rows, hidden), low),
            pltpu.VMEM((slots, length + 2 * PAD, width), wide),
            pltpu.VMEM((slots, 2 * HEAD, length), wide),
            pltpu.VMEM((width // peers, rows), low),
            pltpu.SemaphoreType.DMA((8,)),
            pltpu.SemaphoreType.DMA((4,)),
            pltpu.SemaphoreType.DMA((groups,)),
        ],
        compiler_params=pltpu.CompilerParams(vmem_limit_bytes=VMEM_LIMIT),
        name="backward_block",
    )(scalars, *pieces, unit, scale, a, lse, qkv, mix, act, slope, *weights, depth, gain)


def add_pieces(pieces, small, me, groups, peers):
    width = pieces[0].shape[1]
    cols = width // groups
    pitch, _ = payload_rows(width, groups)
    sums = [None] * 4

    def add(index, value):
        sums[index] = value if sums[index] is None else sums[index] + value

    for key, piece in enumerate(pieces):
        op = piece[2 * pitch : 2 * pitch + EXTRA, :].astype(wide)[TAPS + 2 : TAPS + 3, :]
        matrix = piece[0:cols, :].astype(wide)
        add(0, jnp.where(op == 0.0, matrix, 0.0))
        add(1, jnp.where(op == 2.0, matrix, 0.0))
        add(2, jnp.where(op == 2.0, piece[pitch : pitch + cols, :].astype(wide), 0.0))
        add(3, jnp.where(op == 1.0, piece[0 : cols // peers, :].astype(wide), 0.0))
        terms = piece[2 * pitch : 2 * pitch + EXTRA, :].astype(wide)
        row = lax.broadcasted_iota(jnp.int32, terms.shape, 0)
        terms = jnp.where((row < TAPS) & (op != 1.0), 0.0, terms)
        for index in range(3):
            terms = jnp.where(row == TAPS + 2 + index, (op == index).astype(wide), terms)
        terms = jnp.where(row < TAPS + 5, terms, 0.0)
        small[jnp.bitwise_xor(me, key) % len(pieces)] = terms
    total = small[0]
    for index in range(1, len(pieces)):
        total = total + small[index]
    return sums, total


def relay_kernel(groups, peers, scalars, *refs):
    pieces, (dense, small) = refs[:-2], refs[-2:]
    width = dense.shape[1]
    cols = width // groups
    pitch, point_at, small_at, _ = dense_rows(width, groups, peers)
    sums, total = add_pieces(pieces, small, scalars[5], groups, peers)
    for index in range(3):
        dense[index * pitch : index * pitch + cols, :] = sums[index].astype(low)
    dense[point_at : point_at + cols // peers, :] = sums[3].astype(low)
    dense[small_at : small_at + EXTRA, :] = total.astype(low)


def relay_call(groups, peers, scalars, pieces):
    width = pieces[0].shape[1]
    count = dense_rows(width, groups, peers)[3]
    return pl.pallas_call(
        functools.partial(relay_kernel, groups, peers),
        out_shape=jax.ShapeDtypeStruct((count, width), low),
        in_specs=[pl.BlockSpec(memory_space=pltpu.SMEM)] + [vmem_spec()] * len(pieces),
        out_specs=vmem_spec(),
        scratch_shapes=[pltpu.VMEM((len(pieces), EXTRA, width), wide)],
        compiler_params=pltpu.CompilerParams(vmem_limit_bytes=VMEM_LIMIT),
        name="relay_sum",
    )(scalars, *pieces)


def final_kernel(groups, peers, scalars, *refs):
    half = groups // 2
    inputs = refs[: BLOCKS * (half + 1)]
    (proj, out, f_in, f_out, point, depth, gain, shift) = refs[BLOCKS * (half + 1) : -1]
    small = refs[-1]
    width = inputs[0].shape[1]
    cols = width // groups
    own = width // peers
    hidden_cols = f_in.shape[2]
    pitch, point_at, small_at, _ = dense_rows(width, groups, peers)
    for b in range(BLOCKS):
        *pieces, dense = inputs[b * (half + 1) : (b + 1) * (half + 1)]
        sums, total = add_pieces(pieces, small, scalars[5], groups, peers)
        total = total.astype(low).astype(wide) + dense[small_at : small_at + EXTRA, :].astype(wide)
        share = [1.0 / total[TAPS + 2 + op : TAPS + 3 + op, :] for op in range(3)]
        for index in range(3):
            at = slice(index * pitch, index * pitch + cols)
            sums[index] = sums[index] + dense[at, :].astype(wide)
        points = sums[3] + dense[point_at : point_at + cols // peers, :].astype(wide)
        attn = sums[0] * share[0]
        for j in range(3):
            proj[b, j] = attn[:, j * own : (j + 1) * own].T
        out[b] = attn[:, 3 * own :].T
        f_out[b] = (sums[1] * share[2]).T
        inner = sums[2] * share[2]
        for p in range(own // cols):
            f_in[b, p * cols : (p + 1) * cols, :] = inner[:, p * hidden_cols : (p + 1) * hidden_cols]
        points = points * share[1]
        points = jnp.concatenate([points[:, p * own : (p + 1) * own] for p in range(peers)], axis=0)
        point[b] = points.T
        depth[b] = total[0:TAPS] * share[1]
        gain[b] = total[TAPS : TAPS + 1] * (1.0 / groups)
        shift[b] = total[TAPS + 1 : TAPS + 2] * (1.0 / groups)


def final_call(groups, peers, hidden, scalars, inputs):
    width = inputs[0].shape[1]
    rows, cols = width // peers, width // groups
    shapes = [
        (BLOCKS, 3, rows, cols),
        (BLOCKS, rows, cols),
        (BLOCKS, rows, hidden // groups),
        (BLOCKS, hidden // peers, cols),
        (BLOCKS, rows, cols),
        (BLOCKS, TAPS, width),
        (BLOCKS, 1, width),
        (BLOCKS, 1, width),
    ]
    return pl.pallas_call(
        functools.partial(final_kernel, groups, peers),
        out_shape=[jax.ShapeDtypeStruct(s, wide) for s in shapes],
        in_specs=[pl.BlockSpec(memory_space=pltpu.SMEM)] + [vmem_spec()] * len(inputs),
        out_specs=[vmem_spec()] * len(shapes),
        scratch_shapes=[pltpu.VMEM((groups // 2, EXTRA, width), wide)],
        compiler_params=pltpu.CompilerParams(vmem_limit_bytes=VMEM_LIMIT),
        name="final_sum",
    )(scalars, *inputs)


def across(piece, axis, key):
    return lax.ppermute(piece, axis, [(i, i ^ key) for i in range(lax.axis_size(axis))])


def exchange_group(piece, peers):
    parts = {0: piece}
    reach = peers // 2
    while reach:
        parts.update({key ^ reach: across(part, "seq", reach) for key, part in parts.items()})
        reach //= 2
    return [parts[key] for key in range(peers)]


def local(
    layer_in,
    lengths,
    op_ids,
    kernel_ids,
    attn_proj,
    attn_out,
    ffn_in,
    ffn_out,
    point_weights,
    depth_weights,
    norm_gains,
    norm_shifts,
    cotangent,
):
    slots, span, width = layer_in.shape
    peers = lax.axis_size("seq")
    groups = lax.axis_size("dp")
    place = lax.axis_index("seq").astype(jnp.int32)
    length = span * peers
    weights = (attn_proj, attn_out, ffn_in, ffn_out, point_weights)

    me = lax.axis_index("dp").astype(jnp.int32)
    half = groups // 2

    x_parts = exchange_group(layer_in.astype(low), peers)
    later, x_parts = lax.optimization_barrier((cotangent.astype(low), x_parts))
    cot_parts = [later] + [across(later, "seq", key) for key in range(1, peers)]

    scalars = [
        jnp.concatenate([lengths, jnp.stack([op_ids[0, b], kernel_ids[0, b], place, me])])
        for b in range(BLOCKS)
    ]
    kept = []
    pieces = x_parts
    for b in range(BLOCKS):
        outs = forward_call(
            b, slots, length, peers, b == BLOCKS - 1, scalars[b], pieces, weights,
            depth_weights[b], norm_gains[b][None], norm_shifts[b][None],
        )
        x, a, unit, scale, qkv, mix, lse, act, slope = outs
        kept.append((unit, scale, a, lse, qkv, mix, act, slope))
        pieces = [x]
    layer_out = x

    pieces = cot_parts
    near = [None] * BLOCKS
    far = [None] * BLOCKS
    for b in reversed(range(BLOCKS)):
        g, *sent = backward_call(
            b, slots, length, peers, groups, b == 0, scalars[b], pieces, kept[b], weights,
            depth_weights[b], norm_gains[b][None],
        )
        pieces = [g]
        far[b] = [sent[half]] + [across(sent[half + key], "dp", key) for key in range(1, half)]
        near[b] = [sent[0]] + [across(sent[key], "dp", key) for key in range(1, half)]
    far[1], g = lax.optimization_barrier((far[1], g))
    inputs = [None] * BLOCKS
    for b in reversed(range(BLOCKS)):
        dense = across(relay_call(groups, peers, scalars[b], far[b]), "dp", half)
        inputs[b] = near[b] + [dense]
    outs = final_call(groups, peers, ffn_in.shape[2], scalars[0], inputs[0] + inputs[1])
    *matrices, gain_grad, shift_grad = outs
    return (layer_out, g, *matrices, gain_grad[:, 0], shift_grad[:, 0])


def solution(mesh):
    placed = (
        P("dp", "seq", None),
        P("dp"),
        P("dp", None),
        P("dp", None),
        P(),
        P(),
        P(),
        P(),
        P(),
        P(),
        P(),
        P(),
        P("dp", "seq", None),
    )
    return jax.shard_map(
        local,
        mesh=mesh,
        in_specs=placed,
        out_specs=(
            P("dp", "seq", None),
            P("dp", "seq", None),
            P(None, None, "seq", "dp"),
            P(None, "seq", "dp"),
            P(None, "seq", "dp"),
            P(None, "seq", "dp"),
            P(None, "seq", "dp"),
            P(),
            P(),
            P(),
        ),
        check_vma=False,
    )
```

```python
import functools

import jax
import jax.numpy as jnp
from jax import lax
from jax.experimental import pallas as pl
from jax.experimental.pallas import tpu as pltpu
from jax.sharding import PartitionSpec as P

HEADS = 12
HEAD = 64
TAPS = 7
BLOCKS = 2
EXTRA = 16
PAD = 8
norm_eps = 1e-05
low = jnp.bfloat16
wide = jnp.float32
VMEM_LIMIT = 60 * 1024 * 1024


def nn(left, right):
    return lax.dot_general(left, right, (((1,), (0,)), ((), ())), preferred_element_type=wide)


def nt(left, right):
    return lax.dot_general(left, right, (((1,), (1,)), ((), ())), preferred_element_type=wide)


def tn(left, right):
    return lax.dot_general(left, right, (((0,), (0,)), ((), ())), preferred_element_type=wide)


def live_of(scalars, slot, start, count, width):
    at = lax.broadcasted_iota(jnp.int32, (count, width), 0) + start
    return at < scalars[slot]


def used_tap(scalars, slots, b, offset):
    return (abs(offset - TAPS // 2) <= scalars[slots + 3 + 2 * b] + 1).astype(wide)


def live_tiles(scalars, slot, size):
    return (scalars[slot] + size - 1) // size


def for_reach(scalars, slots, length, body):
    @pl.loop(0, slots)
    def _(slot):
        @pl.when(scalars[slot] <= length // 2)
        def _():
            body(slot, length // 2)

        @pl.when(scalars[slot] > length // 2)
        def _():
            body(slot, length)


def tiles_of(scalars, slots, length, body, rest):
    @pl.loop(0, slots)
    def _(slot):
        count = live_tiles(scalars, slot, TILE)

        @pl.loop(0, count)
        def _(t):
            start = pl.multiple_of(t * TILE, TILE)
            body(slot, start, pl.ds(pl.multiple_of(slot * length + start, TILE), TILE))

        if rest is not None:

            @pl.loop(count, length // TILE)
            def _(t):
                rest(pl.ds(pl.multiple_of(slot * length + t * TILE, TILE), TILE))


def fill_padded(padded, source, slots, length):
    width = padded.shape[2]

    @pl.loop(0, slots)
    def _(slot):
        padded[slot, 0:PAD, :] = jnp.zeros((PAD, width), wide)
        padded[slot, PAD + length : PAD + length + PAD, :] = jnp.zeros((PAD, width), wide)

        @pl.loop(0, length // 128)
        def _(t):
            rows = pl.ds(pl.multiple_of(slot * length + t * 128, 128), 128)
            at = pl.ds(pl.multiple_of(PAD + t * 128, PAD), 128)
            padded[slot, at, :] = source[rows, :].astype(wide)


def window(padded, slot, start):
    return padded[slot, pl.ds(pl.multiple_of(start, TILE), TILE + 2 * PAD), :]


TILE = 256
FACTOR = HEAD**-0.5


def pair_rows(tensor):
    lane = lax.broadcasted_iota(jnp.int32, tensor.shape, 1)
    none = jnp.zeros((), tensor.dtype)
    return jnp.concatenate(
        [jnp.where(lane < HEAD, tensor, none), jnp.where(lane < HEAD, none, tensor)], axis=0
    )


def forward_kernel(slots, length, peers, lengths_of, *refs):
    pieces = refs[:peers]
    (proj_h, out_h, fin_h, fout_h, point_h, depth, gain, shift) = refs[peers : peers + 8]
    refs = refs[peers + 8 :]
    layer_out = refs[0]
    saved = refs[1:8]
    (x_now, update, a_now, unit, stats, weights, mix, active, mine_active, slope, padded) = refs[8:19]
    w_sem, s_sem = refs[19:]
    scalars = lengths_of
    width = a_now.shape[1]
    hidden = slope.shape[1]
    share = mine_active.shape[1]
    span = length // peers
    chunks = hidden // width
    tiles = length // TILE
    place = scalars[slots]

    def part(j):
        return pl.ds(pl.multiple_of(j * width, width), width)

    def heads(j, pair):
        return pl.ds(pl.multiple_of(j * width + pair * 2 * HEAD, 2 * HEAD), 2 * HEAD)

    def op_of(b):
        return scalars[slots + 2 + 2 * b]

    def loads(b, op):
        w = weights.at[b]
        if op == 0:
            pairs = [(proj_h.at[b, j], j) for j in range(3)] + [(out_h.at[b], 3)]
        elif op == 1:
            pairs = [(point_h.at[b], 0)]
        else:
            pairs = [(fin_h.at[b, :, part(j)], j) for j in range(chunks)]
            pairs += [(fout_h.at[b, part(j)], chunks + j) for j in range(chunks)]
        return [pltpu.make_async_copy(source, w.at[j], w_sem.at[b, j]) for source, j in pairs]

    def saves(b, op):
        (a_h, unit_h, stats_h, qkv_h, mix_h, act_h, slope_h) = [ref.at[b] for ref in saved]
        if op == 0:
            pairs = [(slope.at[:, part(j)], qkv_h.at[j]) for j in range(3)] + [(mix, mix_h)]
        elif op == 1:
            pairs = [(mix, mix_h)]
        else:
            pairs = [(mine_active, act_h), (slope, slope_h)]
        return [
            pltpu.make_async_copy(source, target, s_sem.at[b, j])
            for j, (source, target) in enumerate(pairs)
        ]

    def common_saves(b):
        (a_h, unit_h, stats_h) = [ref.at[b] for ref in saved[:3]]
        pairs = [(a_now, a_h), (unit, unit_h), (stats, stats_h)]
        return [
            pltpu.make_async_copy(source, target, s_sem.at[b, 4 + j])
            for j, (source, target) in enumerate(pairs)
        ]

    def by_op(b, action):
        for op in range(3):

            @pl.when(op_of(b) == op)
            def _():
                action(op)

    def each_tile(body, rest):
        tiles_of(scalars, slots, length, body, rest)

    for b in range(BLOCKS):

        def start_all(op):
            for copy in loads(b, op):
                copy.start()

        by_op(b, start_all)

    for key, piece in enumerate(pieces):
        origin = jnp.bitwise_xor(place, key) * span

        @pl.loop(0, slots)
        def _(slot):
            rows = pl.ds(pl.multiple_of(slot * length + origin, span), span)
            keep = live_of(scalars, slot, origin, span, width)
            value = jnp.where(keep, piece[slot].astype(wide), 0.0)
            x_now[rows, :] = value
            a_now[rows, :] = value.astype(low)

    def attention(b):
        w = weights.at[b]

        @pl.loop(0, 3)
        def _(j):
            pltpu.make_async_copy(proj_h.at[b, j], w.at[j], w_sem.at[b, j]).wait()

            def project(slot, start, rows):
                slope[rows, part(j)] = nn(a_now[rows, :], w[j]).astype(low)

            def clear(rows):
                slope[rows, part(j)] = jnp.zeros((TILE, width), low)

            each_tile(project, clear)
            pltpu.make_async_copy(slope.at[:, part(j)], saved[3].at[b, j], s_sem.at[b, j]).start()

        def clear_mix(rows):
            mix[rows, :] = jnp.zeros((TILE, width), low)

        each_tile(lambda slot, start, rows: None, clear_mix)

        def attend(slot, reach):
            base = pl.multiple_of(slot * length, length)
            key_at = lax.broadcasted_iota(jnp.int32, (1, reach), 1)
            bias = jnp.where(key_at < scalars[slot], 0.0, -1000000000.0).astype(wide)
            lane = lax.broadcasted_iota(jnp.int32, (TILE, 2 * HEAD), 1)

            @pl.loop(0, HEADS // 2)
            def _(pair):
                keys = slope[pl.ds(base, reach), heads(1, pair)]
                values = slope[pl.ds(base, reach), heads(2, pair)]
                for t in range(reach // TILE):
                    rows = pl.ds(pl.multiple_of(base + t * TILE, TILE), TILE)
                    scores = nt(pair_rows(slope[rows, heads(0, pair)] * FACTOR), keys) + bias
                    top = jnp.max(scores, axis=-1, keepdims=True)
                    exponent = jnp.exp(scores - top)
                    total = jnp.sum(exponent, axis=-1, keepdims=True)
                    mixed = nn(exponent.astype(low), values) * (1.0 / total)
                    stat = top + jnp.log(total)
                    kept = jnp.where(lane == pair * 2, stat[:TILE], stats[rows, :])
                    stats[rows, :] = jnp.where(lane == pair * 2 + 1, stat[TILE:], kept)
                    both = jnp.where(lane < HEAD, mixed[:TILE], mixed[TILE:])
                    mix[rows, heads(0, pair)] = both.astype(low)

        for_reach(scalars, slots, length, attend)
        saves(b, 0)[3].start()
        loads(b, 0)[3].wait()

        def out(slot, start, rows):
            update[rows, :] = nn(mix[rows, :], w[3])

        each_tile(out, None)

    def convolution(b):
        fill_padded(padded, a_now, slots, length)
        loads(b, 1)[0].wait()

        def run(slot, start, rows):
            near = window(padded, slot, start)
            running = jnp.zeros((TILE, width), wide)
            for offset in range(TAPS):
                at = PAD + offset - TAPS // 2
                tap = depth[b, offset : offset + 1, :] * used_tap(scalars, slots, b, offset)
                running = running + near[at : at + TILE] * tap
            mix[rows, :] = running.astype(low)
            update[rows, :] = nn(running.astype(low), weights[b, 0])

        def clear(rows):
            mix[rows, :] = jnp.zeros((TILE, width), low)

        each_tile(run, clear)
        saves(b, 1)[0].start()

    def feed_forward(b):
        w = weights.at[b]
        mine = pl.ds(pl.multiple_of(place * share, 128), share)

        def run(slot, start, rows):
            opening = (start == 0) & (slot == 0)
            update[rows, :] = jnp.zeros((TILE, width), wide)

            @pl.loop(0, chunks)
            def _(j):
                @pl.when(opening)
                def _():
                    pltpu.make_async_copy(fin_h.at[b, :, part(j)], w.at[j], w_sem.at[b, j]).wait()
                    pltpu.make_async_copy(
                        fout_h.at[b, part(j)], w.at[chunks + j], w_sem.at[b, chunks + j]
                    ).wait()

                h = nn(a_now[rows, :], w[j])
                cdf = 0.5 * (1.0 + lax.erf(h * (0.5**0.5)))
                density = jnp.exp(-0.5 * h * h) * 0.3989422804014327
                value = (h * cdf).astype(low)
                active[:, part(j)] = value
                slope[rows, part(j)] = (cdf + h * density).astype(low)
                update[rows, :] += nn(value, w[chunks + j])

            mine_active[rows, :] = active[:, mine]

        def clear(rows):
            mine_active[rows, :] = jnp.zeros((TILE, share), low)

        each_tile(run, clear)
        for save in saves(b, 2):
            save.start()

    @pl.loop(0, BLOCKS)
    def _(b):
        common_saves(b)[0].start()

        @pl.when(b > 0)
        def _():
            def wait_saves(op):
                for save in saves(b - 1, op):
                    save.wait()

            by_op(b - 1, wait_saves)
            for save in common_saves(b - 1)[1:]:
                save.wait()

        for op, branch in enumerate((attention, convolution, feed_forward)):

            @pl.when(op_of(b) == op)
            def _():
                branch(b)

        common_saves(b)[0].wait()

        def norm(slot, start, rows):
            z = x_now[rows, :] + update[rows, :]
            center = z - jnp.mean(z, axis=-1, keepdims=True)
            scale = lax.rsqrt(jnp.mean(center * center, axis=-1, keepdims=True) + norm_eps)
            value = center * scale
            unit[rows, :] = value
            lane = lax.broadcasted_iota(jnp.int32, (TILE, 2 * HEAD), 1)
            stats[rows, :] = jnp.where(lane == HEADS, scale, stats[rows, :])
            keep = live_of(scalars, slot, start, TILE, width)
            value = jnp.where(keep, value * gain[pl.ds(b, 1), :] + shift[pl.ds(b, 1), :], 0.0)
            x_now[rows, :] = value
            a_now[rows, :] = value.astype(low)

        def clear(rows):
            x_now[rows, :] = jnp.zeros((TILE, width), wide)
            a_now[rows, :] = jnp.zeros((TILE, width), low)

        each_tile(norm, clear)
        for save in common_saves(b)[1:]:
            save.start()

    for slot in range(slots):
        rows = pl.ds(pl.multiple_of(slot * length + place * span, span), span)
        layer_out[slot] = x_now[rows, :]

    def wait_last(op):
        for save in saves(BLOCKS - 1, op):
            save.wait()

    by_op(BLOCKS - 1, wait_last)
    for save in common_saves(BLOCKS - 1)[1:]:
        save.wait()


def any_spec():
    return pl.BlockSpec(memory_space=pl.ANY)


def vmem_spec():
    return pl.BlockSpec(memory_space=pltpu.VMEM)


def forward_call(slots, length, peers, scalars, pieces, weights, depth, gain, shift):
    width = gain.shape[-1]
    hidden = weights[2].shape[2]
    rows = slots * length
    shapes = [((slots, length // peers, width), wide)]
    shapes += [
        ((BLOCKS, rows, width), low),
        ((BLOCKS, rows, width), wide),
        ((BLOCKS, rows, 2 * HEAD), wide),
        ((BLOCKS, 3, rows, width), low),
        ((BLOCKS, rows, width), low),
        ((BLOCKS, rows, hidden // peers), low),
        ((BLOCKS, rows, hidden), low),
    ]
    return pl.pallas_call(
        functools.partial(forward_kernel, slots, length, peers),
        out_shape=[jax.ShapeDtypeStruct(*s) for s in shapes],
        in_specs=[pl.BlockSpec(memory_space=pltpu.SMEM)]
        + [vmem_spec()] * len(pieces)
        + [any_spec()] * 5
        + [vmem_spec()] * 3,
        out_specs=[vmem_spec()] + [any_spec()] * (len(shapes) - 1),
        scratch_shapes=[
            pltpu.VMEM((rows, width), wide),
            pltpu.VMEM((rows, width), wide),
            pltpu.VMEM((rows, width), low),
            pltpu.VMEM((rows, width), wide),
            pltpu.VMEM((rows, 2 * HEAD), wide),
            pltpu.VMEM((BLOCKS, 8, width, width), low),
            pltpu.VMEM((rows, width), low),
            pltpu.VMEM((TILE, hidden), low),
            pltpu.VMEM((rows, hidden // peers), low),
            pltpu.VMEM((rows, hidden), low),
            pltpu.VMEM((slots, length + 2 * PAD, width), wide),
            pltpu.SemaphoreType.DMA((BLOCKS, 8)),
            pltpu.SemaphoreType.DMA((BLOCKS, 8)),
        ],
        compiler_params=pltpu.CompilerParams(vmem_limit_bytes=VMEM_LIMIT),
        name="forward_blocks",
    )(scalars, *pieces, *weights, depth, gain, shift)


def up16(count):
    return -(-count // 16) * 16


def payload_rows(width, groups):
    pitch = up16(width // groups)
    return pitch, 2 * pitch + EXTRA


def dense_rows(width, groups, peers):
    pitch = up16(width // groups)
    tail = up16(width // groups // peers)
    return pitch, 3 * pitch, 3 * pitch + tail, 3 * pitch + tail + EXTRA


def backward_kernel(b, slots, length, peers, groups, first, last, scalars, *refs):
    pieces = refs[: (peers if first else 1)]
    refs = refs[len(pieces) :]
    (a_h, unit_h, stats_h, qkv_h, mix_h, act_h, slope_h) = [ref.at[b] for ref in refs[:7]]
    (proj_h, out_h, fin_h, fout_h, point_h, depth, gain) = refs[7:14]
    g_out = refs[14]
    sent = refs[15 : 15 + groups]
    (payload, gn, du, a_in, unit, stats, w_in, w_out, mix, act, slope, padded, stats_t, turned, small) = refs[
        15 + groups : 30 + groups
    ]
    (w_sem, s_sem, c_sem, p_sem) = refs[30 + groups :]
    width = a_in.shape[1]
    hidden = w_in.shape[1]
    chunks = hidden // width
    tiles = length // TILE
    own = width // peers
    cols = width // groups
    hidden_cols = hidden // groups
    place = scalars[slots]
    me = scalars[slots + 1]
    op = scalars[slots + 2 + 2 * b]
    span = length // peers
    pitch, _ = payload_rows(width, groups)

    def key_of(d):
        return jnp.bitwise_xor(me, d)

    def part(j):
        return pl.ds(j * width, width)

    def heads(j, pair):
        return pl.ds(pl.multiple_of(j * width + pair * 2 * HEAD, 2 * HEAD), 2 * HEAD)

    def slot_copies(slot):
        rows = pl.ds(pl.multiple_of(slot * length, length), length)
        copies = [pltpu.make_async_copy(unit_h.at[rows], unit.at[rows], c_sem.at[2 * slot])]
        if not first:
            copies.append(
                pltpu.make_async_copy(pieces[0].at[rows], gn.at[rows], c_sem.at[2 * slot + 1])
            )
        return copies

    def stats_copy():
        return pltpu.make_async_copy(stats_h, stats, c_sem.at[2 * slots])

    def input_copy():
        return pltpu.make_async_copy(a_h, a_in, c_sem.at[2 * slots + 1])

    def attn_copies():
        return (
            [
                pltpu.make_async_copy(qkv_h.at[j], slope.at[:, part(j)], s_sem.at[j])
                for j in range(3)
            ]
            + [pltpu.make_async_copy(mix_h, mix, s_sem.at[3])]
            + [
                pltpu.make_async_copy(proj_h.at[b, j], w_out.at[part(j)], w_sem.at[j])
                for j in range(3)
            ]
            + [pltpu.make_async_copy(out_h.at[b], w_out.at[part(3)], w_sem.at[3])]
        )

    def conv_copies():
        return [
            pltpu.make_async_copy(mix_h, mix, s_sem.at[0]),
            pltpu.make_async_copy(point_h.at[b], w_out.at[part(0)], w_sem.at[0]),
        ]

    def ffn_copies():
        return [
            pltpu.make_async_copy(fout_h.at[b], w_out, w_sem.at[0]),
            pltpu.make_async_copy(slope_h, slope, s_sem.at[0]),
            pltpu.make_async_copy(fin_h.at[b], w_in, w_sem.at[1]),
            pltpu.make_async_copy(act_h, act, s_sem.at[1]),
        ]

    stats_copy().start()
    for slot in range(slots):
        for copy in slot_copies(slot):
            copy.start()
    for index, copies in enumerate((attn_copies, conv_copies, ffn_copies)):

        @pl.when(op == index)
        def _():
            for copy in copies():
                copy.start()

    input_copy().start()

    def each_tile(body, rest):
        tiles_of(scalars, slots, length, body, rest)

    small[...] = jnp.zeros(small.shape, wide)
    stats_copy().wait()

    @pl.loop(0, slots)
    def _(slot):
        for copy in slot_copies(slot):
            copy.wait()

        @pl.loop(0, peers)
        def _(j):
            start = pl.multiple_of(j * span, span)
            rows = pl.ds(pl.multiple_of(slot * length + start, span), span)

            @pl.when(start < scalars[slot])
            def _():
                if first:
                    for key in range(peers):

                        @pl.when(jnp.bitwise_xor(place, key) == j)
                        def _():
                            gn[rows, :] = pieces[key][slot].astype(wide)

                keep = live_of(scalars, slot, start, span, width)
                g = jnp.where(keep, gn[rows, :], 0.0)
                value = unit[rows, :]
                gu = g * value
                gy = g * gain[b : b + 1, :]
                one = jnp.mean(gy, axis=-1, keepdims=True)
                two = jnp.mean(gu * gain[b : b + 1, :], axis=-1, keepdims=True)
                dz = stats[rows, HEADS : HEADS + 1] * (gy - one - value * two)
                gn[rows, :] = dz
                du[rows, :] = dz.astype(low)
                small[TAPS : TAPS + 1, :] += jnp.sum(gu, axis=0, keepdims=True)
                small[TAPS + 1 : TAPS + 2, :] += jnp.sum(g, axis=0, keepdims=True)

            @pl.when(start >= scalars[slot])
            def _():
                gn[rows, :] = jnp.zeros((span, width), wide)
                du[rows, :] = jnp.zeros((span, width), low)

    small[TAPS + 2 : TAPS + 3, :] = jnp.full((1, width), op.astype(wide), wide)
    input_copy().wait()

    def turn_own(source):
        for s in range(peers):

            @pl.when(place == s)
            def _():
                turned[...] = source[:, s * own : (s + 1) * own].T

    def put_out(start, values):
        for d in range(groups):
            piece = values[d * cols : (d + 1) * cols].astype(low)
            payload[key_of(d), 0:cols, start : start + values.shape[1]] = piece

    def put_point(values):
        count = cols // peers
        for d in range(groups):
            for p in range(peers):
                piece = values[d * cols + p * count : d * cols + (p + 1) * count].astype(low)
                payload[key_of(d), 0:count, p * own : (p + 1) * own] = piece

    def put_in(d, values):
        for p in range(own // cols):
            at = slice(p * hidden_cols, (p + 1) * hidden_cols)
            payload[key_of(d), pitch : pitch + cols, at] = values[p * cols : (p + 1) * cols]

    def add_back(grad):
        if last:
            @pl.loop(0, slots)
            def _(slot):
                rows = pl.ds(pl.multiple_of(slot * length + place * span, span), span)
                keep = live_of(scalars, slot, place * span, span, width)

                @pl.when(place * span < scalars[slot])
                def _():
                    g_out[slot] = jnp.where(keep, gn[rows, :] + grad(rows), 0.0)

                @pl.when(place * span >= scalars[slot])
                def _():
                    g_out[slot] = jnp.zeros((span, width), wide)

        else:

            def add(slot, start, rows):
                g_out[rows, :] = gn[rows, :] + grad(rows)

            each_tile(add, None)

    @pl.when(op == 0)
    def _():
        copies = attn_copies()
        copies[7].wait()
        for copy in copies[:4]:
            copy.wait()
        turn_own(mix)
        put_out(3 * own, nn(turned[...], du[...]).T)

        def back(slot, start, rows):
            mix[rows, :] = nt(du[rows, :], w_out[part(3), :]).astype(low)

        def clear(rows):
            for j in range(3):
                slope[rows, part(j)] = jnp.zeros((TILE, width), low)

        each_tile(back, clear)

        @pl.loop(0, slots)
        def _(slot):
            stats_t[slot] = stats[pl.ds(pl.multiple_of(slot * length, length), length), :].T

        def attend(slot, reach):
            every = pl.ds(pl.multiple_of(slot * length, length), reach)
            upper = lax.broadcasted_iota(jnp.int32, (2 * HEAD, reach), 0) < HEAD

            @pl.loop(0, HEADS // 2)
            def _(pair):
                keys = slope[every, heads(1, pair)]
                values = slope[every, heads(2, pair)]
                queries = pair_rows(slope[every, heads(0, pair)] * FACTOR)
                grads = pair_rows(mix[every, heads(0, pair)])
                stat = jnp.concatenate(
                    [stats_t[slot, pl.ds(pair * 2 + head, 1), 0:reach] for head in range(2)], axis=1
                )
                soft = jnp.exp(jnp.minimum(nt(keys, queries) - stat, 0.0))
                product = soft * nt(values, grads)
                inner = jnp.sum(product, axis=0, keepdims=True)
                grad_scores = (product - soft * inner).astype(low)
                dq = tn(keys * FACTOR, grad_scores)
                dq = jnp.where(upper, dq[:, :reach], dq[:, reach:])
                slope[every, heads(0, pair)] = dq.T.astype(low)
                slope[every, heads(1, pair)] = nn(grad_scores, queries).astype(low)
                slope[every, heads(2, pair)] = nn(soft.astype(low), grads).astype(low)

        for_reach(scalars, slots, length, attend)
        for j in range(3):
            copies[4 + j].wait()
        turn_own(a_in)

        for j in range(3):
            put_out(j * own, nn(turned[...], slope[:, part(j)]).T)

        def grad(rows):
            total = nt(slope[rows, part(0)], w_out[part(0), :])
            for j in range(1, 3):
                total = total + nt(slope[rows, part(j)], w_out[part(j), :])
            return total

        add_back(grad)

    @pl.when(op == 1)
    def _():
        copies = conv_copies()
        for copy in copies:
            copy.wait()
        turn_own(mix)
        put_point(nn(turned[...], du[...]).T)

        def back(slot, start, rows):
            mix[rows, :] = nt(du[rows, :], w_out[part(0), :]).astype(low)

        def clear(rows):
            mix[rows, :] = jnp.zeros((TILE, width), low)

        each_tile(back, clear)
        fill_padded(padded, a_in, slots, length)

        def depth_terms(slot, start, rows):
            near = window(padded, slot, start)
            grads = mix[rows, :].astype(wide)
            for offset in range(TAPS):
                at = PAD + offset - TAPS // 2
                term = jnp.sum(near[at : at + TILE] * grads, axis=0, keepdims=True)
                small[offset : offset + 1, :] += term * used_tap(scalars, slots, b, offset)

        each_tile(depth_terms, None)
        fill_padded(padded, mix, slots, length)

        def spread(slot, start, rows):
            near = window(padded, slot, start)
            running = gn[rows, :]
            for offset in range(TAPS):
                at = PAD - offset + TAPS // 2
                tap = depth[b, offset : offset + 1, :] * used_tap(scalars, slots, b, offset)
                running = running + near[at : at + TILE] * tap
            gn[rows, :] = running

        each_tile(spread, None)
        add_back(lambda rows: 0.0)

    @pl.when(op == 2)
    def _():
        copies = ffn_copies()
        copies[0].wait()
        copies[1].wait()

        def back(slot, start, rows):
            upstream = du[rows, :]
            for j in range(chunks):
                df = nt(upstream, w_out[part(j), :]).astype(low).astype(wide)
                slope[rows, part(j)] = (df * slope[rows, part(j)].astype(wide)).astype(low)

        def clear(rows):
            slope[rows, :] = jnp.zeros((TILE, hidden), low)

        each_tile(back, clear)
        copies[2].wait()
        copies[3].wait()
        put_out(0, nn(du[...].T, act[...]))
        turn_own(a_in)
        for d in range(groups):
            piece = slope[:, d * hidden_cols : (d + 1) * hidden_cols]
            put_in(d, nn(turned[...], piece).astype(low))
        add_back(lambda rows: nt(slope[rows, :], w_in[...]))

    for d in range(groups):
        payload[d, 2 * pitch : 2 * pitch + EXTRA, :] = small[...].astype(low)
    order = sorted(range(groups), key=lambda key: key < groups // 2)
    leaving = [pltpu.make_async_copy(payload.at[key], sent[key], p_sem.at[key]) for key in order]
    for copy in leaving:
        copy.start()
    for copy in leaving:
        copy.wait()


def backward_call(b, slots, length, peers, groups, scalars, pieces, kept, weights, depth, gain):
    width = gain.shape[-1]
    hidden = weights[2].shape[2]
    rows = slots * length
    first = b == BLOCKS - 1
    last = b == 0
    _, count = payload_rows(width, groups)
    shapes = [
        ((slots, length // peers, width) if last else (rows, width), wide),
    ] + [((count, width), low)] * groups
    return pl.pallas_call(
        functools.partial(backward_kernel, b, slots, length, peers, groups, first, last),
        out_shape=[jax.ShapeDtypeStruct(*s) for s in shapes],
        in_specs=[pl.BlockSpec(memory_space=pltpu.SMEM)]
        + [vmem_spec() if first else any_spec()] * len(pieces)
        + [any_spec()] * 12
        + [vmem_spec()] * 2,
        out_specs=[vmem_spec()] + [any_spec()] * groups,
        scratch_shapes=[
            pltpu.VMEM((groups, count, width), low),
            pltpu.VMEM((rows, width), wide),
            pltpu.VMEM((rows, width), low),
            pltpu.VMEM((rows, width), low),
            pltpu.VMEM((rows, width), wide),
            pltpu.VMEM((rows, 2 * HEAD), wide),
            pltpu.VMEM((width, hidden), low),
            pltpu.VMEM((hidden, width), low),
            pltpu.VMEM((rows, width), low),
            pltpu.VMEM((rows, hidden // peers), low),
            pltpu.VMEM((rows, hidden), low),
            pltpu.VMEM((slots, length + 2 * PAD, width), wide),
            pltpu.VMEM((slots, 2 * HEAD, length), wide),
            pltpu.VMEM((width // peers, rows), low),
            pltpu.VMEM((EXTRA, width), wide),
            pltpu.SemaphoreType.DMA((4,)),
            pltpu.SemaphoreType.DMA((4,)),
            pltpu.SemaphoreType.DMA((2 * slots + 2,)),
            pltpu.SemaphoreType.DMA((groups,)),
        ],
        compiler_params=pltpu.CompilerParams(vmem_limit_bytes=VMEM_LIMIT),
        name="backward_block",
    )(scalars, *pieces, *kept, *weights, depth, gain)


def add_pieces(pieces, small, me, groups, peers):
    width = pieces[0].shape[1]
    cols = width // groups
    pitch, _ = payload_rows(width, groups)
    sums = [None] * 4

    def add(index, value):
        sums[index] = value if sums[index] is None else sums[index] + value

    for key, piece in enumerate(pieces):
        op = piece[2 * pitch : 2 * pitch + EXTRA, :].astype(wide)[TAPS + 2 : TAPS + 3, :]
        matrix = piece[0:cols, :].astype(wide)
        add(0, jnp.where(op == 0.0, matrix, 0.0))
        add(1, jnp.where(op == 2.0, matrix, 0.0))
        add(2, jnp.where(op == 2.0, piece[pitch : pitch + cols, :].astype(wide), 0.0))
        add(3, jnp.where(op == 1.0, piece[0 : cols // peers, :].astype(wide), 0.0))
        terms = piece[2 * pitch : 2 * pitch + EXTRA, :].astype(wide)
        row = lax.broadcasted_iota(jnp.int32, terms.shape, 0)
        terms = jnp.where((row < TAPS) & (op != 1.0), 0.0, terms)
        for index in range(3):
            terms = jnp.where(row == TAPS + 2 + index, (op == index).astype(wide), terms)
        terms = jnp.where(row < TAPS + 5, terms, 0.0)
        small[jnp.bitwise_xor(me, key) % len(pieces)] = terms
    total = small[0]
    for index in range(1, len(pieces)):
        total = total + small[index]
    return sums, total


def relay_kernel(groups, peers, slots, scalars, *refs):
    pieces, (dense, small) = refs[:-2], refs[-2:]
    width = dense.shape[1]
    cols = width // groups
    pitch, point_at, small_at, _ = dense_rows(width, groups, peers)
    sums, total = add_pieces(pieces, small, scalars[slots + 1], groups, peers)
    for index in range(3):
        dense[index * pitch : index * pitch + cols, :] = sums[index].astype(low)
    dense[point_at : point_at + cols // peers, :] = sums[3].astype(low)
    dense[small_at : small_at + EXTRA, :] = total.astype(low)


def relay_call(groups, peers, slots, scalars, pieces):
    width = pieces[0].shape[1]
    count = dense_rows(width, groups, peers)[3]
    return pl.pallas_call(
        functools.partial(relay_kernel, groups, peers, slots),
        out_shape=jax.ShapeDtypeStruct((count, width), low),
        in_specs=[pl.BlockSpec(memory_space=pltpu.SMEM)] + [vmem_spec()] * len(pieces),
        out_specs=vmem_spec(),
        scratch_shapes=[pltpu.VMEM((len(pieces), EXTRA, width), wide)],
        compiler_params=pltpu.CompilerParams(vmem_limit_bytes=VMEM_LIMIT),
        name="relay_sum",
    )(scalars, *pieces)


def final_kernel(groups, peers, slots, scalars, *refs):
    half = groups // 2
    inputs = refs[: BLOCKS * (half + 1)]
    (proj, out, f_in, f_out, point, depth, gain, shift) = refs[BLOCKS * (half + 1) : -1]
    small = refs[-1]
    width = inputs[0].shape[1]
    cols = width // groups
    own = width // peers
    hidden_cols = f_in.shape[2]
    pitch, point_at, small_at, _ = dense_rows(width, groups, peers)
    for b in range(BLOCKS):
        *pieces, dense = inputs[b * (half + 1) : (b + 1) * (half + 1)]
        sums, total = add_pieces(pieces, small, scalars[slots + 1], groups, peers)
        total = total.astype(low).astype(wide) + dense[small_at : small_at + EXTRA, :].astype(wide)
        share = [1.0 / total[TAPS + 2 + op : TAPS + 3 + op, :] for op in range(3)]
        for index in range(3):
            at = slice(index * pitch, index * pitch + cols)
            sums[index] = sums[index] + dense[at, :].astype(wide)
        points = sums[3] + dense[point_at : point_at + cols // peers, :].astype(wide)
        attn = sums[0] * share[0]
        for j in range(3):
            proj[b, j] = attn[:, j * own : (j + 1) * own].T
        out[b] = attn[:, 3 * own :].T
        f_out[b] = sums[1] * share[2]
        inner = sums[2] * share[2]
        for p in range(own // cols):
            f_in[b, p * cols : (p + 1) * cols, :] = inner[:, p * hidden_cols : (p + 1) * hidden_cols]
        points = points * share[1]
        points = jnp.concatenate([points[:, p * own : (p + 1) * own] for p in range(peers)], axis=0)
        point[b] = points.T
        depth[:, b, :] = total[0:TAPS] * share[1]
        gain[b : b + 1, :] = total[TAPS : TAPS + 1] * (1.0 / groups)
        shift[b : b + 1, :] = total[TAPS + 1 : TAPS + 2] * (1.0 / groups)


def final_call(groups, peers, slots, hidden, scalars, inputs):
    width = inputs[0].shape[1]
    rows, cols = width // peers, width // groups
    shapes = [
        (BLOCKS, 3, rows, cols),
        (BLOCKS, rows, cols),
        (BLOCKS, rows, hidden // groups),
        (BLOCKS, cols, hidden // peers),
        (BLOCKS, rows, cols),
        (TAPS, BLOCKS, width),
        (BLOCKS, width),
        (BLOCKS, width),
    ]
    return pl.pallas_call(
        functools.partial(final_kernel, groups, peers, slots),
        out_shape=[jax.ShapeDtypeStruct(s, wide) for s in shapes],
        in_specs=[pl.BlockSpec(memory_space=pltpu.SMEM)] + [vmem_spec()] * len(inputs),
        out_specs=[vmem_spec()] * len(shapes),
        scratch_shapes=[pltpu.VMEM((groups // 2, EXTRA, width), wide)],
        compiler_params=pltpu.CompilerParams(vmem_limit_bytes=VMEM_LIMIT),
        name="final_sum",
    )(scalars, *inputs)


def across(piece, axis, key):
    return lax.ppermute(piece, axis, [(i, i ^ key) for i in range(lax.axis_size(axis))])


def exchange_group(piece, peers):
    parts = {0: piece}
    reach = peers // 2
    while reach:
        parts.update({key ^ reach: across(part, "seq", reach) for key, part in parts.items()})
        reach //= 2
    return [parts[key] for key in range(peers)]


def local(
    layer_in,
    lengths,
    op_ids,
    kernel_ids,
    attn_proj,
    attn_out,
    ffn_in,
    ffn_out,
    point_weights,
    depth_weights,
    norm_gains,
    norm_shifts,
    cotangent,
):
    slots, span, width = layer_in.shape
    peers = lax.axis_size("seq")
    groups = lax.axis_size("dp")
    place = lax.axis_index("seq").astype(jnp.int32)
    length = span * peers
    weights = (attn_proj, attn_out, ffn_in, ffn_out, point_weights)

    me = lax.axis_index("dp").astype(jnp.int32)
    half = groups // 2

    x_parts = exchange_group(layer_in.astype(low), peers)
    later, x_parts = lax.optimization_barrier((cotangent.astype(low), x_parts))
    cot_parts = [later] + [across(later, "seq", key) for key in range(1, peers)]

    chosen = jnp.stack([op_ids[0], kernel_ids[0]], axis=1).reshape(-1)
    scalars = jnp.concatenate([lengths, jnp.stack([place, me]), chosen])
    layer_out, *saved = forward_call(
        slots, length, peers, scalars, x_parts, weights, depth_weights, norm_gains, norm_shifts
    )

    pieces = cot_parts
    near = [None] * BLOCKS
    far = [None] * BLOCKS
    for b in reversed(range(BLOCKS)):
        g, *sent = backward_call(
            b, slots, length, peers, groups, scalars, pieces, saved,
            weights, depth_weights, norm_gains,
        )
        pieces = [g]
        far[b] = [sent[half]] + [across(sent[half + key], "dp", key) for key in range(1, half)]
        near[b] = [sent[0]] + [across(sent[key], "dp", key) for key in range(1, half)]
    far[1], near[1], g = lax.optimization_barrier((far[1], near[1], g))
    inputs = [None] * BLOCKS
    for b in reversed(range(BLOCKS)):
        dense = across(relay_call(groups, peers, slots, scalars, far[b]), "dp", half)
        inputs[b] = near[b] + [dense]
    proj, out, f_in, f_out, point, depth, gain, shift = final_call(
        groups, peers, slots, ffn_in.shape[2], scalars, inputs[0] + inputs[1]
    )
    f_out = jnp.swapaxes(f_out, 1, 2)
    depth = jnp.swapaxes(depth, 0, 1)
    return (layer_out, g, proj, out, f_in, f_out, point, depth, gain, shift)


def solution(mesh):
    placed = (
        P("dp", "seq", None),
        P("dp"),
        P("dp", None),
        P("dp", None),
        P(),
        P(),
        P(),
        P(),
        P(),
        P(),
        P(),
        P(),
        P("dp", "seq", None),
    )
    return jax.shard_map(
        local,
        mesh=mesh,
        in_specs=placed,
        out_specs=(
            P("dp", "seq", None),
            P("dp", "seq", None),
            P(None, None, "seq", "dp"),
            P(None, "seq", "dp"),
            P(None, "seq", "dp"),
            P(None, "seq", "dp"),
            P(None, "seq", "dp"),
            P(),
            P(),
            P(),
        ),
        check_vma=False,
    )
```

```python
import functools

import jax
import jax.numpy as jnp
from jax import lax
from jax.experimental import pallas as pl
from jax.experimental.pallas import tpu as pltpu
from jax.sharding import PartitionSpec as P

HEADS = 12
HEAD = 64
TAPS = 7
BLOCKS = 2
EXTRA = 16
PAD = 8
norm_eps = 1e-05
low = jnp.bfloat16
wide = jnp.float32
VMEM_LIMIT = 60 * 1024 * 1024


def nn(left, right):
    return lax.dot_general(left, right, (((1,), (0,)), ((), ())), preferred_element_type=wide)


def nt(left, right):
    return lax.dot_general(left, right, (((1,), (1,)), ((), ())), preferred_element_type=wide)


def tn(left, right):
    return lax.dot_general(left, right, (((0,), (0,)), ((), ())), preferred_element_type=wide)


def live_of(scalars, slot, start, count, width):
    at = lax.broadcasted_iota(jnp.int32, (count, width), 0) + start
    return at < scalars[slot]


def used_tap(scalars, slots, b, offset):
    return (abs(offset - TAPS // 2) <= scalars[slots + 3 + 2 * b] + 1).astype(wide)


def live_tiles(scalars, slot, size):
    return (scalars[slot] + size - 1) // size


def for_reach(scalars, slots, length, body):
    @pl.loop(0, slots)
    def _(slot):
        @pl.when(scalars[slot] <= length // 2)
        def _():
            body(slot, length // 2)

        @pl.when(scalars[slot] > length // 2)
        def _():
            body(slot, length)


def tiles_of(scalars, slots, length, body, rest):
    @pl.loop(0, slots)
    def _(slot):
        count = live_tiles(scalars, slot, TILE)

        @pl.loop(0, count)
        def _(t):
            start = pl.multiple_of(t * TILE, TILE)
            body(slot, start, pl.ds(pl.multiple_of(slot * length + start, TILE), TILE))

        if rest is not None:

            @pl.loop(count, length // TILE)
            def _(t):
                rest(pl.ds(pl.multiple_of(slot * length + t * TILE, TILE), TILE))


def fill_padded(padded, source, slots, length):
    width = padded.shape[2]

    @pl.loop(0, slots)
    def _(slot):
        padded[slot, 0:PAD, :] = jnp.zeros((PAD, width), wide)
        padded[slot, PAD + length : PAD + length + PAD, :] = jnp.zeros((PAD, width), wide)

        @pl.loop(0, length // 128)
        def _(t):
            rows = pl.ds(pl.multiple_of(slot * length + t * 128, 128), 128)
            at = pl.ds(pl.multiple_of(PAD + t * 128, PAD), 128)
            padded[slot, at, :] = source[rows, :].astype(wide)


def window(padded, slot, start):
    return padded[slot, pl.ds(pl.multiple_of(start, TILE), TILE + 2 * PAD), :]


TILE = 256
FACTOR = HEAD**-0.5


def pair_rows(tensor):
    lane = lax.broadcasted_iota(jnp.int32, tensor.shape, 1)
    none = jnp.zeros((), tensor.dtype)
    return jnp.concatenate(
        [jnp.where(lane < HEAD, tensor, none), jnp.where(lane < HEAD, none, tensor)], axis=0
    )


def forward_kernel(slots, length, peers, lengths_of, *refs):
    pieces = refs[:peers]
    (proj_h, out_h, fin_h, fout_h, point_h, depth, gain, shift) = refs[peers : peers + 8]
    refs = refs[peers + 8 :]
    layer_out = refs[0]
    saved = refs[1:8]
    (x_now, update, a_now, unit, stats, weights, mix, active, mine_active, slope, padded) = refs[8:19]
    w_sem, s_sem = refs[19:]
    scalars = lengths_of
    width = a_now.shape[1]
    hidden = slope.shape[1]
    share = mine_active.shape[1]
    span = length // peers
    chunks = hidden // width
    tiles = length // TILE
    place = scalars[slots]

    def part(j):
        return pl.ds(pl.multiple_of(j * width, width), width)

    def heads(j, pair):
        return pl.ds(pl.multiple_of(j * width + pair * 2 * HEAD, 2 * HEAD), 2 * HEAD)

    def op_of(b):
        return scalars[slots + 2 + 2 * b]

    def loads(b, op):
        w = weights.at[b]
        if op == 0:
            pairs = [(proj_h.at[b, j], j) for j in range(3)] + [(out_h.at[b], 3)]
        elif op == 1:
            pairs = [(point_h.at[b], 0)]
        else:
            pairs = [(fin_h.at[b, :, part(j)], j) for j in range(chunks)]
            pairs += [(fout_h.at[b, part(j)], chunks + j) for j in range(chunks)]
        return [pltpu.make_async_copy(source, w.at[j], w_sem.at[b, j]) for source, j in pairs]

    def saves(b, op):
        (a_h, unit_h, stats_h, qkv_h, mix_h, act_h, slope_h) = [ref.at[b] for ref in saved]
        if op == 0:
            pairs = [(slope.at[:, part(j)], qkv_h.at[j]) for j in range(3)] + [(mix, mix_h)]
        elif op == 1:
            pairs = [(mix, mix_h)]
        else:
            pairs = [(mine_active, act_h), (slope, slope_h)]
        return [
            pltpu.make_async_copy(source, target, s_sem.at[b, j])
            for j, (source, target) in enumerate(pairs)
        ]

    def common_saves(b):
        (a_h, unit_h, stats_h) = [ref.at[b] for ref in saved[:3]]
        pairs = [(a_now, a_h), (unit, unit_h), (stats, stats_h)]
        return [
            pltpu.make_async_copy(source, target, s_sem.at[b, 4 + j])
            for j, (source, target) in enumerate(pairs)
        ]

    def by_op(b, action):
        for op in range(3):

            @pl.when(op_of(b) == op)
            def _():
                action(op)

    def each_tile(body, rest):
        tiles_of(scalars, slots, length, body, rest)

    for b in range(BLOCKS):

        def start_all(op):
            for copy in loads(b, op):
                copy.start()

        by_op(b, start_all)

    for key, piece in enumerate(pieces):
        origin = jnp.bitwise_xor(place, key) * span

        @pl.loop(0, slots)
        def _(slot):
            rows = pl.ds(pl.multiple_of(slot * length + origin, span), span)
            keep = live_of(scalars, slot, origin, span, width)
            value = jnp.where(keep, piece[slot].astype(wide), 0.0)
            x_now[rows, :] = value
            a_now[rows, :] = value.astype(low)

    def attention(b):
        w = weights.at[b]

        @pl.loop(0, 3)
        def _(j):
            pltpu.make_async_copy(proj_h.at[b, j], w.at[j], w_sem.at[b, j]).wait()

            def project(slot, start, rows):
                slope[rows, part(j)] = nn(a_now[rows, :], w[j]).astype(low)

            def clear(rows):
                slope[rows, part(j)] = jnp.zeros((TILE, width), low)

            each_tile(project, clear)
            pltpu.make_async_copy(slope.at[:, part(j)], saved[3].at[b, j], s_sem.at[b, j]).start()

        def clear_mix(rows):
            mix[rows, :] = jnp.zeros((TILE, width), low)

        each_tile(lambda slot, start, rows: None, clear_mix)

        def attend(slot, reach):
            base = pl.multiple_of(slot * length, length)
            key_at = lax.broadcasted_iota(jnp.int32, (1, reach), 1)
            bias = jnp.where(key_at < scalars[slot], 0.0, -1000000000.0).astype(wide)
            lane = lax.broadcasted_iota(jnp.int32, (TILE, 2 * HEAD), 1)

            @pl.loop(0, HEADS // 2, unroll=2)
            def _(pair):
                keys = slope[pl.ds(base, reach), heads(1, pair)]
                values = slope[pl.ds(base, reach), heads(2, pair)]
                for t in range(reach // TILE):
                    rows = pl.ds(pl.multiple_of(base + t * TILE, TILE), TILE)
                    scores = nt(pair_rows(slope[rows, heads(0, pair)] * FACTOR), keys) + bias
                    top = jnp.max(scores, axis=-1, keepdims=True)
                    exponent = jnp.exp(scores - top)
                    total = jnp.sum(exponent, axis=-1, keepdims=True)
                    mixed = nn(exponent.astype(low), values) * (1.0 / total)
                    stat = top + jnp.log(total)
                    kept = jnp.where(lane == pair * 2, stat[:TILE], stats[rows, :])
                    stats[rows, :] = jnp.where(lane == pair * 2 + 1, stat[TILE:], kept)
                    both = jnp.where(lane < HEAD, mixed[:TILE], mixed[TILE:])
                    mix[rows, heads(0, pair)] = both.astype(low)

        for_reach(scalars, slots, length, attend)
        saves(b, 0)[3].start()
        loads(b, 0)[3].wait()

        def out(slot, start, rows):
            update[rows, :] = nn(mix[rows, :], w[3])

        each_tile(out, None)

    def convolution(b):
        fill_padded(padded, a_now, slots, length)
        loads(b, 1)[0].wait()

        def run(slot, start, rows):
            near = window(padded, slot, start)
            running = jnp.zeros((TILE, width), wide)
            for offset in range(TAPS):
                at = PAD + offset - TAPS // 2
                tap = depth[offset, pl.ds(b, 1), :] * used_tap(scalars, slots, b, offset)
                running = running + near[at : at + TILE] * tap
            mix[rows, :] = running.astype(low)
            update[rows, :] = nn(running.astype(low), weights[b, 0])

        def clear(rows):
            mix[rows, :] = jnp.zeros((TILE, width), low)

        each_tile(run, clear)
        saves(b, 1)[0].start()

    def feed_forward(b):
        w = weights.at[b]
        mine = pl.ds(pl.multiple_of(place * share, 128), share)

        def run(slot, start, rows):
            opening = (start == 0) & (slot == 0)
            update[rows, :] = jnp.zeros((TILE, width), wide)

            @pl.loop(0, chunks)
            def _(j):
                @pl.when(opening)
                def _():
                    pltpu.make_async_copy(fin_h.at[b, :, part(j)], w.at[j], w_sem.at[b, j]).wait()
                    pltpu.make_async_copy(
                        fout_h.at[b, part(j)], w.at[chunks + j], w_sem.at[b, chunks + j]
                    ).wait()

                h = nn(a_now[rows, :], w[j])
                cdf = 0.5 * (1.0 + lax.erf(h * (0.5**0.5)))
                density = jnp.exp(-0.5 * h * h) * 0.3989422804014327
                value = (h * cdf).astype(low)
                active[:, part(j)] = value
                slope[rows, part(j)] = (cdf + h * density).astype(low)
                update[rows, :] += nn(value, w[chunks + j])

            mine_active[rows, :] = active[:, mine]

        def clear(rows):
            mine_active[rows, :] = jnp.zeros((TILE, share), low)

        each_tile(run, clear)
        for save in saves(b, 2):
            save.start()

    @pl.loop(0, BLOCKS)
    def _(b):
        common_saves(b)[0].start()

        @pl.when(b > 0)
        def _():
            def wait_saves(op):
                for save in saves(b - 1, op):
                    save.wait()

            by_op(b - 1, wait_saves)
            for save in common_saves(b - 1)[1:]:
                save.wait()

        for op, branch in enumerate((attention, convolution, feed_forward)):

            @pl.when(op_of(b) == op)
            def _():
                branch(b)

        common_saves(b)[0].wait()

        def norm(slot, start, rows):
            z = x_now[rows, :] + update[rows, :]
            center = z - jnp.mean(z, axis=-1, keepdims=True)
            scale = lax.rsqrt(jnp.mean(center * center, axis=-1, keepdims=True) + norm_eps)
            value = center * scale
            unit[rows, :] = value
            lane = lax.broadcasted_iota(jnp.int32, (TILE, 2 * HEAD), 1)
            stats[rows, :] = jnp.where(lane == HEADS, scale, stats[rows, :])
            keep = live_of(scalars, slot, start, TILE, width)
            value = jnp.where(keep, value * gain[pl.ds(b, 1), :] + shift[pl.ds(b, 1), :], 0.0)
            x_now[rows, :] = value
            a_now[rows, :] = value.astype(low)

        def clear(rows):
            x_now[rows, :] = jnp.zeros((TILE, width), wide)
            a_now[rows, :] = jnp.zeros((TILE, width), low)

        each_tile(norm, clear)
        for save in common_saves(b)[1:]:
            save.start()

    for slot in range(slots):
        rows = pl.ds(pl.multiple_of(slot * length + place * span, span), span)
        layer_out[slot] = x_now[rows, :]

    def wait_last(op):
        for save in saves(BLOCKS - 1, op):
            save.wait()

    by_op(BLOCKS - 1, wait_last)
    for save in common_saves(BLOCKS - 1)[1:]:
        save.wait()


def any_spec():
    return pl.BlockSpec(memory_space=pl.ANY)


def vmem_spec():
    return pl.BlockSpec(memory_space=pltpu.VMEM)


def forward_call(slots, length, peers, scalars, pieces, weights, depth, gain, shift):
    width = gain.shape[-1]
    hidden = weights[2].shape[2]
    rows = slots * length
    shapes = [((slots, length // peers, width), wide)]
    shapes += [
        ((BLOCKS, rows, width), low),
        ((BLOCKS, rows, width), wide),
        ((BLOCKS, rows, 2 * HEAD), wide),
        ((BLOCKS, 3, rows, width), low),
        ((BLOCKS, rows, width), low),
        ((BLOCKS, rows, hidden // peers), low),
        ((BLOCKS, rows, hidden), low),
    ]
    return pl.pallas_call(
        functools.partial(forward_kernel, slots, length, peers),
        out_shape=[jax.ShapeDtypeStruct(*s) for s in shapes],
        in_specs=[pl.BlockSpec(memory_space=pltpu.SMEM)]
        + [vmem_spec()] * len(pieces)
        + [any_spec()] * 5
        + [vmem_spec()] * 3,
        out_specs=[vmem_spec()] + [any_spec()] * (len(shapes) - 1),
        scratch_shapes=[
            pltpu.VMEM((rows, width), wide),
            pltpu.VMEM((rows, width), wide),
            pltpu.VMEM((rows, width), low),
            pltpu.VMEM((rows, width), wide),
            pltpu.VMEM((rows, 2 * HEAD), wide),
            pltpu.VMEM((BLOCKS, 8, width, width), low),
            pltpu.VMEM((rows, width), low),
            pltpu.VMEM((TILE, hidden), low),
            pltpu.VMEM((rows, hidden // peers), low),
            pltpu.VMEM((rows, hidden), low),
            pltpu.VMEM((slots, length + 2 * PAD, width), wide),
            pltpu.SemaphoreType.DMA((BLOCKS, 8)),
            pltpu.SemaphoreType.DMA((BLOCKS, 8)),
        ],
        compiler_params=pltpu.CompilerParams(vmem_limit_bytes=VMEM_LIMIT),
        name="forward_blocks",
    )(scalars, *pieces, *weights, depth, gain, shift)


def up16(count):
    return -(-count // 16) * 16


def payload_rows(width, groups):
    pitch = up16(width // groups)
    return pitch, 2 * pitch + EXTRA


def dense_rows(width, groups, peers):
    pitch = up16(width // groups)
    tail = up16(width // groups // peers)
    return pitch, 3 * pitch, 3 * pitch + tail, 3 * pitch + tail + EXTRA


def backward_kernel(b, slots, length, peers, groups, first, last, scalars, *refs):
    pieces = refs[: (peers if first else 1)]
    refs = refs[len(pieces) :]
    (a_h, unit_h, stats_h, qkv_h, mix_h, act_h, slope_h) = [ref.at[b] for ref in refs[:7]]
    (proj_h, out_h, fin_h, fout_h, point_h, depth, gain) = refs[7:14]
    g_out = refs[14]
    outputs = 1 if first else groups
    sent = refs[15 : 15 + outputs]
    (payload, gn, du, a_in, unit, stats, w_in, w_out, mix, act, slope, padded, stats_t, turned, small) = refs[
        15 + outputs : 30 + outputs
    ]
    (w_sem, s_sem, c_sem, p_sem) = refs[30 + outputs :]
    width = a_in.shape[1]
    hidden = w_in.shape[1]
    chunks = hidden // width
    tiles = length // TILE
    own = width // peers
    cols = width // groups
    hidden_cols = hidden // groups
    place = scalars[slots]
    me = scalars[slots + 1]
    op = scalars[slots + 2 + 2 * b]
    span = length // peers
    pitch, _ = payload_rows(width, groups)

    def key_of(d):
        return d if first else jnp.bitwise_xor(me, d)

    def part(j):
        return pl.ds(j * width, width)

    def heads(j, pair):
        return pl.ds(pl.multiple_of(j * width + pair * 2 * HEAD, 2 * HEAD), 2 * HEAD)

    def slot_copies(slot):
        rows = pl.ds(pl.multiple_of(slot * length, length), length)
        copies = [pltpu.make_async_copy(unit_h.at[rows], unit.at[rows], c_sem.at[2 * slot])]
        if not first:
            copies.append(
                pltpu.make_async_copy(pieces[0].at[rows], gn.at[rows], c_sem.at[2 * slot + 1])
            )
        return copies

    def stats_copy():
        return pltpu.make_async_copy(stats_h, stats, c_sem.at[2 * slots])

    def input_copy():
        return pltpu.make_async_copy(a_h, a_in, c_sem.at[2 * slots + 1])

    def attn_copies():
        return (
            [
                pltpu.make_async_copy(qkv_h.at[j], slope.at[:, part(j)], s_sem.at[j])
                for j in range(3)
            ]
            + [pltpu.make_async_copy(mix_h, mix, s_sem.at[3])]
            + [
                pltpu.make_async_copy(proj_h.at[b, j], w_out.at[part(j)], w_sem.at[j])
                for j in range(3)
            ]
            + [pltpu.make_async_copy(out_h.at[b], w_out.at[part(3)], w_sem.at[3])]
        )

    def conv_copies():
        return [
            pltpu.make_async_copy(mix_h, mix, s_sem.at[0]),
            pltpu.make_async_copy(point_h.at[b], w_out.at[part(0)], w_sem.at[0]),
        ]

    def ffn_copies():
        return [
            pltpu.make_async_copy(fout_h.at[b], w_out, w_sem.at[0]),
            pltpu.make_async_copy(slope_h, slope, s_sem.at[0]),
            pltpu.make_async_copy(fin_h.at[b], w_in, w_sem.at[1]),
            pltpu.make_async_copy(act_h, act, s_sem.at[1]),
        ]

    stats_copy().start()
    for slot in range(slots):
        for copy in slot_copies(slot):
            copy.start()
    for index, copies in enumerate((attn_copies, conv_copies, ffn_copies)):

        @pl.when(op == index)
        def _():
            for copy in copies():
                copy.start()

    input_copy().start()

    def each_tile(body, rest):
        tiles_of(scalars, slots, length, body, rest)

    small[...] = jnp.zeros(small.shape, wide)
    stats_copy().wait()

    @pl.loop(0, slots)
    def _(slot):
        for copy in slot_copies(slot):
            copy.wait()

        @pl.loop(0, peers)
        def _(j):
            start = pl.multiple_of(j * span, span)
            rows = pl.ds(pl.multiple_of(slot * length + start, span), span)

            @pl.when(start < scalars[slot])
            def _():
                if first:
                    for key in range(peers):

                        @pl.when(jnp.bitwise_xor(place, key) == j)
                        def _():
                            gn[rows, :] = pieces[key][slot].astype(wide)

                keep = live_of(scalars, slot, start, span, width)
                g = jnp.where(keep, gn[rows, :], 0.0)
                value = unit[rows, :]
                gu = g * value
                gy = g * gain[b : b + 1, :]
                one = jnp.mean(gy, axis=-1, keepdims=True)
                two = jnp.mean(gu * gain[b : b + 1, :], axis=-1, keepdims=True)
                dz = stats[rows, HEADS : HEADS + 1] * (gy - one - value * two)
                gn[rows, :] = dz
                du[rows, :] = dz.astype(low)
                small[TAPS : TAPS + 1, :] += jnp.sum(gu, axis=0, keepdims=True)
                small[TAPS + 1 : TAPS + 2, :] += jnp.sum(g, axis=0, keepdims=True)

            @pl.when(start >= scalars[slot])
            def _():
                gn[rows, :] = jnp.zeros((span, width), wide)
                du[rows, :] = jnp.zeros((span, width), low)

    small[TAPS + 2 : TAPS + 3, :] = jnp.full((1, width), op.astype(wide), wide)
    input_copy().wait()

    def turn_own(source):
        for s in range(peers):

            @pl.when(place == s)
            def _():
                turned[...] = source[:, s * own : (s + 1) * own].T

    def put_out(start, values):
        for d in range(groups):
            piece = values[d * cols : (d + 1) * cols].astype(low)
            payload[key_of(d), 0:cols, start : start + values.shape[1]] = piece

    def put_point(values):
        count = cols // peers
        for d in range(groups):
            for p in range(peers):
                piece = values[d * cols + p * count : d * cols + (p + 1) * count].astype(low)
                payload[key_of(d), 0:count, p * own : (p + 1) * own] = piece

    def put_in(d, values):
        for p in range(own // cols):
            at = slice(p * hidden_cols, (p + 1) * hidden_cols)
            payload[key_of(d), pitch : pitch + cols, at] = values[p * cols : (p + 1) * cols]

    def add_back(grad):
        if last:
            @pl.loop(0, slots)
            def _(slot):
                rows = pl.ds(pl.multiple_of(slot * length + place * span, span), span)
                keep = live_of(scalars, slot, place * span, span, width)

                @pl.when(place * span < scalars[slot])
                def _():
                    g_out[slot] = jnp.where(keep, gn[rows, :] + grad(rows), 0.0)

                @pl.when(place * span >= scalars[slot])
                def _():
                    g_out[slot] = jnp.zeros((span, width), wide)

        else:

            def add(slot, start, rows):
                g_out[rows, :] = gn[rows, :] + grad(rows)

            each_tile(add, None)

    @pl.when(op == 0)
    def _():
        copies = attn_copies()
        copies[7].wait()
        for copy in copies[:4]:
            copy.wait()
        turn_own(mix)
        put_out(3 * own, nn(turned[...], du[...]).T)

        def back(slot, start, rows):
            mix[rows, :] = nt(du[rows, :], w_out[part(3), :]).astype(low)

        def clear(rows):
            for j in range(3):
                slope[rows, part(j)] = jnp.zeros((TILE, width), low)

        each_tile(back, clear)

        @pl.loop(0, slots)
        def _(slot):
            stats_t[slot] = stats[pl.ds(pl.multiple_of(slot * length, length), length), :].T

        def attend(slot, reach):
            every = pl.ds(pl.multiple_of(slot * length, length), reach)
            upper = lax.broadcasted_iota(jnp.int32, (2 * HEAD, reach), 0) < HEAD

            @pl.loop(0, HEADS // 2)
            def _(pair):
                keys = slope[every, heads(1, pair)]
                values = slope[every, heads(2, pair)]
                queries = pair_rows(slope[every, heads(0, pair)] * FACTOR)
                grads = pair_rows(mix[every, heads(0, pair)])
                stat = jnp.concatenate(
                    [stats_t[slot, pl.ds(pair * 2 + head, 1), 0:reach] for head in range(2)], axis=1
                )
                soft = jnp.exp(jnp.minimum(nt(keys, queries) - stat, 0.0))
                product = soft * nt(values, grads)
                inner = jnp.sum(product, axis=0, keepdims=True)
                grad_scores = (product - soft * inner).astype(low)
                dq = tn(keys * FACTOR, grad_scores)
                dq = jnp.where(upper, dq[:, :reach], dq[:, reach:])
                slope[every, heads(0, pair)] = dq.T.astype(low)
                slope[every, heads(1, pair)] = nn(grad_scores, queries).astype(low)
                slope[every, heads(2, pair)] = nn(soft.astype(low), grads).astype(low)

        for_reach(scalars, slots, length, attend)
        for j in range(3):
            copies[4 + j].wait()
        turn_own(a_in)

        for j in range(3):
            put_out(j * own, nn(turned[...], slope[:, part(j)]).T)

        def grad(rows):
            total = nt(slope[rows, part(0)], w_out[part(0), :])
            for j in range(1, 3):
                total = total + nt(slope[rows, part(j)], w_out[part(j), :])
            return total

        add_back(grad)

    @pl.when(op == 1)
    def _():
        copies = conv_copies()
        for copy in copies:
            copy.wait()
        turn_own(mix)
        put_point(nn(turned[...], du[...]).T)

        def back(slot, start, rows):
            mix[rows, :] = nt(du[rows, :], w_out[part(0), :]).astype(low)

        def clear(rows):
            mix[rows, :] = jnp.zeros((TILE, width), low)

        each_tile(back, clear)
        fill_padded(padded, a_in, slots, length)

        def depth_terms(slot, start, rows):
            near = window(padded, slot, start)
            grads = mix[rows, :].astype(wide)
            for offset in range(TAPS):
                at = PAD + offset - TAPS // 2
                term = jnp.sum(near[at : at + TILE] * grads, axis=0, keepdims=True)
                small[offset : offset + 1, :] += term * used_tap(scalars, slots, b, offset)

        each_tile(depth_terms, None)
        fill_padded(padded, mix, slots, length)

        def spread(slot, start, rows):
            near = window(padded, slot, start)
            running = gn[rows, :]
            for offset in range(TAPS):
                at = PAD - offset + TAPS // 2
                tap = depth[offset, b : b + 1, :] * used_tap(scalars, slots, b, offset)
                running = running + near[at : at + TILE] * tap
            gn[rows, :] = running

        each_tile(spread, None)
        add_back(lambda rows: 0.0)

    @pl.when(op == 2)
    def _():
        copies = ffn_copies()
        copies[0].wait()
        copies[1].wait()

        def back(slot, start, rows):
            upstream = du[rows, :]
            for j in range(chunks):
                df = nt(upstream, w_out[part(j), :]).astype(low).astype(wide)
                slope[rows, part(j)] = (df * slope[rows, part(j)].astype(wide)).astype(low)

        def clear(rows):
            slope[rows, :] = jnp.zeros((TILE, hidden), low)

        each_tile(back, clear)
        copies[2].wait()
        copies[3].wait()
        put_out(0, nn(du[...].T, act[...]))
        turn_own(a_in)
        for d in range(groups):
            piece = slope[:, d * hidden_cols : (d + 1) * hidden_cols]
            put_in(d, nn(turned[...], piece).astype(low))
        add_back(lambda rows: nt(slope[rows, :], w_in[...]))

    for d in range(groups):
        payload[d, 2 * pitch : 2 * pitch + EXTRA, :] = small[...].astype(low)
    order = sorted(range(groups), key=lambda key: key < groups // 2)
    leaving = [
        pltpu.make_async_copy(
            payload.at[key], sent[0].at[key] if first else sent[key], p_sem.at[key]
        )
        for key in order
    ]
    for copy in leaving:
        copy.start()
    for copy in leaving:
        copy.wait()


def backward_call(b, slots, length, peers, groups, scalars, pieces, kept, weights, depth, gain):
    width = gain.shape[-1]
    hidden = weights[2].shape[2]
    rows = slots * length
    first = b == BLOCKS - 1
    last = b == 0
    _, count = payload_rows(width, groups)
    shapes = [
        ((slots, length // peers, width) if last else (rows, width), wide),
    ] + ([((groups, count, width), low)] if first else [((count, width), low)] * groups)
    return pl.pallas_call(
        functools.partial(backward_kernel, b, slots, length, peers, groups, first, last),
        out_shape=[jax.ShapeDtypeStruct(*s) for s in shapes],
        in_specs=[pl.BlockSpec(memory_space=pltpu.SMEM)]
        + [vmem_spec() if first else any_spec()] * len(pieces)
        + [any_spec()] * 12
        + [vmem_spec()] * 2,
        out_specs=[vmem_spec()] + [any_spec()] * (len(shapes) - 1),
        scratch_shapes=[
            pltpu.VMEM((groups, count, width), low),
            pltpu.VMEM((rows, width), wide),
            pltpu.VMEM((rows, width), low),
            pltpu.VMEM((rows, width), low),
            pltpu.VMEM((rows, width), wide),
            pltpu.VMEM((rows, 2 * HEAD), wide),
            pltpu.VMEM((width, hidden), low),
            pltpu.VMEM((hidden, width), low),
            pltpu.VMEM((rows, width), low),
            pltpu.VMEM((rows, hidden // peers), low),
            pltpu.VMEM((rows, hidden), low),
            pltpu.VMEM((slots, length + 2 * PAD, width), wide),
            pltpu.VMEM((slots, 2 * HEAD, length), wide),
            pltpu.VMEM((width // peers, rows), low),
            pltpu.VMEM((EXTRA, width), wide),
            pltpu.SemaphoreType.DMA((4,)),
            pltpu.SemaphoreType.DMA((4,)),
            pltpu.SemaphoreType.DMA((2 * slots + 2,)),
            pltpu.SemaphoreType.DMA((groups,)),
        ],
        compiler_params=pltpu.CompilerParams(vmem_limit_bytes=VMEM_LIMIT),
        name="backward_block",
    )(scalars, *pieces, *kept, *weights, depth, gain)


def add_pieces(pieces, small, groups, peers):
    width = small.shape[2]
    cols = width // groups
    pitch, _ = payload_rows(width, groups)
    sums = [None] * 4

    def add(index, value):
        sums[index] = value if sums[index] is None else sums[index] + value

    for at, piece in pieces:
        op = piece[2 * pitch : 2 * pitch + EXTRA, :].astype(wide)[TAPS + 2 : TAPS + 3, :]
        matrix = piece[0:cols, :].astype(wide)
        add(0, jnp.where(op == 0.0, matrix, 0.0))
        add(1, jnp.where(op == 2.0, matrix, 0.0))
        add(2, jnp.where(op == 2.0, piece[pitch : pitch + cols, :].astype(wide), 0.0))
        add(3, jnp.where(op == 1.0, piece[0 : cols // peers, :].astype(wide), 0.0))
        terms = piece[2 * pitch : 2 * pitch + EXTRA, :].astype(wide)
        row = lax.broadcasted_iota(jnp.int32, terms.shape, 0)
        terms = jnp.where((row < TAPS) & (op != 1.0), 0.0, terms)
        for index in range(3):
            terms = jnp.where(row == TAPS + 2 + index, (op == index).astype(wide), terms)
        terms = jnp.where(row < TAPS + 5, terms, 0.0)
        small[at] = terms
    total = small[0]
    for index in range(1, len(pieces)):
        total = total + small[index]
    return sums, total


def placed(pieces, me):
    return [(jnp.bitwise_xor(me, key) % len(pieces), piece) for key, piece in enumerate(pieces)]


def relay_kernel(groups, peers, slots, scalars, *refs):
    pieces, (dense, small) = refs[:-2], refs[-2:]
    width = dense.shape[1]
    cols = width // groups
    pitch, point_at, small_at, _ = dense_rows(width, groups, peers)
    sums, total = add_pieces(placed(pieces, scalars[slots + 1]), small, groups, peers)
    for index in range(3):
        dense[index * pitch : index * pitch + cols, :] = sums[index].astype(low)
    dense[point_at : point_at + cols // peers, :] = sums[3].astype(low)
    dense[small_at : small_at + EXTRA, :] = total.astype(low)


def relay_call(groups, peers, slots, scalars, pieces):
    width = pieces[0].shape[1]
    count = dense_rows(width, groups, peers)[3]
    return pl.pallas_call(
        functools.partial(relay_kernel, groups, peers, slots),
        out_shape=jax.ShapeDtypeStruct((count, width), low),
        in_specs=[pl.BlockSpec(memory_space=pltpu.SMEM)] + [vmem_spec()] * len(pieces),
        out_specs=vmem_spec(),
        scratch_shapes=[pltpu.VMEM((len(pieces), EXTRA, width), wide)],
        compiler_params=pltpu.CompilerParams(vmem_limit_bytes=VMEM_LIMIT),
        name="relay_sum",
    )(scalars, *pieces)


def final_kernel(groups, peers, slots, scalars, *refs):
    half = groups // 2
    near, dense, every = refs[:half], refs[half], refs[half + 1]
    (proj, out, f_in, f_out, point, depth, gain, shift, small) = refs[half + 2 :]
    width = dense.shape[1]
    cols = width // groups
    own = width // peers
    hidden_cols = f_in.shape[2]
    pitch, point_at, small_at, _ = dense_rows(width, groups, peers)
    for b in range(BLOCKS):
        if b:
            pieces = [(d, every.at[d]) for d in range(groups)]
        else:
            pieces = placed(near, scalars[slots + 1])
        sums, total = add_pieces(pieces, small, groups, peers)
        points = sums[3]
        if not b:
            total = total.astype(low).astype(wide)
            total = total + dense[small_at : small_at + EXTRA, :].astype(wide)
            for index in range(3):
                at = slice(index * pitch, index * pitch + cols)
                sums[index] = sums[index] + dense[at, :].astype(wide)
            points = points + dense[point_at : point_at + cols // peers, :].astype(wide)
        share = [1.0 / total[TAPS + 2 + op : TAPS + 3 + op, :] for op in range(3)]
        attn = sums[0] * share[0]
        for j in range(3):
            proj[b, j] = attn[:, j * own : (j + 1) * own].T
        out[b] = attn[:, 3 * own :].T
        f_out[b] = sums[1] * share[2]
        inner = sums[2] * share[2]
        for p in range(own // cols):
            f_in[b, p * cols : (p + 1) * cols, :] = inner[:, p * hidden_cols : (p + 1) * hidden_cols]
        points = points * share[1]
        points = jnp.concatenate([points[:, p * own : (p + 1) * own] for p in range(peers)], axis=0)
        point[b] = points.T
        depth[:, b, :] = total[0:TAPS] * share[1]
        gain[b : b + 1, :] = total[TAPS : TAPS + 1] * (1.0 / groups)
        shift[b : b + 1, :] = total[TAPS + 1 : TAPS + 2] * (1.0 / groups)


def final_call(groups, peers, slots, hidden, scalars, inputs):
    width = inputs[0].shape[-1]
    rows, cols = width // peers, width // groups
    shapes = [
        (BLOCKS, 3, rows, cols),
        (BLOCKS, rows, cols),
        (BLOCKS, rows, hidden // groups),
        (BLOCKS, cols, hidden // peers),
        (BLOCKS, rows, cols),
        (TAPS, BLOCKS, width),
        (BLOCKS, width),
        (BLOCKS, width),
    ]
    return pl.pallas_call(
        functools.partial(final_kernel, groups, peers, slots),
        out_shape=[jax.ShapeDtypeStruct(s, wide) for s in shapes],
        in_specs=[pl.BlockSpec(memory_space=pltpu.SMEM)] + [vmem_spec()] * len(inputs),
        out_specs=[vmem_spec()] * len(shapes),
        scratch_shapes=[pltpu.VMEM((groups, EXTRA, width), wide)],
        compiler_params=pltpu.CompilerParams(vmem_limit_bytes=VMEM_LIMIT),
        name="final_sum",
    )(scalars, *inputs)


def across(piece, axis, key):
    return lax.ppermute(piece, axis, [(i, i ^ key) for i in range(lax.axis_size(axis))])


def local(
    layer_in,
    lengths,
    op_ids,
    kernel_ids,
    attn_proj,
    attn_out,
    ffn_in,
    ffn_out,
    point_weights,
    depth_weights,
    norm_gains,
    norm_shifts,
    cotangent,
):
    slots, span, width = layer_in.shape
    peers = lax.axis_size("seq")
    groups = lax.axis_size("dp")
    place = lax.axis_index("seq").astype(jnp.int32)
    length = span * peers
    weights = (attn_proj, attn_out, ffn_in, ffn_out, point_weights)

    me = lax.axis_index("dp").astype(jnp.int32)
    half = groups // 2

    chosen = jnp.stack([op_ids[0], kernel_ids[0]], axis=1).reshape(-1)
    scalars = jnp.concatenate([lengths, jnp.stack([place, me]), chosen])
    depth_weights = jnp.swapaxes(depth_weights, 0, 1)

    later = cotangent.astype(low)
    parts = {0: layer_in.astype(low)}
    reach = peers // 2
    while reach:
        moved = {key ^ reach: across(part, "seq", reach) for key, part in parts.items()}
        if reach == peers // 2:
            moved, later, scalars = lax.optimization_barrier((moved, later, scalars))
        parts.update(moved)
        reach //= 2
    x_parts = [parts[key] for key in range(peers)]
    later, x_parts = lax.optimization_barrier((later, x_parts))
    cot_parts = [later] + [across(later, "seq", key) for key in range(1, peers)]
    layer_out, *saved = forward_call(
        slots, length, peers, scalars, x_parts, weights, depth_weights, norm_gains, norm_shifts
    )

    g, payload = backward_call(
        1, slots, length, peers, groups, scalars, cot_parts, saved, weights, depth_weights, norm_gains
    )
    every = lax.all_to_all(payload, "dp", 0, 0, tiled=True)
    g, *sent = backward_call(
        0, slots, length, peers, groups, scalars, [g], saved, weights, depth_weights, norm_gains
    )
    far = [sent[half]] + [across(sent[half + key], "dp", key) for key in range(1, half)]
    partial = relay_call(groups, peers, slots, scalars, far)
    rest, partial = lax.optimization_barrier((sent[:half], partial))
    dense = across(partial, "dp", half)
    near = [rest[0]] + [across(rest[key], "dp", key) for key in range(1, half)]
    proj, out, f_in, f_out, point, depth, gain, shift = final_call(
        groups, peers, slots, ffn_in.shape[2], scalars, near + [dense, every]
    )
    f_out = jnp.swapaxes(f_out, 1, 2)
    depth = jnp.swapaxes(depth, 0, 1)
    return (layer_out, g, proj, out, f_in, f_out, point, depth, gain, shift)


def solution(mesh):
    placed = (
        P("dp", "seq", None),
        P("dp"),
        P("dp", None),
        P("dp", None),
        P(),
        P(),
        P(),
        P(),
        P(),
        P(),
        P(),
        P(),
        P("dp", "seq", None),
    )
    return jax.shard_map(
        local,
        mesh=mesh,
        in_specs=placed,
        out_specs=(
            P("dp", "seq", None),
            P("dp", "seq", None),
            P(None, None, "seq", "dp"),
            P(None, "seq", "dp"),
            P(None, "seq", "dp"),
            P(None, "seq", "dp"),
            P(None, "seq", "dp"),
            P(),
            P(),
            P(),
        ),
        check_vma=False,
    )
```

```python
import functools

import jax
import jax.numpy as jnp
from jax import lax
from jax.experimental import pallas as pl
from jax.experimental.pallas import tpu as pltpu
from jax.sharding import PartitionSpec as P

HEADS = 12
HEAD = 64
TAPS = 7
BLOCKS = 2
EXTRA = 16
PAD = 8
norm_eps = 1e-05
low = jnp.bfloat16
wide = jnp.float32
VMEM_LIMIT = 60 * 1024 * 1024


def nn(left, right):
    return lax.dot_general(left, right, (((1,), (0,)), ((), ())), preferred_element_type=wide)


def nt(left, right):
    return lax.dot_general(left, right, (((1,), (1,)), ((), ())), preferred_element_type=wide)


def tn(left, right):
    return lax.dot_general(left, right, (((0,), (0,)), ((), ())), preferred_element_type=wide)


def live_of(scalars, slot, start, count, width):
    at = lax.broadcasted_iota(jnp.int32, (count, width), 0) + start
    return at < scalars[slot]


def used_tap(scalars, slots, b, offset):
    return (abs(offset - TAPS // 2) <= scalars[slots + 3 + 2 * b] + 1).astype(wide)


def live_tiles(scalars, slot, size):
    return (scalars[slot] + size - 1) // size


def for_reach(scalars, slots, length, body):
    @pl.loop(0, slots)
    def _(slot):
        @pl.when(scalars[slot] <= length // 2)
        def _():
            body(slot, length // 2)

        @pl.when(scalars[slot] > length // 2)
        def _():
            body(slot, length)


def tiles_of(scalars, slots, length, body, rest):
    @pl.loop(0, slots)
    def _(slot):
        count = live_tiles(scalars, slot, TILE)

        @pl.loop(0, count)
        def _(t):
            start = pl.multiple_of(t * TILE, TILE)
            body(slot, start, pl.ds(pl.multiple_of(slot * length + start, TILE), TILE))

        if rest is not None:

            @pl.loop(count, length // TILE)
            def _(t):
                rest(pl.ds(pl.multiple_of(slot * length + t * TILE, TILE), TILE))


def fill_padded(padded, source, slots, length):
    width = padded.shape[2]

    @pl.loop(0, slots)
    def _(slot):
        padded[slot, 0:PAD, :] = jnp.zeros((PAD, width), wide)
        padded[slot, PAD + length : PAD + length + PAD, :] = jnp.zeros((PAD, width), wide)

        @pl.loop(0, length // 128)
        def _(t):
            rows = pl.ds(pl.multiple_of(slot * length + t * 128, 128), 128)
            at = pl.ds(pl.multiple_of(PAD + t * 128, PAD), 128)
            padded[slot, at, :] = source[rows, :].astype(wide)


def window(padded, slot, start):
    return padded[slot, pl.ds(pl.multiple_of(start, TILE), TILE + 2 * PAD), :]


TILE = 256
FACTOR = HEAD**-0.5


def split_heads(tensor):
    lane = lax.broadcasted_iota(jnp.int32, tensor.shape, 1)
    none = jnp.zeros((), tensor.dtype)
    return [jnp.where(lane < HEAD, tensor, none), jnp.where(lane < HEAD, none, tensor)]


def pair_rows(tensor):
    return jnp.concatenate(split_heads(tensor), axis=0)


def forward_kernel(slots, length, peers, lengths_of, *refs):
    pieces = refs[:peers]
    (proj_h, out_h, fin_h, fout_h, point_h, depth, gain, shift) = refs[peers : peers + 8]
    refs = refs[peers + 8 :]
    layer_out = refs[0]
    saved = refs[1:8]
    (x_now, update, a_now, unit, stats, weights, mix, active, mine_active, slope, padded) = refs[8:19]
    w_sem, s_sem = refs[19:]
    scalars = lengths_of
    width = a_now.shape[1]
    hidden = slope.shape[1]
    share = mine_active.shape[1]
    span = length // peers
    chunks = hidden // width
    tiles = length // TILE
    place = scalars[slots]

    def part(j):
        return pl.ds(pl.multiple_of(j * width, width), width)

    def heads(j, pair):
        return pl.ds(pl.multiple_of(j * width + pair * 2 * HEAD, 2 * HEAD), 2 * HEAD)

    def op_of(b):
        return scalars[slots + 2 + 2 * b]

    def loads(b, op):
        w = weights.at[b]
        if op == 0:
            pairs = [(proj_h.at[b, j], j) for j in range(3)] + [(out_h.at[b], 3)]
        elif op == 1:
            pairs = [(point_h.at[b], 0)]
        else:
            pairs = [(fin_h.at[b, :, part(j)], j) for j in range(chunks)]
            pairs += [(fout_h.at[b, part(j)], chunks + j) for j in range(chunks)]
        return [pltpu.make_async_copy(source, w.at[j], w_sem.at[b, j]) for source, j in pairs]

    def saves(b, op):
        (a_h, unit_h, stats_h, qkv_h, mix_h, act_h, slope_h) = [ref.at[b] for ref in saved]
        if op == 0:
            pairs = [(slope.at[:, part(j)], qkv_h.at[j]) for j in range(3)] + [(mix, mix_h)]
        elif op == 1:
            pairs = [(mix, mix_h)]
        else:
            pairs = [(mine_active, act_h), (slope, slope_h)]
        return [
            pltpu.make_async_copy(source, target, s_sem.at[b, j])
            for j, (source, target) in enumerate(pairs)
        ]

    def common_saves(b):
        (a_h, unit_h, stats_h) = [ref.at[b] for ref in saved[:3]]
        pairs = [(a_now, a_h), (unit, unit_h), (stats, stats_h)]
        return [
            pltpu.make_async_copy(source, target, s_sem.at[b, 4 + j])
            for j, (source, target) in enumerate(pairs)
        ]

    def by_op(b, action):
        for op in range(3):

            @pl.when(op_of(b) == op)
            def _():
                action(op)

    def each_tile(body, rest):
        tiles_of(scalars, slots, length, body, rest)

    for b in range(BLOCKS):

        def start_all(op):
            for copy in loads(b, op):
                copy.start()

        by_op(b, start_all)

    for key, piece in enumerate(pieces):
        origin = jnp.bitwise_xor(place, key) * span

        @pl.loop(0, slots)
        def _(slot):
            rows = pl.ds(pl.multiple_of(slot * length + origin, span), span)
            keep = live_of(scalars, slot, origin, span, width)
            value = jnp.where(keep, piece[slot].astype(wide), 0.0)
            x_now[rows, :] = value
            a_now[rows, :] = value.astype(low)

    def attention(b):
        w = weights.at[b]

        @pl.loop(0, 3)
        def _(j):
            pltpu.make_async_copy(proj_h.at[b, j], w.at[j], w_sem.at[b, j]).wait()

            def project(slot, start, rows):
                slope[rows, part(j)] = nn(a_now[rows, :], w[j]).astype(low)

            def clear(rows):
                slope[rows, part(j)] = jnp.zeros((TILE, width), low)

            each_tile(project, clear)
            pltpu.make_async_copy(slope.at[:, part(j)], saved[3].at[b, j], s_sem.at[b, j]).start()

        def clear_mix(rows):
            mix[rows, :] = jnp.zeros((TILE, width), low)

        each_tile(lambda slot, start, rows: None, clear_mix)

        def attend(slot, reach):
            base = pl.multiple_of(slot * length, length)
            key_at = lax.broadcasted_iota(jnp.int32, (1, reach), 1)
            bias = jnp.where(key_at < scalars[slot], 0.0, -1000000000.0).astype(wide)
            lane = lax.broadcasted_iota(jnp.int32, (TILE, 2 * HEAD), 1)

            @pl.loop(0, HEADS // 2, unroll=3)
            def _(pair):
                keys = slope[pl.ds(base, reach), heads(1, pair)]
                values = slope[pl.ds(base, reach), heads(2, pair)]
                for t in range(reach // TILE):
                    rows = pl.ds(pl.multiple_of(base + t * TILE, TILE), TILE)
                    scores = nt(pair_rows(slope[rows, heads(0, pair)] * FACTOR), keys) + bias
                    top = jnp.max(scores, axis=-1, keepdims=True)
                    exponent = jnp.exp(scores - top)
                    total = jnp.sum(exponent, axis=-1, keepdims=True)
                    mixed = nn(exponent.astype(low), values) * (1.0 / total)
                    stat = top + jnp.log(total)
                    kept = jnp.where(lane == pair * 2, stat[:TILE], stats[rows, :])
                    stats[rows, :] = jnp.where(lane == pair * 2 + 1, stat[TILE:], kept)
                    both = jnp.where(lane < HEAD, mixed[:TILE], mixed[TILE:])
                    mix[rows, heads(0, pair)] = both.astype(low)

        for_reach(scalars, slots, length, attend)
        saves(b, 0)[3].start()
        loads(b, 0)[3].wait()

        def out(slot, start, rows):
            update[rows, :] = nn(mix[rows, :], w[3])

        each_tile(out, None)

    def convolution(b):
        fill_padded(padded, a_now, slots, length)
        loads(b, 1)[0].wait()

        def run(slot, start, rows):
            near = window(padded, slot, start)
            running = jnp.zeros((TILE, width), wide)
            for offset in range(TAPS):
                at = PAD + offset - TAPS // 2
                tap = depth[offset, pl.ds(b, 1), :] * used_tap(scalars, slots, b, offset)
                running = running + near[at : at + TILE] * tap
            mix[rows, :] = running.astype(low)
            update[rows, :] = nn(running.astype(low), weights[b, 0])

        def clear(rows):
            mix[rows, :] = jnp.zeros((TILE, width), low)

        each_tile(run, clear)
        saves(b, 1)[0].start()

    def feed_forward(b):
        w = weights.at[b]
        mine = pl.ds(pl.multiple_of(place * share, 128), share)

        for copy in loads(b, 2):
            copy.wait()

        def run(slot, start, rows):
            update[rows, :] = jnp.zeros((TILE, width), wide)

            @pl.loop(0, chunks, unroll=4)
            def _(j):
                h = nn(a_now[rows, :], w[j])
                cdf = 0.5 * (1.0 + lax.erf(h * (0.5**0.5)))
                density = jnp.exp(-0.5 * h * h) * 0.3989422804014327
                value = (h * cdf).astype(low)
                active[:, part(j)] = value
                slope[rows, part(j)] = (cdf + h * density).astype(low)
                update[rows, :] += nn(value, w[chunks + j])

            mine_active[rows, :] = active[:, mine]

        def clear(rows):
            mine_active[rows, :] = jnp.zeros((TILE, share), low)

        each_tile(run, clear)
        for save in saves(b, 2):
            save.start()

    @pl.loop(0, BLOCKS)
    def _(b):
        common_saves(b)[0].start()

        @pl.when(b > 0)
        def _():
            def wait_saves(op):
                for save in saves(b - 1, op):
                    save.wait()

            by_op(b - 1, wait_saves)
            for save in common_saves(b - 1)[1:]:
                save.wait()

        for op, branch in enumerate((attention, convolution, feed_forward)):

            @pl.when(op_of(b) == op)
            def _():
                branch(b)

        common_saves(b)[0].wait()

        def norm(slot, start, rows):
            z = x_now[rows, :] + update[rows, :]
            center = z - jnp.mean(z, axis=-1, keepdims=True)
            scale = lax.rsqrt(jnp.mean(center * center, axis=-1, keepdims=True) + norm_eps)
            value = center * scale
            unit[rows, :] = value
            lane = lax.broadcasted_iota(jnp.int32, (TILE, 2 * HEAD), 1)
            stats[rows, :] = jnp.where(lane == HEADS, scale, stats[rows, :])
            keep = live_of(scalars, slot, start, TILE, width)
            value = jnp.where(keep, value * gain[pl.ds(b, 1), :] + shift[pl.ds(b, 1), :], 0.0)
            x_now[rows, :] = value
            a_now[rows, :] = value.astype(low)

        def clear(rows):
            x_now[rows, :] = jnp.zeros((TILE, width), wide)
            a_now[rows, :] = jnp.zeros((TILE, width), low)

        each_tile(norm, clear)
        for save in common_saves(b)[1:]:
            save.start()

    for slot in range(slots):
        rows = pl.ds(pl.multiple_of(slot * length + place * span, span), span)
        layer_out[slot] = x_now[rows, :]

    def wait_last(op):
        for save in saves(BLOCKS - 1, op):
            save.wait()

    by_op(BLOCKS - 1, wait_last)
    for save in common_saves(BLOCKS - 1)[1:]:
        save.wait()


def any_spec():
    return pl.BlockSpec(memory_space=pl.ANY)


def vmem_spec():
    return pl.BlockSpec(memory_space=pltpu.VMEM)


def forward_call(slots, length, peers, scalars, pieces, weights, depth, gain, shift):
    width = gain.shape[-1]
    hidden = weights[2].shape[2]
    rows = slots * length
    shapes = [((slots, length // peers, width), wide)]
    shapes += [
        ((BLOCKS, rows, width), low),
        ((BLOCKS, rows, width), wide),
        ((BLOCKS, rows, 2 * HEAD), wide),
        ((BLOCKS, 3, rows, width), low),
        ((BLOCKS, rows, width), low),
        ((BLOCKS, rows, hidden // peers), low),
        ((BLOCKS, rows, hidden), low),
    ]
    return pl.pallas_call(
        functools.partial(forward_kernel, slots, length, peers),
        out_shape=[jax.ShapeDtypeStruct(*s) for s in shapes],
        in_specs=[pl.BlockSpec(memory_space=pltpu.SMEM)]
        + [vmem_spec()] * len(pieces)
        + [any_spec()] * 5
        + [vmem_spec()] * 3,
        out_specs=[vmem_spec()] + [any_spec()] * (len(shapes) - 1),
        scratch_shapes=[
            pltpu.VMEM((rows, width), wide),
            pltpu.VMEM((rows, width), wide),
            pltpu.VMEM((rows, width), low),
            pltpu.VMEM((rows, width), wide),
            pltpu.VMEM((rows, 2 * HEAD), wide),
            pltpu.VMEM((BLOCKS, 8, width, width), low),
            pltpu.VMEM((rows, width), low),
            pltpu.VMEM((TILE, hidden), low),
            pltpu.VMEM((rows, hidden // peers), low),
            pltpu.VMEM((rows, hidden), low),
            pltpu.VMEM((slots, length + 2 * PAD, width), wide),
            pltpu.SemaphoreType.DMA((BLOCKS, 8)),
            pltpu.SemaphoreType.DMA((BLOCKS, 8)),
        ],
        compiler_params=pltpu.CompilerParams(vmem_limit_bytes=VMEM_LIMIT),
        name="forward_blocks",
    )(scalars, *pieces, *weights, depth, gain, shift)


def up16(count):
    return -(-count // 16) * 16


def payload_rows(width, groups):
    pitch = up16(width // groups)
    return pitch, 2 * pitch + EXTRA


def dense_rows(width, groups, peers):
    pitch = up16(width // groups)
    tail = up16(width // groups // peers)
    return pitch, 3 * pitch, 3 * pitch + tail, 3 * pitch + tail + EXTRA


def backward_kernel(b, slots, length, peers, groups, first, last, scalars, *refs):
    pieces = refs[: (peers if first else 1)]
    refs = refs[len(pieces) :]
    (a_h, unit_h, stats_h, qkv_h, mix_h, act_h, slope_h) = [ref.at[b] for ref in refs[:7]]
    (proj_h, out_h, fin_h, fout_h, point_h, depth, gain) = refs[7:14]
    g_out = refs[14]
    outputs = 1 if first else groups
    sent = refs[15 : 15 + outputs]
    (payload, gn, du, a_in, unit, stats, w_in, w_out, mix, act, slope, padded, stats_t, turned, small) = refs[
        15 + outputs : 30 + outputs
    ]
    (w_sem, s_sem, c_sem, p_sem) = refs[30 + outputs :]
    width = a_in.shape[1]
    hidden = w_in.shape[1]
    chunks = hidden // width
    tiles = length // TILE
    own = width // peers
    cols = width // groups
    hidden_cols = hidden // groups
    place = scalars[slots]
    me = scalars[slots + 1]
    op = scalars[slots + 2 + 2 * b]
    span = length // peers
    pitch, _ = payload_rows(width, groups)

    def key_of(d):
        return d if first else jnp.bitwise_xor(me, d)

    def part(j):
        return pl.ds(j * width, width)

    def heads(j, pair):
        return pl.ds(pl.multiple_of(j * width + pair * 2 * HEAD, 2 * HEAD), 2 * HEAD)

    def slot_copies(slot):
        rows = pl.ds(pl.multiple_of(slot * length, length), length)
        copies = [pltpu.make_async_copy(unit_h.at[rows], unit.at[rows], c_sem.at[2 * slot])]
        if not first:
            copies.append(
                pltpu.make_async_copy(pieces[0].at[rows], gn.at[rows], c_sem.at[2 * slot + 1])
            )
        return copies

    def stats_copy():
        return pltpu.make_async_copy(stats_h, stats, c_sem.at[2 * slots])

    def input_copy():
        return pltpu.make_async_copy(a_h, a_in, c_sem.at[2 * slots + 1])

    def attn_copies():
        return (
            [
                pltpu.make_async_copy(qkv_h.at[j], slope.at[:, part(j)], s_sem.at[j])
                for j in range(3)
            ]
            + [pltpu.make_async_copy(mix_h, mix, s_sem.at[3])]
            + [
                pltpu.make_async_copy(proj_h.at[b, j], w_out.at[part(j)], w_sem.at[j])
                for j in range(3)
            ]
            + [pltpu.make_async_copy(out_h.at[b], w_out.at[part(3)], w_sem.at[3])]
        )

    def conv_copies():
        return [
            pltpu.make_async_copy(mix_h, mix, s_sem.at[0]),
            pltpu.make_async_copy(point_h.at[b], w_out.at[part(0)], w_sem.at[0]),
        ]

    def ffn_copies():
        return [
            pltpu.make_async_copy(fout_h.at[b], w_out, w_sem.at[0]),
            pltpu.make_async_copy(slope_h, slope, s_sem.at[0]),
            pltpu.make_async_copy(fin_h.at[b], w_in, w_sem.at[1]),
            pltpu.make_async_copy(act_h, act, s_sem.at[1]),
        ]

    stats_copy().start()
    for slot in range(slots):
        for copy in slot_copies(slot):
            copy.start()
    for index, copies in enumerate((attn_copies, conv_copies, ffn_copies)):

        @pl.when(op == index)
        def _():
            for copy in copies():
                copy.start()

    input_copy().start()

    def each_tile(body, rest):
        tiles_of(scalars, slots, length, body, rest)

    small[...] = jnp.zeros(small.shape, wide)
    stats_copy().wait()

    @pl.loop(0, slots)
    def _(slot):
        for copy in slot_copies(slot):
            copy.wait()

        @pl.loop(0, peers)
        def _(j):
            start = pl.multiple_of(j * span, span)
            rows = pl.ds(pl.multiple_of(slot * length + start, span), span)

            @pl.when(start < scalars[slot])
            def _():
                if first:
                    for key in range(peers):

                        @pl.when(jnp.bitwise_xor(place, key) == j)
                        def _():
                            gn[rows, :] = pieces[key][slot].astype(wide)

                keep = live_of(scalars, slot, start, span, width)
                g = jnp.where(keep, gn[rows, :], 0.0)
                value = unit[rows, :]
                gu = g * value
                gy = g * gain[b : b + 1, :]
                one = jnp.mean(gy, axis=-1, keepdims=True)
                two = jnp.mean(gu * gain[b : b + 1, :], axis=-1, keepdims=True)
                dz = stats[rows, HEADS : HEADS + 1] * (gy - one - value * two)
                gn[rows, :] = dz
                du[rows, :] = dz.astype(low)
                small[TAPS : TAPS + 1, :] += jnp.sum(gu, axis=0, keepdims=True)
                small[TAPS + 1 : TAPS + 2, :] += jnp.sum(g, axis=0, keepdims=True)

            @pl.when(start >= scalars[slot])
            def _():
                gn[rows, :] = jnp.zeros((span, width), wide)
                du[rows, :] = jnp.zeros((span, width), low)

    small[TAPS + 2 : TAPS + 3, :] = jnp.full((1, width), op.astype(wide), wide)
    input_copy().wait()

    def turn_own(source):
        for s in range(peers):

            @pl.when(place == s)
            def _():
                turned[...] = source[:, s * own : (s + 1) * own].T

    def put_out(start, values):
        for d in range(groups):
            piece = values[d * cols : (d + 1) * cols].astype(low)
            payload[key_of(d), 0:cols, start : start + values.shape[1]] = piece

    def put_point(values):
        count = cols // peers
        for d in range(groups):
            for p in range(peers):
                piece = values[d * cols + p * count : d * cols + (p + 1) * count].astype(low)
                payload[key_of(d), 0:count, p * own : (p + 1) * own] = piece

    def put_in(d, values):
        for p in range(own // cols):
            at = slice(p * hidden_cols, (p + 1) * hidden_cols)
            payload[key_of(d), pitch : pitch + cols, at] = values[p * cols : (p + 1) * cols]

    def add_back(grad):
        if last:
            @pl.loop(0, slots)
            def _(slot):
                rows = pl.ds(pl.multiple_of(slot * length + place * span, span), span)
                keep = live_of(scalars, slot, place * span, span, width)

                @pl.when(place * span < scalars[slot])
                def _():
                    g_out[slot] = jnp.where(keep, gn[rows, :] + grad(rows), 0.0)

                @pl.when(place * span >= scalars[slot])
                def _():
                    g_out[slot] = jnp.zeros((span, width), wide)

        else:

            def add(slot, start, rows):
                g_out[rows, :] = gn[rows, :] + grad(rows)

            each_tile(add, None)

    @pl.when(op == 0)
    def _():
        copies = attn_copies()
        copies[7].wait()
        for copy in copies[:4]:
            copy.wait()
        turn_own(mix)
        put_out(3 * own, nn(turned[...], du[...]).T)

        def back(slot, start, rows):
            mix[rows, :] = nt(du[rows, :], w_out[part(3), :]).astype(low)

        def clear(rows):
            for j in range(3):
                slope[rows, part(j)] = jnp.zeros((TILE, width), low)

        each_tile(back, clear)

        @pl.loop(0, slots)
        def _(slot):
            stats_t[slot] = stats[pl.ds(pl.multiple_of(slot * length, length), length), :].T

        def attend(slot, reach):
            every = pl.ds(pl.multiple_of(slot * length, length), reach)
            upper = lax.broadcasted_iota(jnp.int32, (2 * HEAD, reach), 0) < HEAD

            @pl.loop(0, HEADS // 2)
            def _(pair):
                keys = slope[every, heads(1, pair)]
                values = slope[every, heads(2, pair)]
                scaled = keys * FACTOR
                queries = split_heads(slope[every, heads(0, pair)] * FACTOR)
                grads = split_heads(mix[every, heads(0, pair)])
                scores = [nt(keys, one) for one in queries]
                products = [nt(values, one) for one in grads]
                dk = jnp.zeros((reach, 2 * HEAD), wide)
                dv = jnp.zeros((reach, 2 * HEAD), wide)
                dq = []
                for head in range(2):
                    stat = stats_t[slot, pl.ds(pair * 2 + head, 1), 0:reach]
                    soft = jnp.exp(jnp.minimum(scores[head] - stat, 0.0))
                    product = soft * products[head]
                    inner = jnp.sum(product, axis=0, keepdims=True)
                    grad_scores = (product - soft * inner).astype(low)
                    dq.append(tn(scaled, grad_scores))
                    dk = dk + nn(grad_scores, queries[head])
                    dv = dv + nn(soft.astype(low), grads[head])
                dq = jnp.where(upper, dq[0], dq[1])
                slope[every, heads(0, pair)] = dq.T.astype(low)
                slope[every, heads(1, pair)] = dk.astype(low)
                slope[every, heads(2, pair)] = dv.astype(low)

        for_reach(scalars, slots, length, attend)
        for j in range(3):
            copies[4 + j].wait()
        turn_own(a_in)

        for j in range(3):
            put_out(j * own, nn(turned[...], slope[:, part(j)]).T)

        def grad(rows):
            total = nt(slope[rows, part(0)], w_out[part(0), :])
            for j in range(1, 3):
                total = total + nt(slope[rows, part(j)], w_out[part(j), :])
            return total

        add_back(grad)

    @pl.when(op == 1)
    def _():
        copies = conv_copies()
        for copy in copies:
            copy.wait()
        turn_own(mix)
        put_point(nn(turned[...], du[...]).T)

        def back(slot, start, rows):
            mix[rows, :] = nt(du[rows, :], w_out[part(0), :]).astype(low)

        def clear(rows):
            mix[rows, :] = jnp.zeros((TILE, width), low)

        each_tile(back, clear)
        fill_padded(padded, a_in, slots, length)

        def depth_terms(slot, start, rows):
            near = window(padded, slot, start)
            grads = mix[rows, :].astype(wide)
            for offset in range(TAPS):
                at = PAD + offset - TAPS // 2
                term = jnp.sum(near[at : at + TILE] * grads, axis=0, keepdims=True)
                small[offset : offset + 1, :] += term * used_tap(scalars, slots, b, offset)

        each_tile(depth_terms, None)
        fill_padded(padded, mix, slots, length)

        def spread(slot, start, rows):
            near = window(padded, slot, start)
            running = gn[rows, :]
            for offset in range(TAPS):
                at = PAD - offset + TAPS // 2
                tap = depth[offset, b : b + 1, :] * used_tap(scalars, slots, b, offset)
                running = running + near[at : at + TILE] * tap
            gn[rows, :] = running

        each_tile(spread, None)
        add_back(lambda rows: 0.0)

    @pl.when(op == 2)
    def _():
        copies = ffn_copies()
        copies[0].wait()
        copies[1].wait()

        def back(slot, start, rows):
            upstream = du[rows, :]
            for j in range(chunks):
                df = nt(upstream, w_out[part(j), :]).astype(low).astype(wide)
                slope[rows, part(j)] = (df * slope[rows, part(j)].astype(wide)).astype(low)

        def clear(rows):
            slope[rows, :] = jnp.zeros((TILE, hidden), low)

        each_tile(back, clear)
        copies[2].wait()
        copies[3].wait()
        put_out(0, nn(du[...].T, act[...]))
        turn_own(a_in)
        for d in range(groups):
            piece = slope[:, d * hidden_cols : (d + 1) * hidden_cols]
            put_in(d, nn(turned[...], piece).astype(low))
        add_back(lambda rows: nt(slope[rows, :], w_in[...]))

    for d in range(groups):
        payload[d, 2 * pitch : 2 * pitch + EXTRA, :] = small[...].astype(low)
    order = sorted(range(groups), key=lambda key: key < groups // 2)
    leaving = [
        pltpu.make_async_copy(
            payload.at[key], sent[0].at[key] if first else sent[key], p_sem.at[key]
        )
        for key in order
    ]
    for copy in leaving:
        copy.start()
    for copy in leaving:
        copy.wait()


def backward_call(b, slots, length, peers, groups, scalars, pieces, kept, weights, depth, gain):
    width = gain.shape[-1]
    hidden = weights[2].shape[2]
    rows = slots * length
    first = b == BLOCKS - 1
    last = b == 0
    _, count = payload_rows(width, groups)
    shapes = [
        ((slots, length // peers, width) if last else (rows, width), wide),
    ] + ([((groups, count, width), low)] if first else [((count, width), low)] * groups)
    return pl.pallas_call(
        functools.partial(backward_kernel, b, slots, length, peers, groups, first, last),
        out_shape=[jax.ShapeDtypeStruct(*s) for s in shapes],
        in_specs=[pl.BlockSpec(memory_space=pltpu.SMEM)]
        + [vmem_spec() if first else any_spec()] * len(pieces)
        + [any_spec()] * 12
        + [vmem_spec()] * 2,
        out_specs=[vmem_spec()] + [any_spec()] * (len(shapes) - 1),
        scratch_shapes=[
            pltpu.VMEM((groups, count, width), low),
            pltpu.VMEM((rows, width), wide),
            pltpu.VMEM((rows, width), low),
            pltpu.VMEM((rows, width), low),
            pltpu.VMEM((rows, width), wide),
            pltpu.VMEM((rows, 2 * HEAD), wide),
            pltpu.VMEM((width, hidden), low),
            pltpu.VMEM((hidden, width), low),
            pltpu.VMEM((rows, width), low),
            pltpu.VMEM((rows, hidden // peers), low),
            pltpu.VMEM((rows, hidden), low),
            pltpu.VMEM((slots, length + 2 * PAD, width), wide),
            pltpu.VMEM((slots, 2 * HEAD, length), wide),
            pltpu.VMEM((width // peers, rows), low),
            pltpu.VMEM((EXTRA, width), wide),
            pltpu.SemaphoreType.DMA((4,)),
            pltpu.SemaphoreType.DMA((4,)),
            pltpu.SemaphoreType.DMA((2 * slots + 2,)),
            pltpu.SemaphoreType.DMA((groups,)),
        ],
        compiler_params=pltpu.CompilerParams(vmem_limit_bytes=VMEM_LIMIT),
        name="backward_block",
    )(scalars, *pieces, *kept, *weights, depth, gain)


def add_pieces(pieces, small, groups, peers):
    width = small.shape[2]
    cols = width // groups
    pitch, _ = payload_rows(width, groups)
    sums = [None] * 4

    def add(index, value):
        sums[index] = value if sums[index] is None else sums[index] + value

    for at, piece in pieces:
        op = piece[2 * pitch : 2 * pitch + EXTRA, :].astype(wide)[TAPS + 2 : TAPS + 3, :]
        matrix = piece[0:cols, :].astype(wide)
        add(0, jnp.where(op == 0.0, matrix, 0.0))
        add(1, jnp.where(op == 2.0, matrix, 0.0))
        add(2, jnp.where(op == 2.0, piece[pitch : pitch + cols, :].astype(wide), 0.0))
        add(3, jnp.where(op == 1.0, piece[0 : cols // peers, :].astype(wide), 0.0))
        terms = piece[2 * pitch : 2 * pitch + EXTRA, :].astype(wide)
        row = lax.broadcasted_iota(jnp.int32, terms.shape, 0)
        terms = jnp.where((row < TAPS) & (op != 1.0), 0.0, terms)
        for index in range(3):
            terms = jnp.where(row == TAPS + 2 + index, (op == index).astype(wide), terms)
        terms = jnp.where(row < TAPS + 5, terms, 0.0)
        small[at] = terms
    total = small[0]
    for index in range(1, len(pieces)):
        total = total + small[index]
    return sums, total


def placed(pieces, me):
    return [(jnp.bitwise_xor(me, key) % len(pieces), piece) for key, piece in enumerate(pieces)]


def relay_kernel(groups, peers, slots, scalars, *refs):
    pieces, (dense, small) = refs[:-2], refs[-2:]
    width = dense.shape[1]
    cols = width // groups
    pitch, point_at, small_at, _ = dense_rows(width, groups, peers)
    sums, total = add_pieces(placed(pieces, scalars[slots + 1]), small, groups, peers)
    for index in range(3):
        dense[index * pitch : index * pitch + cols, :] = sums[index].astype(low)
    dense[point_at : point_at + cols // peers, :] = sums[3].astype(low)
    dense[small_at : small_at + EXTRA, :] = total.astype(low)


def relay_call(groups, peers, slots, scalars, pieces):
    width = pieces[0].shape[1]
    count = dense_rows(width, groups, peers)[3]
    return pl.pallas_call(
        functools.partial(relay_kernel, groups, peers, slots),
        out_shape=jax.ShapeDtypeStruct((count, width), low),
        in_specs=[pl.BlockSpec(memory_space=pltpu.SMEM)] + [vmem_spec()] * len(pieces),
        out_specs=vmem_spec(),
        scratch_shapes=[pltpu.VMEM((len(pieces), EXTRA, width), wide)],
        compiler_params=pltpu.CompilerParams(vmem_limit_bytes=VMEM_LIMIT),
        name="relay_sum",
    )(scalars, *pieces)


def final_kernel(groups, peers, slots, scalars, *refs):
    half = groups // 2
    near, dense, every = refs[:half], refs[half], refs[half + 1]
    (proj, out, f_in, f_out, point, depth, gain, shift, small) = refs[half + 2 :]
    width = dense.shape[1]
    cols = width // groups
    own = width // peers
    hidden_cols = f_in.shape[2]
    pitch, point_at, small_at, _ = dense_rows(width, groups, peers)
    for b in range(BLOCKS):
        if b:
            pieces = [(d, every.at[d]) for d in range(groups)]
        else:
            pieces = placed(near, scalars[slots + 1])
        sums, total = add_pieces(pieces, small, groups, peers)
        points = sums[3]
        if not b:
            total = total.astype(low).astype(wide)
            total = total + dense[small_at : small_at + EXTRA, :].astype(wide)
            for index in range(3):
                at = slice(index * pitch, index * pitch + cols)
                sums[index] = sums[index] + dense[at, :].astype(wide)
            points = points + dense[point_at : point_at + cols // peers, :].astype(wide)
        share = [1.0 / total[TAPS + 2 + op : TAPS + 3 + op, :] for op in range(3)]
        attn = sums[0] * share[0]
        for j in range(3):
            proj[b, j] = attn[:, j * own : (j + 1) * own].T
        out[b] = attn[:, 3 * own :].T
        f_out[b] = sums[1] * share[2]
        inner = sums[2] * share[2]
        for p in range(own // cols):
            f_in[b, p * cols : (p + 1) * cols, :] = inner[:, p * hidden_cols : (p + 1) * hidden_cols]
        points = points * share[1]
        points = jnp.concatenate([points[:, p * own : (p + 1) * own] for p in range(peers)], axis=0)
        point[b] = points.T
        depth[:, b, :] = total[0:TAPS] * share[1]
        gain[b : b + 1, :] = total[TAPS : TAPS + 1] * (1.0 / groups)
        shift[b : b + 1, :] = total[TAPS + 1 : TAPS + 2] * (1.0 / groups)


def final_call(groups, peers, slots, hidden, scalars, inputs):
    width = inputs[0].shape[-1]
    rows, cols = width // peers, width // groups
    shapes = [
        (BLOCKS, 3, rows, cols),
        (BLOCKS, rows, cols),
        (BLOCKS, rows, hidden // groups),
        (BLOCKS, cols, hidden // peers),
        (BLOCKS, rows, cols),
        (TAPS, BLOCKS, width),
        (BLOCKS, width),
        (BLOCKS, width),
    ]
    return pl.pallas_call(
        functools.partial(final_kernel, groups, peers, slots),
        out_shape=[jax.ShapeDtypeStruct(s, wide) for s in shapes],
        in_specs=[pl.BlockSpec(memory_space=pltpu.SMEM)] + [vmem_spec()] * len(inputs),
        out_specs=[vmem_spec()] * len(shapes),
        scratch_shapes=[pltpu.VMEM((groups, EXTRA, width), wide)],
        compiler_params=pltpu.CompilerParams(vmem_limit_bytes=VMEM_LIMIT),
        name="final_sum",
    )(scalars, *inputs)


def across(piece, axis, key):
    return lax.ppermute(piece, axis, [(i, i ^ key) for i in range(lax.axis_size(axis))])


def local(
    layer_in,
    lengths,
    op_ids,
    kernel_ids,
    attn_proj,
    attn_out,
    ffn_in,
    ffn_out,
    point_weights,
    depth_weights,
    norm_gains,
    norm_shifts,
    cotangent,
):
    slots, span, width = layer_in.shape
    peers = lax.axis_size("seq")
    groups = lax.axis_size("dp")
    place = lax.axis_index("seq").astype(jnp.int32)
    length = span * peers
    weights = (attn_proj, attn_out, ffn_in, ffn_out, point_weights)

    me = lax.axis_index("dp").astype(jnp.int32)
    half = groups // 2

    chosen = jnp.stack([op_ids[0], kernel_ids[0]], axis=1).reshape(-1)
    scalars = jnp.concatenate([lengths, jnp.stack([place, me]), chosen])
    depth_weights = jnp.swapaxes(depth_weights, 0, 1)

    later = cotangent.astype(low)
    parts = {0: layer_in.astype(low)}
    reach = peers // 2
    while reach:
        moved = {key ^ reach: across(part, "seq", reach) for key, part in parts.items()}
        if reach == peers // 2:
            moved, later, scalars = lax.optimization_barrier((moved, later, scalars))
        parts.update(moved)
        reach //= 2
    x_parts = [parts[key] for key in range(peers)]
    later, x_parts = lax.optimization_barrier((later, x_parts))
    cot_parts = [later] + [across(later, "seq", key) for key in range(1, peers)]
    layer_out, *saved = forward_call(
        slots, length, peers, scalars, x_parts, weights, depth_weights, norm_gains, norm_shifts
    )

    g, payload = backward_call(
        1, slots, length, peers, groups, scalars, cot_parts, saved, weights, depth_weights, norm_gains
    )
    every = lax.all_to_all(payload, "dp", 0, 0, tiled=True)
    g, *sent = backward_call(
        0, slots, length, peers, groups, scalars, [g], saved, weights, depth_weights, norm_gains
    )
    far = [sent[half]] + [across(sent[half + key], "dp", key) for key in range(1, half)]
    partial = relay_call(groups, peers, slots, scalars, far)
    rest, partial = lax.optimization_barrier((sent[:half], partial))
    dense = across(partial, "dp", half)
    near = [rest[0]] + [across(rest[key], "dp", key) for key in range(1, half)]
    proj, out, f_in, f_out, point, depth, gain, shift = final_call(
        groups, peers, slots, ffn_in.shape[2], scalars, near + [dense, every]
    )
    f_out = jnp.swapaxes(f_out, 1, 2)
    depth = jnp.swapaxes(depth, 0, 1)
    return (layer_out, g, proj, out, f_in, f_out, point, depth, gain, shift)


def solution(mesh):
    placed = (
        P("dp", "seq", None),
        P("dp"),
        P("dp", None),
        P("dp", None),
        P(),
        P(),
        P(),
        P(),
        P(),
        P(),
        P(),
        P(),
        P("dp", "seq", None),
    )
    return jax.shard_map(
        local,
        mesh=mesh,
        in_specs=placed,
        out_specs=(
            P("dp", "seq", None),
            P("dp", "seq", None),
            P(None, None, "seq", "dp"),
            P(None, "seq", "dp"),
            P(None, "seq", "dp"),
            P(None, "seq", "dp"),
            P(None, "seq", "dp"),
            P(),
            P(),
            P(),
        ),
        check_vma=False,
    )
```

```python
import functools

import jax
import jax.numpy as jnp
from jax import lax
from jax.experimental import pallas as pl
from jax.experimental.pallas import tpu as pltpu
from jax.sharding import PartitionSpec as P

HEADS = 12
HEAD = 64
TAPS = 7
BLOCKS = 2
EXTRA = 16
PAD = 8
norm_eps = 1e-05
low = jnp.bfloat16
wide = jnp.float32
VMEM_LIMIT = 60 * 1024 * 1024


def nn(left, right):
    return lax.dot_general(left, right, (((1,), (0,)), ((), ())), preferred_element_type=wide)


def nt(left, right):
    return lax.dot_general(left, right, (((1,), (1,)), ((), ())), preferred_element_type=wide)


def tn(left, right):
    return lax.dot_general(left, right, (((0,), (0,)), ((), ())), preferred_element_type=wide)


def live_of(scalars, slot, start, count, width):
    at = lax.broadcasted_iota(jnp.int32, (count, width), 0) + start
    return at < scalars[slot]


def used_tap(scalars, slots, b, offset):
    return (abs(offset - TAPS // 2) <= scalars[slots + 3 + 2 * b] + 1).astype(wide)


def live_tiles(scalars, slot, size):
    return (scalars[slot] + size - 1) // size


def for_reach(scalars, slots, length, body):
    @pl.loop(0, slots)
    def _(slot):
        @pl.when(scalars[slot] <= length // 2)
        def _():
            body(slot, length // 2)

        @pl.when(scalars[slot] > length // 2)
        def _():
            body(slot, length)


def tiles_of(scalars, slots, length, body, rest):
    @pl.loop(0, slots)
    def _(slot):
        count = live_tiles(scalars, slot, TILE)

        @pl.loop(0, count)
        def _(t):
            start = pl.multiple_of(t * TILE, TILE)
            body(slot, start, pl.ds(pl.multiple_of(slot * length + start, TILE), TILE))

        if rest is not None:

            @pl.loop(count, length // TILE)
            def _(t):
                rest(pl.ds(pl.multiple_of(slot * length + t * TILE, TILE), TILE))


def fill_padded(padded, source, slots, length):
    width = padded.shape[2]

    @pl.loop(0, slots)
    def _(slot):
        padded[slot, 0:PAD, :] = jnp.zeros((PAD, width), wide)
        padded[slot, PAD + length : PAD + length + PAD, :] = jnp.zeros((PAD, width), wide)

        @pl.loop(0, length // 128)
        def _(t):
            rows = pl.ds(pl.multiple_of(slot * length + t * 128, 128), 128)
            at = pl.ds(pl.multiple_of(PAD + t * 128, PAD), 128)
            padded[slot, at, :] = source[rows, :].astype(wide)


def window(padded, slot, start):
    return padded[slot, pl.ds(pl.multiple_of(start, TILE), TILE + 2 * PAD), :]


TILE = 256
FACTOR = HEAD**-0.5


def split_heads(tensor):
    lane = lax.broadcasted_iota(jnp.int32, tensor.shape, 1)
    none = jnp.zeros((), tensor.dtype)
    return [jnp.where(lane < HEAD, tensor, none), jnp.where(lane < HEAD, none, tensor)]


def pair_rows(tensor):
    return jnp.concatenate(split_heads(tensor), axis=0)


def forward_kernel(slots, length, peers, lengths_of, *refs):
    pieces = refs[:peers]
    (proj_h, out_h, fin_h, fout_h, point_h, depth, gain, shift) = refs[peers : peers + 8]
    refs = refs[peers + 8 :]
    layer_out = refs[0]
    saved = refs[1:8]
    (x_now, update, a_now, unit, stats, weights, mix, active, mine_active, slope, padded) = refs[8:19]
    w_sem, s_sem = refs[19:]
    scalars = lengths_of
    width = a_now.shape[1]
    hidden = slope.shape[1]
    share = mine_active.shape[1]
    span = length // peers
    chunks = hidden // width
    tiles = length // TILE
    place = scalars[slots]

    def part(j):
        return pl.ds(pl.multiple_of(j * width, width), width)

    def heads(j, pair):
        return pl.ds(pl.multiple_of(j * width + pair * 2 * HEAD, 2 * HEAD), 2 * HEAD)

    def op_of(b):
        return scalars[slots + 2 + 2 * b]

    def loads(b, op):
        w = weights.at[b]
        if op == 0:
            pairs = [(proj_h.at[b, j], j) for j in range(3)] + [(out_h.at[b], 3)]
        elif op == 1:
            pairs = [(point_h.at[b], 0)]
        else:
            pairs = [(fin_h.at[b, :, part(j)], j) for j in range(chunks)]
            pairs += [(fout_h.at[b, part(j)], chunks + j) for j in range(chunks)]
        return [pltpu.make_async_copy(source, w.at[j], w_sem.at[b, j]) for source, j in pairs]

    def saves(b, op):
        (a_h, unit_h, stats_h, qkv_h, mix_h, act_h, slope_h) = [ref.at[b] for ref in saved]
        if op == 0:
            pairs = [(slope.at[:, part(j)], qkv_h.at[j]) for j in range(3)] + [(mix, mix_h)]
        elif op == 1:
            pairs = [(mix, mix_h)]
        else:
            pairs = [(mine_active, act_h), (slope, slope_h)]
        return [
            pltpu.make_async_copy(source, target, s_sem.at[b, j])
            for j, (source, target) in enumerate(pairs)
        ]

    def common_saves(b):
        (a_h, unit_h, stats_h) = [ref.at[b] for ref in saved[:3]]
        pairs = [(a_now, a_h), (unit, unit_h), (stats, stats_h)]
        return [
            pltpu.make_async_copy(source, target, s_sem.at[b, 4 + j])
            for j, (source, target) in enumerate(pairs)
        ]

    def by_op(b, action):
        for op in range(3):

            @pl.when(op_of(b) == op)
            def _():
                action(op)

    def each_tile(body, rest):
        tiles_of(scalars, slots, length, body, rest)

    for b in range(BLOCKS):

        def start_all(op):
            for copy in loads(b, op):
                copy.start()

        by_op(b, start_all)

    for key, piece in enumerate(pieces):
        origin = jnp.bitwise_xor(place, key) * span

        @pl.loop(0, slots)
        def _(slot):
            rows = pl.ds(pl.multiple_of(slot * length + origin, span), span)
            keep = live_of(scalars, slot, origin, span, width)
            value = jnp.where(keep, piece[slot].astype(wide), 0.0)
            x_now[rows, :] = value
            a_now[rows, :] = value.astype(low)

    def attention(b):
        w = weights.at[b]

        @pl.loop(0, 3)
        def _(j):
            pltpu.make_async_copy(proj_h.at[b, j], w.at[j], w_sem.at[b, j]).wait()

            def project(slot, start, rows):
                slope[rows, part(j)] = nn(a_now[rows, :], w[j]).astype(low)

            def clear(rows):
                slope[rows, part(j)] = jnp.zeros((TILE, width), low)

            each_tile(project, clear)
            pltpu.make_async_copy(slope.at[:, part(j)], saved[3].at[b, j], s_sem.at[b, j]).start()

        def clear_mix(rows):
            mix[rows, :] = jnp.zeros((TILE, width), low)

        each_tile(lambda slot, start, rows: None, clear_mix)

        def attend(slot, reach):
            base = pl.multiple_of(slot * length, length)
            key_at = lax.broadcasted_iota(jnp.int32, (1, reach), 1)
            bias = jnp.where(key_at < scalars[slot], 0.0, -1000000000.0).astype(wide)
            lane = lax.broadcasted_iota(jnp.int32, (TILE, 2 * HEAD), 1)

            @pl.loop(0, HEADS // 2, unroll=3)
            def _(pair):
                keys = slope[pl.ds(base, reach), heads(1, pair)]
                values = slope[pl.ds(base, reach), heads(2, pair)]
                for t in range(reach // TILE):
                    rows = pl.ds(pl.multiple_of(base + t * TILE, TILE), TILE)
                    scores = nt(pair_rows(slope[rows, heads(0, pair)] * FACTOR), keys) + bias
                    top = jnp.max(scores, axis=-1, keepdims=True)
                    exponent = jnp.exp(scores - top)
                    total = jnp.sum(exponent, axis=-1, keepdims=True)
                    mixed = nn(exponent.astype(low), values) * (1.0 / total)
                    stat = top + jnp.log(total)
                    kept = jnp.where(lane == pair * 2, stat[:TILE], stats[rows, :])
                    stats[rows, :] = jnp.where(lane == pair * 2 + 1, stat[TILE:], kept)
                    both = jnp.where(lane < HEAD, mixed[:TILE], mixed[TILE:])
                    mix[rows, heads(0, pair)] = both.astype(low)

        for_reach(scalars, slots, length, attend)
        saves(b, 0)[3].start()
        loads(b, 0)[3].wait()

        def out(slot, start, rows):
            update[rows, :] = nn(mix[rows, :], w[3])

        each_tile(out, None)

    def convolution(b):
        fill_padded(padded, a_now, slots, length)
        loads(b, 1)[0].wait()

        def run(slot, start, rows):
            near = window(padded, slot, start)
            running = jnp.zeros((TILE, width), wide)
            for offset in range(TAPS):
                at = PAD + offset - TAPS // 2
                tap = depth[offset, pl.ds(b, 1), :] * used_tap(scalars, slots, b, offset)
                running = running + near[at : at + TILE] * tap
            mix[rows, :] = running.astype(low)
            update[rows, :] = nn(running.astype(low), weights[b, 0])

        def clear(rows):
            mix[rows, :] = jnp.zeros((TILE, width), low)

        each_tile(run, clear)
        saves(b, 1)[0].start()

    def feed_forward(b):
        w = weights.at[b]
        mine = pl.ds(pl.multiple_of(place * share, 128), share)

        for copy in loads(b, 2):
            copy.wait()

        def run(slot, start, rows):
            update[rows, :] = jnp.zeros((TILE, width), wide)

            @pl.loop(0, chunks, unroll=4)
            def _(j):
                h = nn(a_now[rows, :], w[j])
                cdf = 0.5 * (1.0 + lax.erf(h * (0.5**0.5)))
                density = jnp.exp(-0.5 * h * h) * 0.3989422804014327
                value = (h * cdf).astype(low)
                active[:, part(j)] = value
                slope[rows, part(j)] = (cdf + h * density).astype(low)
                update[rows, :] += nn(value, w[chunks + j])

            mine_active[rows, :] = active[:, mine]

        def clear(rows):
            mine_active[rows, :] = jnp.zeros((TILE, share), low)

        each_tile(run, clear)
        for save in saves(b, 2):
            save.start()

    @pl.loop(0, BLOCKS)
    def _(b):
        common_saves(b)[0].start()

        @pl.when(b > 0)
        def _():
            def wait_saves(op):
                for save in saves(b - 1, op):
                    save.wait()

            by_op(b - 1, wait_saves)
            for save in common_saves(b - 1)[1:]:
                save.wait()

        for op, branch in enumerate((attention, convolution, feed_forward)):

            @pl.when(op_of(b) == op)
            def _():
                branch(b)

        common_saves(b)[0].wait()

        def norm(slot, start, rows):
            z = x_now[rows, :] + update[rows, :]
            center = z - jnp.mean(z, axis=-1, keepdims=True)
            scale = lax.rsqrt(jnp.mean(center * center, axis=-1, keepdims=True) + norm_eps)
            value = center * scale
            unit[rows, :] = value
            lane = lax.broadcasted_iota(jnp.int32, (TILE, 2 * HEAD), 1)
            stats[rows, :] = jnp.where(lane == HEADS, scale, stats[rows, :])
            keep = live_of(scalars, slot, start, TILE, width)
            value = jnp.where(keep, value * gain[pl.ds(b, 1), :] + shift[pl.ds(b, 1), :], 0.0)
            x_now[rows, :] = value
            a_now[rows, :] = value.astype(low)

        def clear(rows):
            x_now[rows, :] = jnp.zeros((TILE, width), wide)
            a_now[rows, :] = jnp.zeros((TILE, width), low)

        each_tile(norm, clear)
        for save in common_saves(b)[1:]:
            save.start()

    for slot in range(slots):
        rows = pl.ds(pl.multiple_of(slot * length + place * span, span), span)
        layer_out[slot] = x_now[rows, :]

    def wait_last(op):
        for save in saves(BLOCKS - 1, op):
            save.wait()

    by_op(BLOCKS - 1, wait_last)
    for save in common_saves(BLOCKS - 1)[1:]:
        save.wait()


def any_spec():
    return pl.BlockSpec(memory_space=pl.ANY)


def vmem_spec():
    return pl.BlockSpec(memory_space=pltpu.VMEM)


def forward_call(slots, length, peers, scalars, pieces, weights, depth, gain, shift):
    width = gain.shape[-1]
    hidden = weights[2].shape[2]
    rows = slots * length
    shapes = [((slots, length // peers, width), wide)]
    shapes += [
        ((BLOCKS, rows, width), low),
        ((BLOCKS, rows, width), wide),
        ((BLOCKS, rows, 2 * HEAD), wide),
        ((BLOCKS, 3, rows, width), low),
        ((BLOCKS, rows, width), low),
        ((BLOCKS, rows, hidden // peers), low),
        ((BLOCKS, rows, hidden), low),
    ]
    return pl.pallas_call(
        functools.partial(forward_kernel, slots, length, peers),
        out_shape=[jax.ShapeDtypeStruct(*s) for s in shapes],
        in_specs=[pl.BlockSpec(memory_space=pltpu.SMEM)]
        + [vmem_spec()] * len(pieces)
        + [any_spec()] * 5
        + [vmem_spec()] * 3,
        out_specs=[vmem_spec()] + [any_spec()] * (len(shapes) - 1),
        scratch_shapes=[
            pltpu.VMEM((rows, width), wide),
            pltpu.VMEM((rows, width), wide),
            pltpu.VMEM((rows, width), low),
            pltpu.VMEM((rows, width), wide),
            pltpu.VMEM((rows, 2 * HEAD), wide),
            pltpu.VMEM((BLOCKS, 8, width, width), low),
            pltpu.VMEM((rows, width), low),
            pltpu.VMEM((TILE, hidden), low),
            pltpu.VMEM((rows, hidden // peers), low),
            pltpu.VMEM((rows, hidden), low),
            pltpu.VMEM((slots, length + 2 * PAD, width), wide),
            pltpu.SemaphoreType.DMA((BLOCKS, 8)),
            pltpu.SemaphoreType.DMA((BLOCKS, 8)),
        ],
        compiler_params=pltpu.CompilerParams(vmem_limit_bytes=VMEM_LIMIT),
        name="forward_blocks",
    )(scalars, *pieces, *weights, depth, gain, shift)


def up16(count):
    return -(-count // 16) * 16


def payload_rows(width, groups, split):
    pitch = up16(width // groups)
    inner = 0 if split else pitch
    return inner, inner + pitch, inner + pitch + EXTRA


def dense_rows(width, groups, peers):
    pitch = up16(width // groups)
    tail = up16(width // groups // peers)
    return pitch, 2 * pitch, 2 * pitch + tail, 2 * pitch + tail + EXTRA


def norm_back(b, scalars, gain, slot, start, rows, unit, stats, gn, du, small):
    span, width = rows.size, gn.shape[1]
    keep = live_of(scalars, slot, start, span, width)
    g = jnp.where(keep, gn[rows, :], 0.0)
    value = unit[rows, :]
    gu = g * value
    gy = g * gain[b : b + 1, :]
    one = jnp.mean(gy, axis=-1, keepdims=True)
    two = jnp.mean(gu * gain[b : b + 1, :], axis=-1, keepdims=True)
    dz = stats[rows, HEADS : HEADS + 1] * (gy - one - value * two)
    gn[rows, :] = dz
    du[rows, :] = dz.astype(low)
    small[TAPS : TAPS + 1, :] += jnp.sum(gu, axis=0, keepdims=True)
    small[TAPS + 1 : TAPS + 2, :] += jnp.sum(g, axis=0, keepdims=True)


def pair_place(me, d, half):
    key = jnp.bitwise_xor(me, d)
    return 2 * (key % half) + (key < half).astype(jnp.int32)


def norm_kernel(slots, length, peers, groups, scalars, g_h, unit_h, stats_h, act_h, gain, *refs):
    (gn_out, du_out, small) = refs[:3]
    half = groups // 2
    sent = refs[3 : 3 + half]
    (gn, du, unit, stats, act, payload, c_sem, p_sem) = refs[3 + half :]
    b = 0
    width = gn.shape[1]
    cols = width // groups
    span = length // peers
    op = scalars[slots + 2]
    me = scalars[slots + 1]

    def slot_copies(slot):
        rows = pl.ds(pl.multiple_of(slot * length, length), length)
        pairs = [(g_h, gn), (unit_h.at[b], unit), (stats_h.at[b], stats)]
        return [
            pltpu.make_async_copy(source.at[rows], target.at[rows], c_sem.at[3 * slot + j])
            for j, (source, target) in enumerate(pairs)
        ]

    def act_copy():
        return pltpu.make_async_copy(act_h.at[b], act, c_sem.at[3 * slots])

    for slot in range(slots):
        for copy in slot_copies(slot):
            copy.start()

    @pl.when(op == 2)
    def _():
        act_copy().start()

    small[...] = jnp.zeros(small.shape, wide)
    small[TAPS + 2 : TAPS + 3, :] = jnp.full((1, width), op.astype(wide), wide)

    @pl.loop(0, slots)
    def _(slot):
        for copy in slot_copies(slot):
            copy.wait()

        @pl.loop(0, peers)
        def _(j):
            start = pl.multiple_of(j * span, span)
            rows = pl.ds(pl.multiple_of(slot * length + start, span), span)

            @pl.when(start < scalars[slot])
            def _():
                norm_back(b, scalars, gain, slot, start, rows, unit, stats, gn, du, small)

            @pl.when(start >= scalars[slot])
            def _():
                gn[rows, :] = jnp.zeros((span, width), wide)
                du[rows, :] = jnp.zeros((span, width), low)

    saves = [
        pltpu.make_async_copy(gn, gn_out, p_sem.at[half]),
        pltpu.make_async_copy(du, du_out, p_sem.at[half + 1]),
    ]
    for save in saves:
        save.start()

    @pl.when(op == 2)
    def _():
        act_copy().wait()
        values = nn(du[...].T, act[...]).astype(low)
        for d in range(groups):
            payload[pair_place(me, d, half), 0:cols, :] = values[d * cols : (d + 1) * cols]

    @pl.when(op != 2)
    def _():
        for d in range(groups):
            payload[d] = jnp.zeros(payload.shape[1:], low)

    leaving = [
        pltpu.make_async_copy(payload.at[pl.ds(2 * key, 2)], sent[key], p_sem.at[key])
        for key in range(half)
    ]
    for copy in leaving:
        copy.start()
    for copy in leaving + saves:
        copy.wait()


def norm_call(slots, length, peers, groups, scalars, g, kept, gain):
    rows, width = g.shape
    (_, unit, stats, _, _, act, _) = kept
    half = groups // 2
    pitch = up16(width // groups)
    shapes = [((rows, width), wide), ((rows, width), low), ((EXTRA, width), wide)]
    shapes += [((2, pitch, width), low)] * half
    return pl.pallas_call(
        functools.partial(norm_kernel, slots, length, peers, groups),
        out_shape=[jax.ShapeDtypeStruct(*s) for s in shapes],
        in_specs=[pl.BlockSpec(memory_space=pltpu.SMEM)] + [any_spec()] * 4 + [vmem_spec()],
        out_specs=[any_spec(), any_spec(), vmem_spec()] + [any_spec()] * half,
        scratch_shapes=[
            pltpu.VMEM((rows, width), wide),
            pltpu.VMEM((rows, width), low),
            pltpu.VMEM((rows, width), wide),
            pltpu.VMEM((rows, 2 * HEAD), wide),
            pltpu.VMEM((rows, act.shape[2]), low),
            pltpu.VMEM((groups, pitch, width), low),
            pltpu.SemaphoreType.DMA((3 * slots + 1,)),
            pltpu.SemaphoreType.DMA((half + 2,)),
        ],
        compiler_params=pltpu.CompilerParams(vmem_limit_bytes=VMEM_LIMIT),
        name="norm_backward",
    )(scalars, g, unit, stats, act, gain)


def backward_kernel(b, slots, length, peers, groups, first, last, scalars, *refs):
    pieces = refs[: (peers if first else 3)]
    refs = refs[len(pieces) :]
    (a_h, unit_h, stats_h, qkv_h, mix_h, act_h, slope_h) = [ref.at[b] for ref in refs[:7]]
    (proj_h, out_h, fin_h, fout_h, point_h, depth, gain) = refs[7:14]
    g_out = refs[14]
    outputs = 1 if first else groups
    sent = refs[15 : 15 + outputs]
    (payload, gn, du, a_in, unit, stats, w_in, w_out, mix, act, slope, padded, stats_t, turned, small) = refs[
        15 + outputs : 30 + outputs
    ]
    (w_sem, s_sem, c_sem, p_sem) = refs[30 + outputs :]
    width = a_in.shape[1]
    hidden = w_in.shape[1]
    chunks = hidden // width
    tiles = length // TILE
    own = width // peers
    cols = width // groups
    hidden_cols = hidden // groups
    place = scalars[slots]
    me = scalars[slots + 1]
    op = scalars[slots + 2 + 2 * b]
    span = length // peers
    inner_at, small_at, _ = payload_rows(width, groups, last)

    def key_of(d):
        return d if first else jnp.bitwise_xor(me, d)

    def part(j):
        return pl.ds(j * width, width)

    def heads(j, pair):
        return pl.ds(pl.multiple_of(j * width + pair * 2 * HEAD, 2 * HEAD), 2 * HEAD)

    def slot_copies(slot):
        rows = pl.ds(pl.multiple_of(slot * length, length), length)
        if first:
            pairs = [(unit_h, unit)]
        else:
            pairs = [(pieces[0], gn), (pieces[1], du)]
        return [
            pltpu.make_async_copy(source.at[rows], target.at[rows], c_sem.at[2 * slot + j])
            for j, (source, target) in enumerate(pairs)
        ]

    def stats_copy():
        return pltpu.make_async_copy(stats_h, stats, c_sem.at[2 * slots])

    def input_copy():
        return pltpu.make_async_copy(a_h, a_in, c_sem.at[2 * slots + 1])

    def attn_copies():
        return (
            [
                pltpu.make_async_copy(qkv_h.at[j], slope.at[:, part(j)], s_sem.at[j])
                for j in range(3)
            ]
            + [pltpu.make_async_copy(mix_h, mix, s_sem.at[3])]
            + [
                pltpu.make_async_copy(proj_h.at[b, j], w_out.at[part(j)], w_sem.at[j])
                for j in range(3)
            ]
            + [pltpu.make_async_copy(out_h.at[b], w_out.at[part(3)], w_sem.at[3])]
        )

    def conv_copies():
        return [
            pltpu.make_async_copy(mix_h, mix, s_sem.at[0]),
            pltpu.make_async_copy(point_h.at[b], w_out.at[part(0)], w_sem.at[0]),
        ]

    def ffn_copies():
        return [
            pltpu.make_async_copy(fout_h.at[b], w_out, w_sem.at[0]),
            pltpu.make_async_copy(slope_h, slope, s_sem.at[0]),
            pltpu.make_async_copy(fin_h.at[b], w_in, w_sem.at[1]),
        ] + ([pltpu.make_async_copy(act_h, act, s_sem.at[1])] if first else [])

    stats_copy().start()
    for slot in range(slots):
        for copy in slot_copies(slot):
            copy.start()
    for index, copies in enumerate((attn_copies, conv_copies, ffn_copies)):

        @pl.when(op == index)
        def _():
            for copy in copies():
                copy.start()

    input_copy().start()

    def each_tile(body, rest):
        tiles_of(scalars, slots, length, body, rest)

    stats_copy().wait()
    if first:
        small[...] = jnp.zeros(small.shape, wide)
        small[TAPS + 2 : TAPS + 3, :] = jnp.full((1, width), op.astype(wide), wide)

        @pl.loop(0, slots)
        def _(slot):
            for copy in slot_copies(slot):
                copy.wait()

            @pl.loop(0, peers)
            def _(j):
                start = pl.multiple_of(j * span, span)
                rows = pl.ds(pl.multiple_of(slot * length + start, span), span)

                @pl.when(start < scalars[slot])
                def _():
                    if first:
                        for key in range(peers):

                            @pl.when(jnp.bitwise_xor(place, key) == j)
                            def _():
                                gn[rows, :] = pieces[key][slot].astype(wide)

                    norm_back(b, scalars, gain, slot, start, rows, unit, stats, gn, du, small)

                @pl.when(start >= scalars[slot])
                def _():
                    gn[rows, :] = jnp.zeros((span, width), wide)
                    du[rows, :] = jnp.zeros((span, width), low)

    else:
        small[...] = pieces[2][...]
        for slot in range(slots):
            for copy in slot_copies(slot):
                copy.wait()
    input_copy().wait()

    def turn_own(source):
        for s in range(peers):

            @pl.when(place == s)
            def _():
                turned[...] = source[:, s * own : (s + 1) * own].T

    def put_out(start, values):
        for d in range(groups):
            piece = values[d * cols : (d + 1) * cols].astype(low)
            payload[key_of(d), 0:cols, start : start + values.shape[1]] = piece

    def put_point(values):
        count = cols // peers
        for d in range(groups):
            for p in range(peers):
                piece = values[d * cols + p * count : d * cols + (p + 1) * count].astype(low)
                payload[key_of(d), 0:count, p * own : (p + 1) * own] = piece

    def put_in(d, values):
        for p in range(own // cols):
            at = slice(p * hidden_cols, (p + 1) * hidden_cols)
            payload[key_of(d), inner_at : inner_at + cols, at] = values[p * cols : (p + 1) * cols]

    def add_back(grad):
        if last:
            @pl.loop(0, slots)
            def _(slot):
                rows = pl.ds(pl.multiple_of(slot * length + place * span, span), span)
                keep = live_of(scalars, slot, place * span, span, width)

                @pl.when(place * span < scalars[slot])
                def _():
                    g_out[slot] = jnp.where(keep, gn[rows, :] + grad(rows), 0.0)

                @pl.when(place * span >= scalars[slot])
                def _():
                    g_out[slot] = jnp.zeros((span, width), wide)

        else:

            def add(slot, start, rows):
                g_out[rows, :] = gn[rows, :] + grad(rows)

            each_tile(add, None)

    @pl.when(op == 0)
    def _():
        copies = attn_copies()
        copies[7].wait()
        for copy in copies[:4]:
            copy.wait()
        turn_own(mix)
        put_out(3 * own, nn(turned[...], du[...]).T)

        def back(slot, start, rows):
            mix[rows, :] = nt(du[rows, :], w_out[part(3), :]).astype(low)

        def clear(rows):
            for j in range(3):
                slope[rows, part(j)] = jnp.zeros((TILE, width), low)

        each_tile(back, clear)

        @pl.loop(0, slots)
        def _(slot):
            stats_t[slot] = stats[pl.ds(pl.multiple_of(slot * length, length), length), :].T

        def attend(slot, reach):
            every = pl.ds(pl.multiple_of(slot * length, length), reach)
            upper = lax.broadcasted_iota(jnp.int32, (2 * HEAD, reach), 0) < HEAD

            @pl.loop(0, HEADS // 2)
            def _(pair):
                keys = slope[every, heads(1, pair)]
                values = slope[every, heads(2, pair)]
                scaled = keys * FACTOR
                queries = split_heads(slope[every, heads(0, pair)] * FACTOR)
                grads = split_heads(mix[every, heads(0, pair)])
                scores = [nt(keys, one) for one in queries]
                products = [nt(values, one) for one in grads]
                dk = jnp.zeros((reach, 2 * HEAD), wide)
                dv = jnp.zeros((reach, 2 * HEAD), wide)
                dq = []
                for head in range(2):
                    stat = stats_t[slot, pl.ds(pair * 2 + head, 1), 0:reach]
                    soft = jnp.exp(jnp.minimum(scores[head] - stat, 0.0))
                    product = soft * products[head]
                    inner = jnp.sum(product, axis=0, keepdims=True)
                    grad_scores = (product - soft * inner).astype(low)
                    dq.append(tn(scaled, grad_scores))
                    dk = dk + nn(grad_scores, queries[head])
                    dv = dv + nn(soft.astype(low), grads[head])
                dq = jnp.where(upper, dq[0], dq[1])
                slope[every, heads(0, pair)] = dq.T.astype(low)
                slope[every, heads(1, pair)] = dk.astype(low)
                slope[every, heads(2, pair)] = dv.astype(low)

        for_reach(scalars, slots, length, attend)
        for j in range(3):
            copies[4 + j].wait()
        turn_own(a_in)

        for j in range(3):
            put_out(j * own, nn(turned[...], slope[:, part(j)]).T)

        def grad(rows):
            total = nt(slope[rows, part(0)], w_out[part(0), :])
            for j in range(1, 3):
                total = total + nt(slope[rows, part(j)], w_out[part(j), :])
            return total

        add_back(grad)

    @pl.when(op == 1)
    def _():
        copies = conv_copies()
        for copy in copies:
            copy.wait()
        turn_own(mix)
        put_point(nn(turned[...], du[...]).T)

        def back(slot, start, rows):
            mix[rows, :] = nt(du[rows, :], w_out[part(0), :]).astype(low)

        def clear(rows):
            mix[rows, :] = jnp.zeros((TILE, width), low)

        each_tile(back, clear)
        fill_padded(padded, a_in, slots, length)

        def depth_terms(slot, start, rows):
            near = window(padded, slot, start)
            grads = mix[rows, :].astype(wide)
            for offset in range(TAPS):
                at = PAD + offset - TAPS // 2
                term = jnp.sum(near[at : at + TILE] * grads, axis=0, keepdims=True)
                small[offset : offset + 1, :] += term * used_tap(scalars, slots, b, offset)

        each_tile(depth_terms, None)
        fill_padded(padded, mix, slots, length)

        def spread(slot, start, rows):
            near = window(padded, slot, start)
            running = gn[rows, :]
            for offset in range(TAPS):
                at = PAD - offset + TAPS // 2
                tap = depth[offset, b : b + 1, :] * used_tap(scalars, slots, b, offset)
                running = running + near[at : at + TILE] * tap
            gn[rows, :] = running

        each_tile(spread, None)
        add_back(lambda rows: 0.0)

    @pl.when(op == 2)
    def _():
        copies = ffn_copies()
        copies[0].wait()
        copies[1].wait()

        def back(slot, start, rows):
            upstream = du[rows, :]
            for j in range(chunks):
                df = nt(upstream, w_out[part(j), :]).astype(low).astype(wide)
                slope[rows, part(j)] = (df * slope[rows, part(j)].astype(wide)).astype(low)

        def clear(rows):
            slope[rows, :] = jnp.zeros((TILE, hidden), low)

        each_tile(back, clear)
        copies[2].wait()
        if first:
            copies[3].wait()
            put_out(0, nn(du[...].T, act[...]))
        turn_own(a_in)
        for d in range(groups):
            piece = slope[:, d * hidden_cols : (d + 1) * hidden_cols]
            put_in(d, nn(turned[...], piece).astype(low))
        add_back(lambda rows: nt(slope[rows, :], w_in[...]))

    for d in range(groups):
        payload[d, small_at : small_at + EXTRA, :] = small[...].astype(low)
    order = sorted(range(groups), key=lambda key: key < groups // 2)
    leaving = [
        pltpu.make_async_copy(
            payload.at[key], sent[0].at[key] if first else sent[key], p_sem.at[key]
        )
        for key in order
    ]
    for copy in leaving:
        copy.start()
    for copy in leaving:
        copy.wait()


def backward_call(b, slots, length, peers, groups, scalars, pieces, kept, weights, depth, gain):
    width = gain.shape[-1]
    hidden = weights[2].shape[2]
    rows = slots * length
    first = b == BLOCKS - 1
    last = b == 0
    count = payload_rows(width, groups, last)[2]
    shapes = [
        ((slots, length // peers, width) if last else (rows, width), wide),
    ] + ([((groups, count, width), low)] if first else [((count, width), low)] * groups)
    return pl.pallas_call(
        functools.partial(backward_kernel, b, slots, length, peers, groups, first, last),
        out_shape=[jax.ShapeDtypeStruct(*s) for s in shapes],
        in_specs=[pl.BlockSpec(memory_space=pltpu.SMEM)]
        + ([vmem_spec()] * peers if first else [any_spec(), any_spec(), vmem_spec()])
        + [any_spec()] * 12
        + [vmem_spec()] * 2,
        out_specs=[vmem_spec()] + [any_spec()] * (len(shapes) - 1),
        scratch_shapes=[
            pltpu.VMEM((groups, count, width), low),
            pltpu.VMEM((rows, width), wide),
            pltpu.VMEM((rows, width), low),
            pltpu.VMEM((rows, width), low),
            pltpu.VMEM((rows, width), wide),
            pltpu.VMEM((rows, 2 * HEAD), wide),
            pltpu.VMEM((width, hidden), low),
            pltpu.VMEM((hidden, width), low),
            pltpu.VMEM((rows, width), low),
            pltpu.VMEM((rows, hidden // peers), low),
            pltpu.VMEM((rows, hidden), low),
            pltpu.VMEM((slots, length + 2 * PAD, width), wide),
            pltpu.VMEM((slots, 2 * HEAD, length), wide),
            pltpu.VMEM((width // peers, rows), low),
            pltpu.VMEM((EXTRA, width), wide),
            pltpu.SemaphoreType.DMA((4,)),
            pltpu.SemaphoreType.DMA((4,)),
            pltpu.SemaphoreType.DMA((2 * slots + 2,)),
            pltpu.SemaphoreType.DMA((groups,)),
        ],
        compiler_params=pltpu.CompilerParams(vmem_limit_bytes=VMEM_LIMIT),
        name="backward_block",
    )(scalars, *pieces, *kept, *weights, depth, gain)


def add_pieces(pieces, small, groups, peers, split):
    width = small.shape[2]
    cols = width // groups
    inner_at, small_at, _ = payload_rows(width, groups, split)
    sums = [None] * 4

    def add(index, value):
        sums[index] = value if sums[index] is None else sums[index] + value

    for at, piece in pieces:
        terms = piece[small_at : small_at + EXTRA, :].astype(wide)
        op = terms[TAPS + 2 : TAPS + 3, :]
        matrix = piece[0:cols, :].astype(wide)
        add(0, jnp.where(op == 0.0, matrix, 0.0))
        if not split:
            add(1, jnp.where(op == 2.0, matrix, 0.0))
        inner = piece[inner_at : inner_at + cols, :].astype(wide)
        add(2, jnp.where(op == 2.0, inner, 0.0))
        add(3, jnp.where(op == 1.0, piece[0 : cols // peers, :].astype(wide), 0.0))
        row = lax.broadcasted_iota(jnp.int32, terms.shape, 0)
        terms = jnp.where((row < TAPS) & (op != 1.0), 0.0, terms)
        for index in range(3):
            terms = jnp.where(row == TAPS + 2 + index, (op == index).astype(wide), terms)
        terms = jnp.where(row < TAPS + 5, terms, 0.0)
        small[at] = terms
    total = small[0]
    for index in range(1, len(pieces)):
        total = total + small[index]
    return sums, total


def placed(pieces, me):
    return [(jnp.bitwise_xor(me, key) % len(pieces), piece) for key, piece in enumerate(pieces)]


def early_kernel(index, *refs):
    pieces, total = refs[:-1], refs[-1]
    value = pieces[0][index].astype(wide)
    for piece in pieces[1:]:
        value = value + piece[index].astype(wide)
    total[...] = value.astype(low)


def early_call(pieces):
    return pl.pallas_call(
        functools.partial(early_kernel, 0),
        out_shape=jax.ShapeDtypeStruct(pieces[0].shape[1:], low),
        in_specs=[vmem_spec()] * len(pieces),
        out_specs=vmem_spec(),
        compiler_params=pltpu.CompilerParams(vmem_limit_bytes=VMEM_LIMIT),
        name="early_sum",
    )(*pieces)


def relay_kernel(groups, peers, slots, scalars, *refs):
    pieces, (dense, small) = refs[:-2], refs[-2:]
    width = dense.shape[1]
    cols = width // groups
    inner_at, point_at, small_at, _ = dense_rows(width, groups, peers)
    sums, total = add_pieces(placed(pieces, scalars[slots + 1]), small, groups, peers, True)
    dense[0:cols, :] = sums[0].astype(low)
    dense[inner_at : inner_at + cols, :] = sums[2].astype(low)
    dense[point_at : point_at + cols // peers, :] = sums[3].astype(low)
    dense[small_at : small_at + EXTRA, :] = total.astype(low)


def relay_call(groups, peers, slots, scalars, pieces):
    width = pieces[0].shape[1]
    count = dense_rows(width, groups, peers)[3]
    return pl.pallas_call(
        functools.partial(relay_kernel, groups, peers, slots),
        out_shape=jax.ShapeDtypeStruct((count, width), low),
        in_specs=[pl.BlockSpec(memory_space=pltpu.SMEM)] + [vmem_spec()] * len(pieces),
        out_specs=vmem_spec(),
        scratch_shapes=[pltpu.VMEM((len(pieces), EXTRA, width), wide)],
        compiler_params=pltpu.CompilerParams(vmem_limit_bytes=VMEM_LIMIT),
        name="relay_sum",
    )(scalars, *pieces)


def final_kernel(groups, peers, slots, scalars, *refs):
    half = groups // 2
    near, early, (early_dense, dense, every) = refs[:half], refs[half : 2 * half], refs[2 * half : 2 * half + 3]
    (proj, out, f_in, f_out, point, depth, gain, shift, small) = refs[2 * half + 3 :]
    width = dense.shape[1]
    cols = width // groups
    own = width // peers
    hidden_cols = f_in.shape[2]
    inner_at, point_at, small_at, _ = dense_rows(width, groups, peers)
    for b in range(BLOCKS):
        if b:
            pieces = [(d, every.at[d]) for d in range(groups)]
        else:
            pieces = placed(near, scalars[slots + 1])
        sums, total = add_pieces(pieces, small, groups, peers, not b)
        points = sums[3]
        if not b:
            total = total.astype(low).astype(wide)
            total = total + dense[small_at : small_at + EXTRA, :].astype(wide)
            sums[0] = sums[0] + dense[0:cols, :].astype(wide)
            sums[1] = early_dense[0:cols, :].astype(wide)
            for piece in early:
                sums[1] = sums[1] + piece[1, 0:cols, :].astype(wide)
            sums[2] = sums[2] + dense[inner_at : inner_at + cols, :].astype(wide)
            points = points + dense[point_at : point_at + cols // peers, :].astype(wide)
        share = [1.0 / total[TAPS + 2 + op : TAPS + 3 + op, :] for op in range(3)]
        attn = sums[0] * share[0]
        for j in range(3):
            proj[b, j] = attn[:, j * own : (j + 1) * own].T
        out[b] = attn[:, 3 * own :].T
        f_out[b] = sums[1] * share[2]
        inner = sums[2] * share[2]
        for p in range(own // cols):
            f_in[b, p * cols : (p + 1) * cols, :] = inner[:, p * hidden_cols : (p + 1) * hidden_cols]
        points = points * share[1]
        points = jnp.concatenate([points[:, p * own : (p + 1) * own] for p in range(peers)], axis=0)
        point[b] = points.T
        depth[:, b, :] = total[0:TAPS] * share[1]
        gain[b : b + 1, :] = total[TAPS : TAPS + 1] * (1.0 / groups)
        shift[b : b + 1, :] = total[TAPS + 1 : TAPS + 2] * (1.0 / groups)


def final_call(groups, peers, slots, hidden, scalars, inputs):
    width = inputs[0].shape[-1]
    rows, cols = width // peers, width // groups
    shapes = [
        (BLOCKS, 3, rows, cols),
        (BLOCKS, rows, cols),
        (BLOCKS, rows, hidden // groups),
        (BLOCKS, cols, hidden // peers),
        (BLOCKS, rows, cols),
        (TAPS, BLOCKS, width),
        (BLOCKS, width),
        (BLOCKS, width),
    ]
    return pl.pallas_call(
        functools.partial(final_kernel, groups, peers, slots),
        out_shape=[jax.ShapeDtypeStruct(s, wide) for s in shapes],
        in_specs=[pl.BlockSpec(memory_space=pltpu.SMEM)] + [vmem_spec()] * len(inputs),
        out_specs=[vmem_spec()] * len(shapes),
        scratch_shapes=[pltpu.VMEM((groups, EXTRA, width), wide)],
        compiler_params=pltpu.CompilerParams(vmem_limit_bytes=VMEM_LIMIT),
        name="final_sum",
    )(scalars, *inputs)


def across(piece, axis, key):
    return lax.ppermute(piece, axis, [(i, i ^ key) for i in range(lax.axis_size(axis))])


def local(
    layer_in,
    lengths,
    op_ids,
    kernel_ids,
    attn_proj,
    attn_out,
    ffn_in,
    ffn_out,
    point_weights,
    depth_weights,
    norm_gains,
    norm_shifts,
    cotangent,
):
    slots, span, width = layer_in.shape
    peers = lax.axis_size("seq")
    groups = lax.axis_size("dp")
    place = lax.axis_index("seq").astype(jnp.int32)
    length = span * peers
    weights = (attn_proj, attn_out, ffn_in, ffn_out, point_weights)

    me = lax.axis_index("dp").astype(jnp.int32)
    half = groups // 2

    chosen = jnp.stack([op_ids[0], kernel_ids[0]], axis=1).reshape(-1)
    scalars = jnp.concatenate([lengths, jnp.stack([place, me]), chosen])
    depth_weights = jnp.swapaxes(depth_weights, 0, 1)

    later = cotangent.astype(low)
    parts = {0: layer_in.astype(low)}
    reach = peers // 2
    while reach:
        moved = {key ^ reach: across(part, "seq", reach) for key, part in parts.items()}
        if reach == peers // 2:
            moved, later, scalars = lax.optimization_barrier((moved, later, scalars))
        parts.update(moved)
        reach //= 2
    x_parts = [parts[key] for key in range(peers)]
    later, x_parts = lax.optimization_barrier((later, x_parts))
    cot_parts = [later] + [across(later, "seq", key) for key in range(1, peers)]
    layer_out, *saved = forward_call(
        slots, length, peers, scalars, x_parts, weights, depth_weights, norm_gains, norm_shifts
    )

    g, payload = backward_call(
        1, slots, length, peers, groups, scalars, cot_parts, saved, weights, depth_weights, norm_gains
    )
    every = lax.all_to_all(payload, "dp", 0, 0, tiled=True)
    grad, rounded, small, *early = norm_call(
        slots, length, peers, groups, scalars, g, saved, norm_gains
    )
    early = [early[0]] + [across(early[key], "dp", key) for key in range(1, half)]
    g, *sent = backward_call(
        0, slots, length, peers, groups, scalars, [grad, rounded, small], saved, weights,
        depth_weights, norm_gains,
    )
    early, g = lax.optimization_barrier((early, g))
    early_sum = early_call(early)
    early_dense = across(early_sum, "dp", half)
    far = [sent[half]] + [across(sent[half + key], "dp", key) for key in range(1, half)]
    far, _ = lax.optimization_barrier((far, early_sum))
    partial = relay_call(groups, peers, slots, scalars, far)
    rest, partial = lax.optimization_barrier((sent[:half], partial))
    dense = across(partial, "dp", half)
    near = [rest[0]] + [across(rest[key], "dp", key) for key in range(1, half)]
    proj, out, f_in, f_out, point, depth, gain, shift = final_call(
        groups, peers, slots, ffn_in.shape[2], scalars, near + early + [early_dense, dense, every]
    )
    f_out = jnp.swapaxes(f_out, 1, 2)
    depth = jnp.swapaxes(depth, 0, 1)
    return (layer_out, g, proj, out, f_in, f_out, point, depth, gain, shift)


def solution(mesh):
    placed = (
        P("dp", "seq", None),
        P("dp"),
        P("dp", None),
        P("dp", None),
        P(),
        P(),
        P(),
        P(),
        P(),
        P(),
        P(),
        P(),
        P("dp", "seq", None),
    )
    return jax.shard_map(
        local,
        mesh=mesh,
        in_specs=placed,
        out_specs=(
            P("dp", "seq", None),
            P("dp", "seq", None),
            P(None, None, "seq", "dp"),
            P(None, "seq", "dp"),
            P(None, "seq", "dp"),
            P(None, "seq", "dp"),
            P(None, "seq", "dp"),
            P(),
            P(),
            P(),
        ),
        check_vma=False,
    )
```

```python
import functools

import jax
import jax.numpy as jnp
from jax import lax
from jax.experimental import pallas as pl
from jax.experimental.pallas import tpu as pltpu
from jax.sharding import PartitionSpec as P

HEADS = 12
HEAD = 64
TAPS = 7
BLOCKS = 2
EXTRA = 16
PAD = 8
norm_eps = 1e-05
low = jnp.bfloat16
wide = jnp.float32
VMEM_LIMIT = 60 * 1024 * 1024


def nn(left, right):
    return lax.dot_general(left, right, (((1,), (0,)), ((), ())), preferred_element_type=wide)


def nt(left, right):
    return lax.dot_general(left, right, (((1,), (1,)), ((), ())), preferred_element_type=wide)


def tn(left, right):
    return lax.dot_general(left, right, (((0,), (0,)), ((), ())), preferred_element_type=wide)


def live_of(scalars, slot, start, count, width):
    at = lax.broadcasted_iota(jnp.int32, (count, width), 0) + start
    return at < scalars[slot]


def used_tap(scalars, slots, b, offset):
    return (abs(offset - TAPS // 2) <= scalars[slots + 3 + 2 * b] + 1).astype(wide)


def live_tiles(scalars, slot, size):
    return (scalars[slot] + size - 1) // size


def for_reach(scalars, slots, length, body):
    @pl.loop(0, slots)
    def _(slot):
        @pl.when(scalars[slot] <= length // 2)
        def _():
            body(slot, length // 2)

        @pl.when(scalars[slot] > length // 2)
        def _():
            body(slot, length)


def tiles_of(scalars, slots, length, body, rest):
    @pl.loop(0, slots)
    def _(slot):
        count = live_tiles(scalars, slot, TILE)

        @pl.loop(0, count)
        def _(t):
            start = pl.multiple_of(t * TILE, TILE)
            body(slot, start, pl.ds(pl.multiple_of(slot * length + start, TILE), TILE))

        if rest is not None:

            @pl.loop(count, length // TILE)
            def _(t):
                rest(pl.ds(pl.multiple_of(slot * length + t * TILE, TILE), TILE))


def fill_padded(padded, source, slots, length):
    width = padded.shape[2]

    @pl.loop(0, slots)
    def _(slot):
        padded[slot, 0:PAD, :] = jnp.zeros((PAD, width), wide)
        padded[slot, PAD + length : PAD + length + PAD, :] = jnp.zeros((PAD, width), wide)

        @pl.loop(0, length // 128)
        def _(t):
            rows = pl.ds(pl.multiple_of(slot * length + t * 128, 128), 128)
            at = pl.ds(pl.multiple_of(PAD + t * 128, PAD), 128)
            padded[slot, at, :] = source[rows, :].astype(wide)


def window(padded, slot, start):
    return padded[slot, pl.ds(pl.multiple_of(start, TILE), TILE + 2 * PAD), :]


TILE = 256
FACTOR = HEAD**-0.5


def split_heads(tensor):
    lane = lax.broadcasted_iota(jnp.int32, tensor.shape, 1)
    none = jnp.zeros((), tensor.dtype)
    return [jnp.where(lane < HEAD, tensor, none), jnp.where(lane < HEAD, none, tensor)]


def pair_rows(tensor):
    return jnp.concatenate(split_heads(tensor), axis=0)


def forward_kernel(slots, length, peers, lengths_of, *refs):
    pieces = refs[:peers]
    (proj_h, out_h, fin_h, fout_h, point_h, depth, gain, shift) = refs[peers : peers + 8]
    refs = refs[peers + 8 :]
    layer_out = refs[0]
    saved = refs[1:8]
    (x_now, update, a_now, unit, stats, weights, mix, active, mine_active, slope, padded) = refs[8:19]
    w_sem, s_sem = refs[19:]
    scalars = lengths_of
    width = a_now.shape[1]
    hidden = slope.shape[1]
    share = mine_active.shape[1]
    span = length // peers
    chunks = hidden // width
    tiles = length // TILE
    place = scalars[slots]

    def part(j):
        return pl.ds(pl.multiple_of(j * width, width), width)

    def heads(j, pair):
        return pl.ds(pl.multiple_of(j * width + pair * 2 * HEAD, 2 * HEAD), 2 * HEAD)

    def op_of(b):
        return scalars[slots + 2 + 2 * b]

    def loads(b, op):
        w = weights.at[b]
        if op == 0:
            pairs = [(proj_h.at[b, j], j) for j in range(3)] + [(out_h.at[b], 3)]
        elif op == 1:
            pairs = [(point_h.at[b], 0)]
        else:
            pairs = [(fin_h.at[b, :, part(j)], j) for j in range(chunks)]
            pairs += [(fout_h.at[b, part(j)], chunks + j) for j in range(chunks)]
        return [pltpu.make_async_copy(source, w.at[j], w_sem.at[b, j]) for source, j in pairs]

    def saves(b, op):
        (a_h, unit_h, stats_h, qkv_h, mix_h, act_h, slope_h) = [ref.at[b] for ref in saved]
        if op == 0:
            pairs = [(slope.at[:, part(j)], qkv_h.at[j]) for j in range(3)] + [(mix, mix_h)]
        elif op == 1:
            pairs = [(mix, mix_h)]
        else:
            pairs = [(mine_active, act_h), (slope, slope_h)]
        return [
            pltpu.make_async_copy(source, target, s_sem.at[b, j])
            for j, (source, target) in enumerate(pairs)
        ]

    def common_saves(b):
        (a_h, unit_h, stats_h) = [ref.at[b] for ref in saved[:3]]
        pairs = [(a_now, a_h), (unit, unit_h), (stats, stats_h)]
        return [
            pltpu.make_async_copy(source, target, s_sem.at[b, 4 + j])
            for j, (source, target) in enumerate(pairs)
        ]

    def by_op(b, action):
        for op in range(3):

            @pl.when(op_of(b) == op)
            def _():
                action(op)

    def each_tile(body, rest):
        tiles_of(scalars, slots, length, body, rest)

    for b in range(BLOCKS):

        def start_all(op):
            for copy in loads(b, op):
                copy.start()

        by_op(b, start_all)

    for key, piece in enumerate(pieces):
        origin = jnp.bitwise_xor(place, key) * span

        @pl.loop(0, slots)
        def _(slot):
            rows = pl.ds(pl.multiple_of(slot * length + origin, span), span)
            keep = live_of(scalars, slot, origin, span, width)
            value = jnp.where(keep, piece[slot].astype(wide), 0.0)
            x_now[rows, :] = value
            a_now[rows, :] = value.astype(low)

    def attention(b):
        w = weights.at[b]

        @pl.loop(0, 3)
        def _(j):
            pltpu.make_async_copy(proj_h.at[b, j], w.at[j], w_sem.at[b, j]).wait()

            def project(slot, start, rows):
                slope[rows, part(j)] = nn(a_now[rows, :], w[j]).astype(low)

            def clear(rows):
                slope[rows, part(j)] = jnp.zeros((TILE, width), low)

            each_tile(project, clear)
            pltpu.make_async_copy(slope.at[:, part(j)], saved[3].at[b, j], s_sem.at[b, j]).start()

        def clear_mix(rows):
            mix[rows, :] = jnp.zeros((TILE, width), low)

        each_tile(lambda slot, start, rows: None, clear_mix)

        def attend(slot, reach):
            base = pl.multiple_of(slot * length, length)
            key_at = lax.broadcasted_iota(jnp.int32, (1, reach), 1)
            bias = jnp.where(key_at < scalars[slot], 0.0, -1000000000.0).astype(wide)
            lane = lax.broadcasted_iota(jnp.int32, (TILE, 2 * HEAD), 1)

            @pl.loop(0, HEADS // 2, unroll=3)
            def _(pair):
                keys = slope[pl.ds(base, reach), heads(1, pair)]
                values = slope[pl.ds(base, reach), heads(2, pair)]
                for t in range(reach // TILE):
                    rows = pl.ds(pl.multiple_of(base + t * TILE, TILE), TILE)
                    scores = nt(pair_rows(slope[rows, heads(0, pair)] * FACTOR), keys) + bias
                    top = jnp.max(scores, axis=-1, keepdims=True)
                    exponent = jnp.exp(scores - top)
                    total = jnp.sum(exponent, axis=-1, keepdims=True)
                    mixed = nn(exponent.astype(low), values) * (1.0 / total)
                    stat = top + jnp.log(total)
                    kept = jnp.where(lane == pair * 2, stat[:TILE], stats[rows, :])
                    stats[rows, :] = jnp.where(lane == pair * 2 + 1, stat[TILE:], kept)
                    both = jnp.where(lane < HEAD, mixed[:TILE], mixed[TILE:])
                    mix[rows, heads(0, pair)] = both.astype(low)

        for_reach(scalars, slots, length, attend)
        saves(b, 0)[3].start()
        loads(b, 0)[3].wait()

        def out(slot, start, rows):
            update[rows, :] = nn(mix[rows, :], w[3])

        each_tile(out, None)

    def convolution(b):
        fill_padded(padded, a_now, slots, length)
        loads(b, 1)[0].wait()

        def run(slot, start, rows):
            near = window(padded, slot, start)
            running = jnp.zeros((TILE, width), wide)
            for offset in range(TAPS):
                at = PAD + offset - TAPS // 2
                tap = depth[offset, pl.ds(b, 1), :] * used_tap(scalars, slots, b, offset)
                running = running + near[at : at + TILE] * tap
            mix[rows, :] = running.astype(low)
            update[rows, :] = nn(running.astype(low), weights[b, 0])

        def clear(rows):
            mix[rows, :] = jnp.zeros((TILE, width), low)

        each_tile(run, clear)
        saves(b, 1)[0].start()

    def feed_forward(b):
        w = weights.at[b]
        mine = pl.ds(pl.multiple_of(place * share, 128), share)

        for copy in loads(b, 2):
            copy.wait()

        def run(slot, start, rows):
            update[rows, :] = jnp.zeros((TILE, width), wide)

            @pl.loop(0, chunks, unroll=4)
            def _(j):
                h = nn(a_now[rows, :], w[j])
                cdf = 0.5 * (1.0 + lax.erf(h * (0.5**0.5)))
                density = jnp.exp(-0.5 * h * h) * 0.3989422804014327
                value = (h * cdf).astype(low)
                active[:, part(j)] = value
                slope[rows, part(j)] = (cdf + h * density).astype(low)
                update[rows, :] += nn(value, w[chunks + j])

            mine_active[rows, :] = active[:, mine]

        def clear(rows):
            mine_active[rows, :] = jnp.zeros((TILE, share), low)

        each_tile(run, clear)
        for save in saves(b, 2):
            save.start()

    @pl.loop(0, BLOCKS)
    def _(b):
        common_saves(b)[0].start()

        @pl.when(b > 0)
        def _():
            def wait_saves(op):
                for save in saves(b - 1, op):
                    save.wait()

            by_op(b - 1, wait_saves)
            for save in common_saves(b - 1)[1:]:
                save.wait()

        for op, branch in enumerate((attention, convolution, feed_forward)):

            @pl.when(op_of(b) == op)
            def _():
                branch(b)

        common_saves(b)[0].wait()

        def norm(slot, start, rows):
            z = x_now[rows, :] + update[rows, :]
            center = z - jnp.mean(z, axis=-1, keepdims=True)
            scale = lax.rsqrt(jnp.mean(center * center, axis=-1, keepdims=True) + norm_eps)
            value = center * scale
            unit[rows, :] = value
            lane = lax.broadcasted_iota(jnp.int32, (TILE, 2 * HEAD), 1)
            stats[rows, :] = jnp.where(lane == HEADS, scale, stats[rows, :])
            keep = live_of(scalars, slot, start, TILE, width)
            value = jnp.where(keep, value * gain[pl.ds(b, 1), :] + shift[pl.ds(b, 1), :], 0.0)
            x_now[rows, :] = value
            a_now[rows, :] = value.astype(low)

        def clear(rows):
            x_now[rows, :] = jnp.zeros((TILE, width), wide)
            a_now[rows, :] = jnp.zeros((TILE, width), low)

        each_tile(norm, clear)
        for save in common_saves(b)[1:]:
            save.start()

    for slot in range(slots):
        rows = pl.ds(pl.multiple_of(slot * length + place * span, span), span)
        layer_out[slot] = x_now[rows, :]

    def wait_last(op):
        for save in saves(BLOCKS - 1, op):
            save.wait()

    by_op(BLOCKS - 1, wait_last)
    for save in common_saves(BLOCKS - 1)[1:]:
        save.wait()


def any_spec():
    return pl.BlockSpec(memory_space=pl.ANY)


def vmem_spec():
    return pl.BlockSpec(memory_space=pltpu.VMEM)


def forward_call(slots, length, peers, scalars, pieces, weights, depth, gain, shift):
    width = gain.shape[-1]
    hidden = weights[2].shape[2]
    rows = slots * length
    shapes = [((slots, length // peers, width), wide)]
    shapes += [
        ((BLOCKS, rows, width), low),
        ((BLOCKS, rows, width), wide),
        ((BLOCKS, rows, 2 * HEAD), wide),
        ((BLOCKS, 3, rows, width), low),
        ((BLOCKS, rows, width), low),
        ((BLOCKS, rows, hidden // peers), low),
        ((BLOCKS, rows, hidden), low),
    ]
    return pl.pallas_call(
        functools.partial(forward_kernel, slots, length, peers),
        out_shape=[jax.ShapeDtypeStruct(*s) for s in shapes],
        in_specs=[pl.BlockSpec(memory_space=pltpu.SMEM)]
        + [vmem_spec()] * len(pieces)
        + [any_spec()] * 5
        + [vmem_spec()] * 3,
        out_specs=[vmem_spec()] + [any_spec()] * (len(shapes) - 1),
        scratch_shapes=[
            pltpu.VMEM((rows, width), wide),
            pltpu.VMEM((rows, width), wide),
            pltpu.VMEM((rows, width), low),
            pltpu.VMEM((rows, width), wide),
            pltpu.VMEM((rows, 2 * HEAD), wide),
            pltpu.VMEM((BLOCKS, 8, width, width), low),
            pltpu.VMEM((rows, width), low),
            pltpu.VMEM((TILE, hidden), low),
            pltpu.VMEM((rows, hidden // peers), low),
            pltpu.VMEM((rows, hidden), low),
            pltpu.VMEM((slots, length + 2 * PAD, width), wide),
            pltpu.SemaphoreType.DMA((BLOCKS, 8)),
            pltpu.SemaphoreType.DMA((BLOCKS, 8)),
        ],
        compiler_params=pltpu.CompilerParams(vmem_limit_bytes=VMEM_LIMIT),
        name="forward_blocks",
    )(scalars, *pieces, *weights, depth, gain, shift)


def up16(count):
    return -(-count // 16) * 16


def payload_rows(width, groups):
    pitch = up16(width // groups)
    return 0, pitch, pitch + EXTRA


def dense_rows(width, groups, peers):
    pitch = up16(width // groups)
    tail = up16(width // groups // peers)
    return pitch, 2 * pitch, 2 * pitch + tail, 2 * pitch + tail + EXTRA


def norm_back(b, scalars, gain, slot, start, rows, unit, stats, gn, du, small):
    span, width = rows.size, gn.shape[1]
    keep = live_of(scalars, slot, start, span, width)
    g = jnp.where(keep, gn[rows, :], 0.0)
    value = unit[rows, :]
    gu = g * value
    gy = g * gain[b : b + 1, :]
    one = jnp.mean(gy, axis=-1, keepdims=True)
    two = jnp.mean(gu * gain[b : b + 1, :], axis=-1, keepdims=True)
    dz = stats[rows, HEADS : HEADS + 1] * (gy - one - value * two)
    gn[rows, :] = dz
    du[rows, :] = dz.astype(low)
    small[TAPS : TAPS + 1, :] += jnp.sum(gu, axis=0, keepdims=True)
    small[TAPS + 1 : TAPS + 2, :] += jnp.sum(g, axis=0, keepdims=True)


def pair_place(me, d, half):
    key = jnp.bitwise_xor(me, d)
    return 2 * (key % half) + (key < half).astype(jnp.int32)


def norm_kernel(b, slots, length, peers, groups, scalars, *refs):
    first = b == BLOCKS - 1
    pieces = refs[: peers if first else 1]
    refs = refs[len(pieces) :]
    (unit_h, stats_h, act_h, gain, gn_out, du_out, small) = refs[:7]
    half = groups // 2
    outputs = 1 if first else half
    sent = refs[7 : 7 + outputs]
    (gn, du, unit, stats, act, payload, c_sem, p_sem) = refs[7 + outputs :]
    width = gn.shape[1]
    cols = width // groups
    span = length // peers
    op = scalars[slots + 2 + 2 * b]
    place = scalars[slots]
    me = scalars[slots + 1]

    def place_of(d):
        return d if first else pair_place(me, d, half)

    def slot_copies(slot):
        rows = pl.ds(pl.multiple_of(slot * length, length), length)
        pairs = [(unit_h.at[b], unit), (stats_h.at[b], stats)]
        if not first:
            pairs.append((pieces[0], gn))
        return [
            pltpu.make_async_copy(source.at[rows], target.at[rows], c_sem.at[3 * slot + j])
            for j, (source, target) in enumerate(pairs)
        ]

    def act_copy():
        return pltpu.make_async_copy(act_h.at[b], act, c_sem.at[3 * slots])

    for slot in range(slots):
        for copy in slot_copies(slot):
            copy.start()

    @pl.when(op == 2)
    def _():
        act_copy().start()

    small[...] = jnp.zeros(small.shape, wide)
    small[TAPS + 2 : TAPS + 3, :] = jnp.full((1, width), op.astype(wide), wide)

    @pl.loop(0, slots)
    def _(slot):
        for copy in slot_copies(slot):
            copy.wait()

        @pl.loop(0, peers)
        def _(j):
            start = pl.multiple_of(j * span, span)
            rows = pl.ds(pl.multiple_of(slot * length + start, span), span)

            @pl.when(start < scalars[slot])
            def _():
                if first:
                    for key in range(peers):

                        @pl.when(jnp.bitwise_xor(place, key) == j)
                        def _():
                            gn[rows, :] = pieces[key][slot].astype(wide)

                norm_back(b, scalars, gain, slot, start, rows, unit, stats, gn, du, small)

            @pl.when(start >= scalars[slot])
            def _():
                gn[rows, :] = jnp.zeros((span, width), wide)
                du[rows, :] = jnp.zeros((span, width), low)

    saves = [
        pltpu.make_async_copy(gn, gn_out, p_sem.at[half]),
        pltpu.make_async_copy(du, du_out, p_sem.at[half + 1]),
    ]
    for save in saves:
        save.start()

    @pl.when(op == 2)
    def _():
        act_copy().wait()
        values = nn(du[...].T, act[...]).astype(low)
        for d in range(groups):
            payload[place_of(d), 0:cols, :] = values[d * cols : (d + 1) * cols]

    @pl.when(op != 2)
    def _():
        for d in range(groups):
            payload[d] = jnp.zeros(payload.shape[1:], low)

    leaving = [
        pltpu.make_async_copy(
            payload.at[pl.ds(2 * key, 2)],
            sent[0].at[pl.ds(2 * key, 2)] if first else sent[key],
            p_sem.at[key],
        )
        for key in range(half)
    ]
    for copy in leaving:
        copy.start()
    for copy in leaving + saves:
        copy.wait()


def norm_call(b, slots, length, peers, groups, scalars, pieces, kept, gain):
    (_, unit, stats, _, _, act, _) = kept
    rows, width = unit.shape[1:]
    first = b == BLOCKS - 1
    half = groups // 2
    pitch = up16(width // groups)
    shapes = [((rows, width), wide), ((rows, width), low), ((EXTRA, width), wide)]
    shapes += [((groups, pitch, width), low)] if first else [((2, pitch, width), low)] * half
    return pl.pallas_call(
        functools.partial(norm_kernel, b, slots, length, peers, groups),
        out_shape=[jax.ShapeDtypeStruct(*s) for s in shapes],
        in_specs=[pl.BlockSpec(memory_space=pltpu.SMEM)]
        + [vmem_spec() if first else any_spec()] * len(pieces)
        + [any_spec()] * 3
        + [vmem_spec()],
        out_specs=[any_spec(), any_spec(), vmem_spec()] + [any_spec()] * (len(shapes) - 3),
        scratch_shapes=[
            pltpu.VMEM((rows, width), wide),
            pltpu.VMEM((rows, width), low),
            pltpu.VMEM((rows, width), wide),
            pltpu.VMEM((rows, 2 * HEAD), wide),
            pltpu.VMEM((rows, act.shape[2]), low),
            pltpu.VMEM((groups, pitch, width), low),
            pltpu.SemaphoreType.DMA((3 * slots + 1,)),
            pltpu.SemaphoreType.DMA((half + 2,)),
        ],
        compiler_params=pltpu.CompilerParams(vmem_limit_bytes=VMEM_LIMIT),
        name="norm_backward",
    )(scalars, *pieces, unit, stats, act, gain)


def backward_kernel(b, slots, length, peers, groups, first, last, scalars, *refs):
    pieces = refs[:3]
    refs = refs[3:]
    (a_h, _, stats_h, qkv_h, mix_h, _, slope_h) = [ref.at[b] for ref in refs[:7]]
    (proj_h, out_h, fin_h, fout_h, point_h, depth, gain) = refs[7:14]
    g_out = refs[14]
    outputs = 1 if first else groups
    sent = refs[15 : 15 + outputs]
    (payload, gn, du, a_in, stats, w_in, w_out, mix, slope, padded, stats_t, turned, small) = refs[
        15 + outputs : 28 + outputs
    ]
    (w_sem, s_sem, c_sem, p_sem) = refs[28 + outputs :]
    width = a_in.shape[1]
    hidden = w_in.shape[1]
    chunks = hidden // width
    tiles = length // TILE
    own = width // peers
    cols = width // groups
    hidden_cols = hidden // groups
    place = scalars[slots]
    me = scalars[slots + 1]
    op = scalars[slots + 2 + 2 * b]
    span = length // peers
    inner_at, small_at, _ = payload_rows(width, groups)

    def key_of(d):
        return d if first else jnp.bitwise_xor(me, d)

    def part(j):
        return pl.ds(j * width, width)

    def heads(j, pair):
        return pl.ds(pl.multiple_of(j * width + pair * 2 * HEAD, 2 * HEAD), 2 * HEAD)

    def slot_copies(slot):
        rows = pl.ds(pl.multiple_of(slot * length, length), length)
        pairs = [(pieces[0], gn), (pieces[1], du)]
        return [
            pltpu.make_async_copy(source.at[rows], target.at[rows], c_sem.at[2 * slot + j])
            for j, (source, target) in enumerate(pairs)
        ]

    def stats_copy():
        return pltpu.make_async_copy(stats_h, stats, c_sem.at[2 * slots])

    def input_copy():
        return pltpu.make_async_copy(a_h, a_in, c_sem.at[2 * slots + 1])

    def attn_copies():
        return (
            [
                pltpu.make_async_copy(qkv_h.at[j], slope.at[:, part(j)], s_sem.at[j])
                for j in range(3)
            ]
            + [pltpu.make_async_copy(mix_h, mix, s_sem.at[3])]
            + [
                pltpu.make_async_copy(proj_h.at[b, j], w_out.at[part(j)], w_sem.at[j])
                for j in range(3)
            ]
            + [pltpu.make_async_copy(out_h.at[b], w_out.at[part(3)], w_sem.at[3])]
        )

    def conv_copies():
        return [
            pltpu.make_async_copy(mix_h, mix, s_sem.at[0]),
            pltpu.make_async_copy(point_h.at[b], w_out.at[part(0)], w_sem.at[0]),
        ]

    def ffn_copies():
        return [
            pltpu.make_async_copy(fout_h.at[b], w_out, w_sem.at[0]),
            pltpu.make_async_copy(slope_h, slope, s_sem.at[0]),
            pltpu.make_async_copy(fin_h.at[b], w_in, w_sem.at[1]),
        ]

    stats_copy().start()
    for slot in range(slots):
        for copy in slot_copies(slot):
            copy.start()
    for index, copies in enumerate((attn_copies, conv_copies, ffn_copies)):

        @pl.when(op == index)
        def _():
            for copy in copies():
                copy.start()

    input_copy().start()

    def each_tile(body, rest):
        tiles_of(scalars, slots, length, body, rest)

    stats_copy().wait()
    small[...] = pieces[2][...]
    for slot in range(slots):
        for copy in slot_copies(slot):
            copy.wait()
    input_copy().wait()

    def turn_own(source):
        for s in range(peers):

            @pl.when(place == s)
            def _():
                turned[...] = source[:, s * own : (s + 1) * own].T

    def put_out(start, values):
        for d in range(groups):
            piece = values[d * cols : (d + 1) * cols].astype(low)
            payload[key_of(d), 0:cols, start : start + values.shape[1]] = piece

    def put_point(values):
        count = cols // peers
        for d in range(groups):
            for p in range(peers):
                piece = values[d * cols + p * count : d * cols + (p + 1) * count].astype(low)
                payload[key_of(d), 0:count, p * own : (p + 1) * own] = piece

    def put_in(d, values):
        for p in range(own // cols):
            at = slice(p * hidden_cols, (p + 1) * hidden_cols)
            payload[key_of(d), inner_at : inner_at + cols, at] = values[p * cols : (p + 1) * cols]

    def add_back(grad):
        if last:
            @pl.loop(0, slots)
            def _(slot):
                rows = pl.ds(pl.multiple_of(slot * length + place * span, span), span)
                keep = live_of(scalars, slot, place * span, span, width)

                @pl.when(place * span < scalars[slot])
                def _():
                    g_out[slot] = jnp.where(keep, gn[rows, :] + grad(rows), 0.0)

                @pl.when(place * span >= scalars[slot])
                def _():
                    g_out[slot] = jnp.zeros((span, width), wide)

        else:

            def add(slot, start, rows):
                g_out[rows, :] = gn[rows, :] + grad(rows)

            each_tile(add, None)

    @pl.when(op == 0)
    def _():
        copies = attn_copies()
        copies[7].wait()
        for copy in copies[:4]:
            copy.wait()
        turn_own(mix)
        put_out(3 * own, nn(turned[...], du[...]).T)

        def back(slot, start, rows):
            mix[rows, :] = nt(du[rows, :], w_out[part(3), :]).astype(low)

        def clear(rows):
            for j in range(3):
                slope[rows, part(j)] = jnp.zeros((TILE, width), low)

        each_tile(back, clear)

        @pl.loop(0, slots)
        def _(slot):
            stats_t[slot] = stats[pl.ds(pl.multiple_of(slot * length, length), length), :].T

        def attend(slot, reach):
            every = pl.ds(pl.multiple_of(slot * length, length), reach)
            upper = lax.broadcasted_iota(jnp.int32, (2 * HEAD, reach), 0) < HEAD

            @pl.loop(0, HEADS // 2)
            def _(pair):
                keys = slope[every, heads(1, pair)]
                values = slope[every, heads(2, pair)]
                scaled = keys * FACTOR
                queries = split_heads(slope[every, heads(0, pair)] * FACTOR)
                grads = split_heads(mix[every, heads(0, pair)])
                scores = [nt(keys, one) for one in queries]
                products = [nt(values, one) for one in grads]
                dk = jnp.zeros((reach, 2 * HEAD), wide)
                dv = jnp.zeros((reach, 2 * HEAD), wide)
                dq = []
                for head in range(2):
                    stat = stats_t[slot, pl.ds(pair * 2 + head, 1), 0:reach]
                    soft = jnp.exp(jnp.minimum(scores[head] - stat, 0.0))
                    product = soft * products[head]
                    inner = jnp.sum(product, axis=0, keepdims=True)
                    grad_scores = (product - soft * inner).astype(low)
                    dq.append(tn(scaled, grad_scores))
                    dk = dk + nn(grad_scores, queries[head])
                    dv = dv + nn(soft.astype(low), grads[head])
                dq = jnp.where(upper, dq[0], dq[1])
                slope[every, heads(0, pair)] = dq.T.astype(low)
                slope[every, heads(1, pair)] = dk.astype(low)
                slope[every, heads(2, pair)] = dv.astype(low)

        for_reach(scalars, slots, length, attend)
        for j in range(3):
            copies[4 + j].wait()
        turn_own(a_in)

        for j in range(3):
            put_out(j * own, nn(turned[...], slope[:, part(j)]).T)

        def grad(rows):
            total = nt(slope[rows, part(0)], w_out[part(0), :])
            for j in range(1, 3):
                total = total + nt(slope[rows, part(j)], w_out[part(j), :])
            return total

        add_back(grad)

    @pl.when(op == 1)
    def _():
        copies = conv_copies()
        for copy in copies:
            copy.wait()
        turn_own(mix)
        put_point(nn(turned[...], du[...]).T)

        def back(slot, start, rows):
            mix[rows, :] = nt(du[rows, :], w_out[part(0), :]).astype(low)

        def clear(rows):
            mix[rows, :] = jnp.zeros((TILE, width), low)

        each_tile(back, clear)
        fill_padded(padded, a_in, slots, length)

        def depth_terms(slot, start, rows):
            near = window(padded, slot, start)
            grads = mix[rows, :].astype(wide)
            for offset in range(TAPS):
                at = PAD + offset - TAPS // 2
                term = jnp.sum(near[at : at + TILE] * grads, axis=0, keepdims=True)
                small[offset : offset + 1, :] += term * used_tap(scalars, slots, b, offset)

        each_tile(depth_terms, None)
        fill_padded(padded, mix, slots, length)

        def spread(slot, start, rows):
            near = window(padded, slot, start)
            running = gn[rows, :]
            for offset in range(TAPS):
                at = PAD - offset + TAPS // 2
                tap = depth[offset, b : b + 1, :] * used_tap(scalars, slots, b, offset)
                running = running + near[at : at + TILE] * tap
            gn[rows, :] = running

        each_tile(spread, None)
        add_back(lambda rows: 0.0)

    @pl.when(op == 2)
    def _():
        copies = ffn_copies()
        copies[0].wait()
        copies[1].wait()

        def back(slot, start, rows):
            upstream = du[rows, :]
            for j in range(chunks):
                df = nt(upstream, w_out[part(j), :]).astype(low).astype(wide)
                slope[rows, part(j)] = (df * slope[rows, part(j)].astype(wide)).astype(low)

        def clear(rows):
            slope[rows, :] = jnp.zeros((TILE, hidden), low)

        each_tile(back, clear)
        copies[2].wait()
        turn_own(a_in)
        for d in range(groups):
            piece = slope[:, d * hidden_cols : (d + 1) * hidden_cols]
            put_in(d, nn(turned[...], piece).astype(low))
        add_back(lambda rows: nt(slope[rows, :], w_in[...]))

    for d in range(groups):
        payload[d, small_at : small_at + EXTRA, :] = small[...].astype(low)
    order = sorted(range(groups), key=lambda key: key < groups // 2)
    leaving = [
        pltpu.make_async_copy(
            payload.at[key], sent[0].at[key] if first else sent[key], p_sem.at[key]
        )
        for key in order
    ]
    for copy in leaving:
        copy.start()
    for copy in leaving:
        copy.wait()


def backward_call(b, slots, length, peers, groups, scalars, pieces, kept, weights, depth, gain):
    width = gain.shape[-1]
    hidden = weights[2].shape[2]
    rows = slots * length
    first = b == BLOCKS - 1
    last = b == 0
    count = payload_rows(width, groups)[2]
    shapes = [
        ((slots, length // peers, width) if last else (rows, width), wide),
    ] + ([((groups, count, width), low)] if first else [((count, width), low)] * groups)
    return pl.pallas_call(
        functools.partial(backward_kernel, b, slots, length, peers, groups, first, last),
        out_shape=[jax.ShapeDtypeStruct(*s) for s in shapes],
        in_specs=[pl.BlockSpec(memory_space=pltpu.SMEM)]
        + [any_spec(), any_spec(), vmem_spec()]
        + [any_spec()] * 12
        + [vmem_spec()] * 2,
        out_specs=[vmem_spec()] + [any_spec()] * (len(shapes) - 1),
        scratch_shapes=[
            pltpu.VMEM((groups, count, width), low),
            pltpu.VMEM((rows, width), wide),
            pltpu.VMEM((rows, width), low),
            pltpu.VMEM((rows, width), low),
            pltpu.VMEM((rows, 2 * HEAD), wide),
            pltpu.VMEM((width, hidden), low),
            pltpu.VMEM((hidden, width), low),
            pltpu.VMEM((rows, width), low),
            pltpu.VMEM((rows, hidden), low),
            pltpu.VMEM((slots, length + 2 * PAD, width), wide),
            pltpu.VMEM((slots, 2 * HEAD, length), wide),
            pltpu.VMEM((width // peers, rows), low),
            pltpu.VMEM((EXTRA, width), wide),
            pltpu.SemaphoreType.DMA((4,)),
            pltpu.SemaphoreType.DMA((4,)),
            pltpu.SemaphoreType.DMA((2 * slots + 2,)),
            pltpu.SemaphoreType.DMA((groups,)),
        ],
        compiler_params=pltpu.CompilerParams(vmem_limit_bytes=VMEM_LIMIT),
        name="backward_block",
    )(scalars, *pieces, *kept, *weights, depth, gain)


def add_pieces(pieces, small, groups, peers):
    width = small.shape[2]
    cols = width // groups
    inner_at, small_at, _ = payload_rows(width, groups)
    sums = [None] * 4

    def add(index, value):
        sums[index] = value if sums[index] is None else sums[index] + value

    for at, piece in pieces:
        terms = piece[small_at : small_at + EXTRA, :].astype(wide)
        op = terms[TAPS + 2 : TAPS + 3, :]
        matrix = piece[0:cols, :].astype(wide)
        add(0, jnp.where(op == 0.0, matrix, 0.0))
        inner = piece[inner_at : inner_at + cols, :].astype(wide)
        add(2, jnp.where(op == 2.0, inner, 0.0))
        add(3, jnp.where(op == 1.0, piece[0 : cols // peers, :].astype(wide), 0.0))
        row = lax.broadcasted_iota(jnp.int32, terms.shape, 0)
        terms = jnp.where((row < TAPS) & (op != 1.0), 0.0, terms)
        for index in range(3):
            terms = jnp.where(row == TAPS + 2 + index, (op == index).astype(wide), terms)
        terms = jnp.where(row < TAPS + 5, terms, 0.0)
        small[at] = terms
    total = small[0]
    for index in range(1, len(pieces)):
        total = total + small[index]
    return sums, total


def placed(pieces, me):
    return [(jnp.bitwise_xor(me, key) % len(pieces), piece) for key, piece in enumerate(pieces)]


def early_kernel(index, *refs):
    pieces, total = refs[:-1], refs[-1]
    value = pieces[0][index].astype(wide)
    for piece in pieces[1:]:
        value = value + piece[index].astype(wide)
    total[...] = value.astype(low)


def early_call(pieces):
    return pl.pallas_call(
        functools.partial(early_kernel, 0),
        out_shape=jax.ShapeDtypeStruct(pieces[0].shape[1:], low),
        in_specs=[vmem_spec()] * len(pieces),
        out_specs=vmem_spec(),
        compiler_params=pltpu.CompilerParams(vmem_limit_bytes=VMEM_LIMIT),
        name="early_sum",
    )(*pieces)


def relay_kernel(groups, peers, slots, scalars, *refs):
    pieces, (dense, small) = refs[:-2], refs[-2:]
    width = dense.shape[1]
    cols = width // groups
    inner_at, point_at, small_at, _ = dense_rows(width, groups, peers)
    sums, total = add_pieces(placed(pieces, scalars[slots + 1]), small, groups, peers)
    dense[0:cols, :] = sums[0].astype(low)
    dense[inner_at : inner_at + cols, :] = sums[2].astype(low)
    dense[point_at : point_at + cols // peers, :] = sums[3].astype(low)
    dense[small_at : small_at + EXTRA, :] = total.astype(low)


def relay_call(groups, peers, slots, scalars, pieces):
    width = pieces[0].shape[1]
    count = dense_rows(width, groups, peers)[3]
    return pl.pallas_call(
        functools.partial(relay_kernel, groups, peers, slots),
        out_shape=jax.ShapeDtypeStruct((count, width), low),
        in_specs=[pl.BlockSpec(memory_space=pltpu.SMEM)] + [vmem_spec()] * len(pieces),
        out_specs=vmem_spec(),
        scratch_shapes=[pltpu.VMEM((len(pieces), EXTRA, width), wide)],
        compiler_params=pltpu.CompilerParams(vmem_limit_bytes=VMEM_LIMIT),
        name="relay_sum",
    )(scalars, *pieces)


def final_kernel(groups, peers, slots, scalars, *refs):
    half = groups // 2
    near, early = refs[:half], refs[half : 2 * half]
    (early_dense, dense, early_every, every) = refs[2 * half : 2 * half + 4]
    (proj, out, f_in, f_out, point, depth, gain, shift, small) = refs[2 * half + 4 :]
    width = dense.shape[1]
    cols = width // groups
    own = width // peers
    hidden_cols = f_in.shape[2]
    inner_at, point_at, small_at, _ = dense_rows(width, groups, peers)
    for b in range(BLOCKS):
        if b:
            pieces = [(d, every.at[d]) for d in range(groups)]
        else:
            pieces = placed(near, scalars[slots + 1])
        sums, total = add_pieces(pieces, small, groups, peers)
        points = sums[3]
        if b:
            sums[1] = early_every[0, 0:cols, :].astype(wide)
            for d in range(1, groups):
                sums[1] = sums[1] + early_every[d, 0:cols, :].astype(wide)
        else:
            total = total.astype(low).astype(wide)
            total = total + dense[small_at : small_at + EXTRA, :].astype(wide)
            sums[0] = sums[0] + dense[0:cols, :].astype(wide)
            sums[1] = early_dense[0:cols, :].astype(wide)
            for piece in early:
                sums[1] = sums[1] + piece[1, 0:cols, :].astype(wide)
            sums[2] = sums[2] + dense[inner_at : inner_at + cols, :].astype(wide)
            points = points + dense[point_at : point_at + cols // peers, :].astype(wide)
        share = [1.0 / total[TAPS + 2 + op : TAPS + 3 + op, :] for op in range(3)]
        attn = sums[0] * share[0]
        for j in range(3):
            proj[b, j] = attn[:, j * own : (j + 1) * own].T
        out[b] = attn[:, 3 * own :].T
        f_out[b] = sums[1] * share[2]
        inner = sums[2] * share[2]
        for p in range(own // cols):
            f_in[b, p * cols : (p + 1) * cols, :] = inner[:, p * hidden_cols : (p + 1) * hidden_cols]
        points = points * share[1]
        points = jnp.concatenate([points[:, p * own : (p + 1) * own] for p in range(peers)], axis=0)
        point[b] = points.T
        depth[:, b, :] = total[0:TAPS] * share[1]
        gain[b : b + 1, :] = total[TAPS : TAPS + 1] * (1.0 / groups)
        shift[b : b + 1, :] = total[TAPS + 1 : TAPS + 2] * (1.0 / groups)


def final_call(groups, peers, slots, hidden, scalars, inputs):
    width = inputs[0].shape[-1]
    rows, cols = width // peers, width // groups
    shapes = [
        (BLOCKS, 3, rows, cols),
        (BLOCKS, rows, cols),
        (BLOCKS, rows, hidden // groups),
        (BLOCKS, cols, hidden // peers),
        (BLOCKS, rows, cols),
        (TAPS, BLOCKS, width),
        (BLOCKS, width),
        (BLOCKS, width),
    ]
    return pl.pallas_call(
        functools.partial(final_kernel, groups, peers, slots),
        out_shape=[jax.ShapeDtypeStruct(s, wide) for s in shapes],
        in_specs=[pl.BlockSpec(memory_space=pltpu.SMEM)] + [vmem_spec()] * len(inputs),
        out_specs=[vmem_spec()] * len(shapes),
        scratch_shapes=[pltpu.VMEM((groups, EXTRA, width), wide)],
        compiler_params=pltpu.CompilerParams(vmem_limit_bytes=VMEM_LIMIT),
        name="final_sum",
    )(scalars, *inputs)


def across(piece, axis, key):
    return lax.ppermute(piece, axis, [(i, i ^ key) for i in range(lax.axis_size(axis))])


def local(
    layer_in,
    lengths,
    op_ids,
    kernel_ids,
    attn_proj,
    attn_out,
    ffn_in,
    ffn_out,
    point_weights,
    depth_weights,
    norm_gains,
    norm_shifts,
    cotangent,
):
    slots, span, width = layer_in.shape
    peers = lax.axis_size("seq")
    groups = lax.axis_size("dp")
    place = lax.axis_index("seq").astype(jnp.int32)
    length = span * peers
    weights = (attn_proj, attn_out, ffn_in, ffn_out, point_weights)

    me = lax.axis_index("dp").astype(jnp.int32)
    half = groups // 2

    chosen = jnp.stack([op_ids[0], kernel_ids[0]], axis=1).reshape(-1)
    scalars = jnp.concatenate([lengths, jnp.stack([place, me]), chosen])
    depth_weights = jnp.swapaxes(depth_weights, 0, 1)

    later = cotangent.astype(low)
    parts = {0: layer_in.astype(low)}
    reach = peers // 2
    while reach:
        moved = {key ^ reach: across(part, "seq", reach) for key, part in parts.items()}
        if reach == peers // 2:
            moved, later, scalars = lax.optimization_barrier((moved, later, scalars))
        parts.update(moved)
        reach //= 2
    x_parts = [parts[key] for key in range(peers)]
    later, x_parts = lax.optimization_barrier((later, x_parts))
    cot_parts = [later] + [across(later, "seq", key) for key in range(1, peers)]
    layer_out, *saved = forward_call(
        slots, length, peers, scalars, x_parts, weights, depth_weights, norm_gains, norm_shifts
    )

    *state, early_payload = norm_call(
        1, slots, length, peers, groups, scalars, cot_parts, saved, norm_gains
    )
    early_every = lax.all_to_all(early_payload, "dp", 0, 0, tiled=True)
    g, payload = backward_call(
        1, slots, length, peers, groups, scalars, state, saved, weights, depth_weights, norm_gains
    )
    early_every, payload = lax.optimization_barrier((early_every, payload))
    every = lax.all_to_all(payload, "dp", 0, 0, tiled=True)
    grad, rounded, small, *early = norm_call(
        0, slots, length, peers, groups, scalars, [g], saved, norm_gains
    )
    early = [early[0]] + [across(early[key], "dp", key) for key in range(1, half)]
    g, *sent = backward_call(
        0, slots, length, peers, groups, scalars, [grad, rounded, small], saved, weights,
        depth_weights, norm_gains,
    )
    early, g = lax.optimization_barrier((early, g))
    early_sum = early_call(early)
    early_dense = across(early_sum, "dp", half)
    far = [sent[half]] + [across(sent[half + key], "dp", key) for key in range(1, half)]
    far, _ = lax.optimization_barrier((far, early_sum))
    partial = relay_call(groups, peers, slots, scalars, far)
    rest, partial = lax.optimization_barrier((sent[:half], partial))
    dense = across(partial, "dp", half)
    near = [rest[0]] + [across(rest[key], "dp", key) for key in range(1, half)]
    proj, out, f_in, f_out, point, depth, gain, shift = final_call(
        groups, peers, slots, ffn_in.shape[2], scalars, near + early + [early_dense, dense, early_every, every]
    )
    f_out = jnp.swapaxes(f_out, 1, 2)
    depth = jnp.swapaxes(depth, 0, 1)
    return (layer_out, g, proj, out, f_in, f_out, point, depth, gain, shift)


def solution(mesh):
    placed = (
        P("dp", "seq", None),
        P("dp"),
        P("dp", None),
        P("dp", None),
        P(),
        P(),
        P(),
        P(),
        P(),
        P(),
        P(),
        P(),
        P("dp", "seq", None),
    )
    return jax.shard_map(
        local,
        mesh=mesh,
        in_specs=placed,
        out_specs=(
            P("dp", "seq", None),
            P("dp", "seq", None),
            P(None, None, "seq", "dp"),
            P(None, "seq", "dp"),
            P(None, "seq", "dp"),
            P(None, "seq", "dp"),
            P(None, "seq", "dp"),
            P(),
            P(),
            P(),
        ),
        check_vma=False,
    )
```

```python
import functools

import jax
import jax.numpy as jnp
from jax import lax
from jax.experimental import pallas as pl
from jax.experimental.pallas import tpu as pltpu
from jax.sharding import PartitionSpec as P

HEADS = 12
HEAD = 64
TAPS = 7
BLOCKS = 2
EXTRA = 16
PAD = 8
norm_eps = 1e-05
low = jnp.bfloat16
wide = jnp.float32
VMEM_LIMIT = 60 * 1024 * 1024


def nn(left, right):
    return lax.dot_general(left, right, (((1,), (0,)), ((), ())), preferred_element_type=wide)


def nt(left, right):
    return lax.dot_general(left, right, (((1,), (1,)), ((), ())), preferred_element_type=wide)


def tn(left, right):
    return lax.dot_general(left, right, (((0,), (0,)), ((), ())), preferred_element_type=wide)


def live_of(scalars, slot, start, count, width):
    at = lax.broadcasted_iota(jnp.int32, (count, width), 0) + start
    return at < scalars[slot]


def used_tap(scalars, slots, b, offset):
    return (abs(offset - TAPS // 2) <= scalars[slots + 3 + 2 * b] + 1).astype(wide)


def live_tiles(scalars, slot, size):
    return (scalars[slot] + size - 1) // size


def for_reach(scalars, slots, length, body):
    @pl.loop(0, slots)
    def _(slot):
        @pl.when(scalars[slot] <= length // 2)
        def _():
            body(slot, length // 2)

        @pl.when(scalars[slot] > length // 2)
        def _():
            body(slot, length)


def tiles_of(scalars, slots, length, body, rest):
    @pl.loop(0, slots)
    def _(slot):
        count = live_tiles(scalars, slot, TILE)

        @pl.loop(0, count)
        def _(t):
            start = pl.multiple_of(t * TILE, TILE)
            body(slot, start, pl.ds(pl.multiple_of(slot * length + start, TILE), TILE))

        if rest is not None:

            @pl.loop(count, length // TILE)
            def _(t):
                rest(pl.ds(pl.multiple_of(slot * length + t * TILE, TILE), TILE))


def fill_padded(padded, source, slots, length):
    width = padded.shape[2]

    @pl.loop(0, slots)
    def _(slot):
        padded[slot, 0:PAD, :] = jnp.zeros((PAD, width), wide)
        padded[slot, PAD + length : PAD + length + PAD, :] = jnp.zeros((PAD, width), wide)

        @pl.loop(0, length // 128)
        def _(t):
            rows = pl.ds(pl.multiple_of(slot * length + t * 128, 128), 128)
            at = pl.ds(pl.multiple_of(PAD + t * 128, PAD), 128)
            padded[slot, at, :] = source[rows, :].astype(wide)


def window(padded, slot, start):
    return padded[slot, pl.ds(pl.multiple_of(start, TILE), TILE + 2 * PAD), :]


TILE = 256
INNER = 16
FACTOR = HEAD**-0.5


def split_heads(tensor):
    lane = lax.broadcasted_iota(jnp.int32, tensor.shape, 1)
    none = jnp.zeros((), tensor.dtype)
    return [jnp.where(lane < HEAD, tensor, none), jnp.where(lane < HEAD, none, tensor)]


def pair_rows(tensor):
    return jnp.concatenate(split_heads(tensor), axis=0)


def forward_kernel(slots, length, peers, lengths_of, *refs):
    pieces = refs[:peers]
    (proj_h, out_h, fin_h, fout_h, point_h, depth, gain, shift) = refs[peers : peers + 8]
    refs = refs[peers + 8 :]
    layer_out = refs[0]
    saved = refs[1:8]
    (x_now, update, a_now, unit, stats, weights, mix, active, mine_active, slope, padded) = refs[8:19]
    w_sem, s_sem = refs[19:]
    scalars = lengths_of
    width = a_now.shape[1]
    hidden = slope.shape[1]
    share = mine_active.shape[1]
    span = length // peers
    chunks = hidden // width
    tiles = length // TILE
    place = scalars[slots]

    def part(j):
        return pl.ds(pl.multiple_of(j * width, width), width)

    def heads(j, pair):
        return pl.ds(pl.multiple_of(j * width + pair * 2 * HEAD, 2 * HEAD), 2 * HEAD)

    def op_of(b):
        return scalars[slots + 2 + 2 * b]

    def loads(b, op):
        w = weights.at[b]
        if op == 0:
            pairs = [(proj_h.at[b, j], j) for j in range(3)] + [(out_h.at[b], 3)]
        elif op == 1:
            pairs = [(point_h.at[b], 0)]
        else:
            pairs = [(fin_h.at[b, :, part(j)], j) for j in range(chunks)]
            pairs += [(fout_h.at[b, part(j)], chunks + j) for j in range(chunks)]
        return [pltpu.make_async_copy(source, w.at[j], w_sem.at[b, j]) for source, j in pairs]

    def saves(b, op):
        (a_h, unit_h, stats_h, qkv_h, mix_h, act_h, slope_h) = [ref.at[b] for ref in saved]
        if op == 0:
            pairs = [(slope.at[:, part(j)], qkv_h.at[j]) for j in range(3)] + [(mix, mix_h)]
        elif op == 1:
            pairs = [(mix, mix_h)]
        else:
            pairs = [(mine_active, act_h), (slope, slope_h)]
        return [
            pltpu.make_async_copy(source, target, s_sem.at[b, j])
            for j, (source, target) in enumerate(pairs)
        ]

    def common_saves(b):
        (a_h, unit_h, stats_h) = [ref.at[b] for ref in saved[:3]]
        pairs = [(a_now, a_h), (unit, unit_h), (stats, stats_h)]
        return [
            pltpu.make_async_copy(source, target, s_sem.at[b, 4 + j])
            for j, (source, target) in enumerate(pairs)
        ]

    def by_op(b, action):
        for op in range(3):

            @pl.when(op_of(b) == op)
            def _():
                action(op)

    def each_tile(body, rest):
        tiles_of(scalars, slots, length, body, rest)

    for b in range(BLOCKS):

        def start_all(op):
            for copy in loads(b, op):
                copy.start()

        by_op(b, start_all)

    for key, piece in enumerate(pieces):
        origin = jnp.bitwise_xor(place, key) * span

        @pl.loop(0, slots)
        def _(slot):
            rows = pl.ds(pl.multiple_of(slot * length + origin, span), span)
            keep = live_of(scalars, slot, origin, span, width)
            value = jnp.where(keep, piece[slot].astype(wide), 0.0)
            x_now[rows, :] = value
            a_now[rows, :] = value.astype(low)

    def attention(b):
        w = weights.at[b]

        @pl.loop(0, 3)
        def _(j):
            pltpu.make_async_copy(proj_h.at[b, j], w.at[j], w_sem.at[b, j]).wait()

            def project(slot, start, rows):
                slope[rows, part(j)] = nn(a_now[rows, :], w[j]).astype(low)

            def clear(rows):
                slope[rows, part(j)] = jnp.zeros((TILE, width), low)

            each_tile(project, clear)
            pltpu.make_async_copy(slope.at[:, part(j)], saved[3].at[b, j], s_sem.at[b, j]).start()

        def clear_mix(rows):
            mix[rows, :] = jnp.zeros((TILE, width), low)

        each_tile(lambda slot, start, rows: None, clear_mix)

        def attend(slot, reach):
            base = pl.multiple_of(slot * length, length)
            key_at = lax.broadcasted_iota(jnp.int32, (1, reach), 1)
            bias = jnp.where(key_at < scalars[slot], 0.0, -1000000000.0).astype(wide)
            lane = lax.broadcasted_iota(jnp.int32, (TILE, 2 * HEAD), 1)

            @pl.loop(0, HEADS // 2, unroll=3)
            def _(pair):
                keys = slope[pl.ds(base, reach), heads(1, pair)]
                values = slope[pl.ds(base, reach), heads(2, pair)]
                for t in range(reach // TILE):
                    rows = pl.ds(pl.multiple_of(base + t * TILE, TILE), TILE)
                    scores = nt(pair_rows(slope[rows, heads(0, pair)] * FACTOR), keys) + bias
                    top = jnp.max(scores, axis=-1, keepdims=True)
                    exponent = jnp.exp(scores - top)
                    total = jnp.sum(exponent, axis=-1, keepdims=True)
                    mixed = nn(exponent.astype(low), values) * (1.0 / total)
                    stat = top + jnp.log(total)
                    kept = jnp.where(lane == pair * 2, stat[:TILE], stats[rows, :])
                    stats[rows, :] = jnp.where(lane == pair * 2 + 1, stat[TILE:], kept)
                    both = jnp.where(lane < HEAD, mixed[:TILE], mixed[TILE:])
                    mix[rows, heads(0, pair)] = both.astype(low)

        for_reach(scalars, slots, length, attend)
        saves(b, 0)[3].start()
        loads(b, 0)[3].wait()

        def out(slot, start, rows):
            update[rows, :] = nn(mix[rows, :], w[3])

        each_tile(out, None)

    def convolution(b):
        fill_padded(padded, a_now, slots, length)
        loads(b, 1)[0].wait()

        def run(slot, start, rows):
            near = window(padded, slot, start)
            running = jnp.zeros((TILE, width), wide)
            for offset in range(TAPS):
                at = PAD + offset - TAPS // 2
                tap = depth[offset, pl.ds(b, 1), :] * used_tap(scalars, slots, b, offset)
                running = running + near[at : at + TILE] * tap
            mix[rows, :] = running.astype(low)
            update[rows, :] = nn(running.astype(low), weights[b, 0])

        def clear(rows):
            mix[rows, :] = jnp.zeros((TILE, width), low)

        each_tile(run, clear)
        saves(b, 1)[0].start()

    def feed_forward(b):
        w = weights.at[b]
        mine = pl.ds(pl.multiple_of(place * share, 128), share)

        for copy in loads(b, 2):
            copy.wait()

        def run(slot, start, rows):
            update[rows, :] = jnp.zeros((TILE, width), wide)

            @pl.loop(0, chunks, unroll=4)
            def _(j):
                h = nn(a_now[rows, :], w[j])
                cdf = 0.5 * (1.0 + lax.erf(h * (0.5**0.5)))
                density = jnp.exp(-0.5 * h * h) * 0.3989422804014327
                value = (h * cdf).astype(low)
                active[:, part(j)] = value
                slope[rows, part(j)] = (cdf + h * density).astype(low)
                update[rows, :] += nn(value, w[chunks + j])

            mine_active[rows, :] = active[:, mine]

        def clear(rows):
            mine_active[rows, :] = jnp.zeros((TILE, share), low)

        each_tile(run, clear)
        for save in saves(b, 2):
            save.start()

    @pl.loop(0, BLOCKS)
    def _(b):
        common_saves(b)[0].start()

        @pl.when(b > 0)
        def _():
            def wait_saves(op):
                for save in saves(b - 1, op):
                    save.wait()

            by_op(b - 1, wait_saves)
            for save in common_saves(b - 1)[1:]:
                save.wait()

        for op, branch in enumerate((attention, convolution, feed_forward)):

            @pl.when(op_of(b) == op)
            def _():
                branch(b)

        common_saves(b)[0].wait()

        def norm(slot, start, rows):
            z = x_now[rows, :] + update[rows, :]
            center = z - jnp.mean(z, axis=-1, keepdims=True)
            scale = lax.rsqrt(jnp.mean(center * center, axis=-1, keepdims=True) + norm_eps)
            value = center * scale
            unit[rows, :] = value.astype(low)
            lane = lax.broadcasted_iota(jnp.int32, (TILE, 2 * HEAD), 1)
            stats[rows, :] = jnp.where(lane == HEADS, scale, stats[rows, :])
            keep = live_of(scalars, slot, start, TILE, width)
            value = jnp.where(keep, value * gain[pl.ds(b, 1), :] + shift[pl.ds(b, 1), :], 0.0)
            x_now[rows, :] = value
            a_now[rows, :] = value.astype(low)

        def clear(rows):
            x_now[rows, :] = jnp.zeros((TILE, width), wide)
            a_now[rows, :] = jnp.zeros((TILE, width), low)

        each_tile(norm, clear)
        for save in common_saves(b)[1:]:
            save.start()

    for slot in range(slots):
        rows = pl.ds(pl.multiple_of(slot * length + place * span, span), span)
        layer_out[slot] = x_now[rows, :]

    def wait_last(op):
        for save in saves(BLOCKS - 1, op):
            save.wait()

    by_op(BLOCKS - 1, wait_last)
    for save in common_saves(BLOCKS - 1)[1:]:
        save.wait()


def any_spec():
    return pl.BlockSpec(memory_space=pl.ANY)


def vmem_spec():
    return pl.BlockSpec(memory_space=pltpu.VMEM)


def forward_call(slots, length, peers, scalars, pieces, weights, depth, gain, shift):
    width = gain.shape[-1]
    hidden = weights[2].shape[2]
    rows = slots * length
    shapes = [((slots, length // peers, width), wide)]
    shapes += [
        ((BLOCKS, rows, width), low),
        ((BLOCKS, rows, width), low),
        ((BLOCKS, rows, 2 * HEAD), wide),
        ((BLOCKS, 3, rows, width), low),
        ((BLOCKS, rows, width), low),
        ((BLOCKS, rows, hidden // peers), low),
        ((BLOCKS, rows, hidden), low),
    ]
    return pl.pallas_call(
        functools.partial(forward_kernel, slots, length, peers),
        out_shape=[jax.ShapeDtypeStruct(*s) for s in shapes],
        in_specs=[pl.BlockSpec(memory_space=pltpu.SMEM)]
        + [vmem_spec()] * len(pieces)
        + [any_spec()] * 5
        + [vmem_spec()] * 3,
        out_specs=[vmem_spec()] + [any_spec()] * (len(shapes) - 1),
        scratch_shapes=[
            pltpu.VMEM((rows, width), wide),
            pltpu.VMEM((rows, width), wide),
            pltpu.VMEM((rows, width), low),
            pltpu.VMEM((rows, width), low),
            pltpu.VMEM((rows, 2 * HEAD), wide),
            pltpu.VMEM((BLOCKS, 8, width, width), low),
            pltpu.VMEM((rows, width), low),
            pltpu.VMEM((TILE, hidden), low),
            pltpu.VMEM((rows, hidden // peers), low),
            pltpu.VMEM((rows, hidden), low),
            pltpu.VMEM((slots, length + 2 * PAD, width), wide),
            pltpu.SemaphoreType.DMA((BLOCKS, 8)),
            pltpu.SemaphoreType.DMA((BLOCKS, 8)),
        ],
        compiler_params=pltpu.CompilerParams(vmem_limit_bytes=VMEM_LIMIT),
        name="forward_blocks",
    )(scalars, *pieces, *weights, depth, gain, shift)


def up16(count):
    return -(-count // 16) * 16


def payload_rows(width, groups, split):
    pitch = up16(width // groups)
    inner = 0 if split else pitch
    return inner, inner + pitch, inner + pitch + EXTRA


def dense_rows(width, groups, peers):
    pitch = up16(width // groups)
    tail = up16(width // groups // peers)
    return pitch, 2 * pitch, 2 * pitch + tail, 2 * pitch + tail + EXTRA


def norm_back(b, scalars, gain, slot, start, rows, unit, stats, gn, du, small):
    span, width = rows.size, gn.shape[1]
    keep = live_of(scalars, slot, start, span, width)
    g = jnp.where(keep, gn[rows, :], 0.0)
    value = unit[rows, :].astype(wide)
    gu = g * value
    gy = g * gain[b : b + 1, :]
    one = jnp.mean(gy, axis=-1, keepdims=True)
    two = jnp.mean(gu * gain[b : b + 1, :], axis=-1, keepdims=True)
    dz = stats[rows, HEADS : HEADS + 1] * (gy - one - value * two)
    gn[rows, :] = dz
    du[rows, :] = dz.astype(low)
    small[TAPS : TAPS + 1, :] += jnp.sum(gu, axis=0, keepdims=True)
    small[TAPS + 1 : TAPS + 2, :] += jnp.sum(g, axis=0, keepdims=True)


def pair_place(me, d, half):
    key = jnp.bitwise_xor(me, d)
    return 2 * (key % half) + (key < half).astype(jnp.int32)


def norm_kernel(slots, length, peers, groups, scalars, g_h, unit_h, stats_h, act_h, gain, *refs):
    (gn_out, du_out, small) = refs[:3]
    half = groups // 2
    sent = refs[3 : 3 + half]
    (gn, du, unit, stats, act, payload, c_sem, p_sem) = refs[3 + half :]
    b = 0
    width = gn.shape[1]
    cols = width // groups
    span = length // peers
    op = scalars[slots + 2]
    me = scalars[slots + 1]

    def slot_copies(slot):
        rows = pl.ds(pl.multiple_of(slot * length, length), length)
        pairs = [(g_h, gn), (unit_h.at[b], unit), (stats_h.at[b], stats)]
        return [
            pltpu.make_async_copy(source.at[rows], target.at[rows], c_sem.at[3 * slot + j])
            for j, (source, target) in enumerate(pairs)
        ]

    def act_copy():
        return pltpu.make_async_copy(act_h.at[b], act, c_sem.at[3 * slots])

    for slot in range(slots):
        for copy in slot_copies(slot):
            copy.start()

    @pl.when(op == 2)
    def _():
        act_copy().start()

    small[...] = jnp.zeros(small.shape, wide)
    small[TAPS + 2 : TAPS + 3, :] = jnp.full((1, width), op.astype(wide), wide)

    @pl.loop(0, slots)
    def _(slot):
        for copy in slot_copies(slot):
            copy.wait()

        @pl.loop(0, peers)
        def _(j):
            start = pl.multiple_of(j * span, span)
            rows = pl.ds(pl.multiple_of(slot * length + start, span), span)

            @pl.when(start < scalars[slot])
            def _():
                norm_back(b, scalars, gain, slot, start, rows, unit, stats, gn, du, small)

            @pl.when(start >= scalars[slot])
            def _():
                gn[rows, :] = jnp.zeros((span, width), wide)
                du[rows, :] = jnp.zeros((span, width), low)

    saves = [
        pltpu.make_async_copy(gn, gn_out, p_sem.at[half]),
        pltpu.make_async_copy(du, du_out, p_sem.at[half + 1]),
    ]
    for save in saves:
        save.start()

    @pl.when(op == 2)
    def _():
        act_copy().wait()
        values = nn(du[...].T, act[...]).astype(low)
        for d in range(groups):
            payload[pair_place(me, d, half), 0:cols, :] = values[d * cols : (d + 1) * cols]

    @pl.when(op != 2)
    def _():
        for d in range(groups):
            payload[d] = jnp.zeros(payload.shape[1:], low)

    leaving = [
        pltpu.make_async_copy(payload.at[pl.ds(2 * key, 2)], sent[key], p_sem.at[key])
        for key in range(half)
    ]
    for copy in leaving:
        copy.start()
    for copy in leaving + saves:
        copy.wait()


def norm_call(slots, length, peers, groups, scalars, g, kept, gain):
    rows, width = g.shape
    (_, unit, stats, _, _, act, _) = kept
    half = groups // 2
    pitch = up16(width // groups)
    shapes = [((rows, width), wide), ((rows, width), low), ((EXTRA, width), wide)]
    shapes += [((2, pitch, width), low)] * half
    return pl.pallas_call(
        functools.partial(norm_kernel, slots, length, peers, groups),
        out_shape=[jax.ShapeDtypeStruct(*s) for s in shapes],
        in_specs=[pl.BlockSpec(memory_space=pltpu.SMEM)] + [any_spec()] * 4 + [vmem_spec()],
        out_specs=[any_spec(), any_spec(), vmem_spec()] + [any_spec()] * half,
        scratch_shapes=[
            pltpu.VMEM((rows, width), wide),
            pltpu.VMEM((rows, width), low),
            pltpu.VMEM((rows, width), low),
            pltpu.VMEM((rows, 2 * HEAD), wide),
            pltpu.VMEM((rows, act.shape[2]), low),
            pltpu.VMEM((groups, pitch, width), low),
            pltpu.SemaphoreType.DMA((3 * slots + 1,)),
            pltpu.SemaphoreType.DMA((half + 2,)),
        ],
        compiler_params=pltpu.CompilerParams(vmem_limit_bytes=VMEM_LIMIT),
        name="norm_backward",
    )(scalars, g, unit, stats, act, gain)


def backward_kernel(b, slots, length, peers, groups, first, last, scalars, *refs):
    pieces = refs[: (peers if first else 3)]
    refs = refs[len(pieces) :]
    (a_h, unit_h, stats_h, qkv_h, mix_h, act_h, slope_h) = [ref.at[b] for ref in refs[:7]]
    (proj_h, out_h, fin_h, fout_h, point_h, depth, gain) = refs[7:14]
    g_out = refs[14]
    outputs = 1 if first else groups
    sent = refs[15 : 15 + outputs]
    (payload, gn, du, a_in, unit, stats, w_in, w_out, mix, act, slope, padded, stats_t, turned, small) = refs[
        15 + outputs : 30 + outputs
    ]
    (w_sem, s_sem, c_sem, p_sem) = refs[30 + outputs :]
    width = a_in.shape[1]
    hidden = w_in.shape[1]
    chunks = hidden // width
    tiles = length // TILE
    own = width // peers
    cols = width // groups
    hidden_cols = hidden // groups
    place = scalars[slots]
    me = scalars[slots + 1]
    op = scalars[slots + 2 + 2 * b]
    span = length // peers
    inner_at, small_at, _ = payload_rows(width, groups, last)

    def key_of(d):
        return d if first else jnp.bitwise_xor(me, d)

    def part(j):
        return pl.ds(j * width, width)

    def heads(j, pair):
        return pl.ds(pl.multiple_of(j * width + pair * 2 * HEAD, 2 * HEAD), 2 * HEAD)

    def slot_copies(slot):
        rows = pl.ds(pl.multiple_of(slot * length, length), length)
        if first:
            pairs = [(unit_h, unit)]
        else:
            pairs = [(pieces[0], gn), (pieces[1], du)]
        return [
            pltpu.make_async_copy(source.at[rows], target.at[rows], c_sem.at[2 * slot + j])
            for j, (source, target) in enumerate(pairs)
        ]

    def stats_copy():
        return pltpu.make_async_copy(stats_h, stats, c_sem.at[2 * slots])

    def input_copy():
        return pltpu.make_async_copy(a_h, a_in, c_sem.at[2 * slots + 1])

    def attn_copies():
        return (
            [
                pltpu.make_async_copy(qkv_h.at[j], slope.at[:, part(j)], s_sem.at[j])
                for j in range(3)
            ]
            + [pltpu.make_async_copy(mix_h, mix, s_sem.at[3])]
            + [
                pltpu.make_async_copy(proj_h.at[b, j], w_out.at[part(j)], w_sem.at[j])
                for j in range(3)
            ]
            + [pltpu.make_async_copy(out_h.at[b], w_out.at[part(3)], w_sem.at[3])]
        )

    def conv_copies():
        return [
            pltpu.make_async_copy(mix_h, mix, s_sem.at[0]),
            pltpu.make_async_copy(point_h.at[b], w_out.at[part(0)], w_sem.at[0]),
        ]

    def ffn_copies():
        return [
            pltpu.make_async_copy(fout_h.at[b], w_out, w_sem.at[0]),
            pltpu.make_async_copy(slope_h, slope, s_sem.at[0]),
            pltpu.make_async_copy(fin_h.at[b], w_in, w_sem.at[1]),
        ] + ([pltpu.make_async_copy(act_h, act, s_sem.at[1])] if first else [])

    stats_copy().start()
    for slot in range(slots):
        for copy in slot_copies(slot):
            copy.start()
    for index, copies in enumerate((attn_copies, conv_copies, ffn_copies)):

        @pl.when(op == index)
        def _():
            for copy in copies():
                copy.start()

    input_copy().start()

    def each_tile(body, rest):
        tiles_of(scalars, slots, length, body, rest)

    stats_copy().wait()
    if first:
        small[...] = jnp.zeros(small.shape, wide)
        small[TAPS + 2 : TAPS + 3, :] = jnp.full((1, width), op.astype(wide), wide)

        @pl.loop(0, slots)
        def _(slot):
            for copy in slot_copies(slot):
                copy.wait()

            @pl.loop(0, peers)
            def _(j):
                start = pl.multiple_of(j * span, span)
                rows = pl.ds(pl.multiple_of(slot * length + start, span), span)

                @pl.when(start < scalars[slot])
                def _():
                    if first:
                        for key in range(peers):

                            @pl.when(jnp.bitwise_xor(place, key) == j)
                            def _():
                                gn[rows, :] = pieces[key][slot].astype(wide)

                    norm_back(b, scalars, gain, slot, start, rows, unit, stats, gn, du, small)

                @pl.when(start >= scalars[slot])
                def _():
                    gn[rows, :] = jnp.zeros((span, width), wide)
                    du[rows, :] = jnp.zeros((span, width), low)

    else:
        small[...] = pieces[2][...]
        for slot in range(slots):
            for copy in slot_copies(slot):
                copy.wait()
    input_copy().wait()

    def turn_own(source):
        for s in range(peers):

            @pl.when(place == s)
            def _():
                turned[...] = source[:, s * own : (s + 1) * own].T

    def put_out(start, values):
        for d in range(groups):
            piece = values[d * cols : (d + 1) * cols].astype(low)
            payload[key_of(d), 0:cols, start : start + values.shape[1]] = piece

    def put_point(values):
        count = cols // peers
        for d in range(groups):
            for p in range(peers):
                piece = values[d * cols + p * count : d * cols + (p + 1) * count].astype(low)
                payload[key_of(d), 0:count, p * own : (p + 1) * own] = piece

    def put_in(d, values):
        for p in range(own // cols):
            at = slice(p * hidden_cols, (p + 1) * hidden_cols)
            payload[key_of(d), inner_at : inner_at + cols, at] = values[p * cols : (p + 1) * cols]

    def add_back(grad):
        if last:
            @pl.loop(0, slots)
            def _(slot):
                rows = pl.ds(pl.multiple_of(slot * length + place * span, span), span)
                keep = live_of(scalars, slot, place * span, span, width)

                @pl.when(place * span < scalars[slot])
                def _():
                    g_out[slot] = jnp.where(keep, gn[rows, :] + grad(rows), 0.0)

                @pl.when(place * span >= scalars[slot])
                def _():
                    g_out[slot] = jnp.zeros((span, width), wide)

        else:

            def add(slot, start, rows):
                g_out[rows, :] = gn[rows, :] + grad(rows)

            each_tile(add, None)

    @pl.when(op == 0)
    def _():
        copies = attn_copies()
        copies[7].wait()
        for copy in copies[:4]:
            copy.wait()
        turn_own(mix)
        put_out(3 * own, nn(turned[...], du[...]).T)

        feature = lax.broadcasted_iota(jnp.int32, (width, 2 * HEAD), 0)
        column = (lax.broadcasted_iota(jnp.int32, (width, 2 * HEAD), 1) - INNER) * HEAD
        of_head = ((feature >= column) & (feature < column + HEAD)).astype(wide).astype(low)

        def back(slot, start, rows):
            grads = nt(du[rows, :], w_out[part(3), :]).astype(low)
            both = grads.astype(wide) * mix[rows, :].astype(wide)
            high = both.astype(low)
            rest = (both - high.astype(wide)).astype(low)
            lane = lax.broadcasted_iota(jnp.int32, (TILE, 2 * HEAD), 1)
            inner = nn(high, of_head) + nn(rest, of_head)
            stats[rows, :] = jnp.where(lane < INNER, stats[rows, :], inner)
            mix[rows, :] = grads

        def clear(rows):
            for j in range(3):
                slope[rows, part(j)] = jnp.zeros((TILE, width), low)

        each_tile(back, clear)

        @pl.loop(0, slots)
        def _(slot):
            stats_t[slot] = stats[pl.ds(pl.multiple_of(slot * length, length), length), :].T

        def attend(slot, reach):
            every = pl.ds(pl.multiple_of(slot * length, length), reach)
            upper = lax.broadcasted_iota(jnp.int32, (2 * HEAD, reach), 0) < HEAD

            @pl.loop(0, HEADS // 2)
            def _(pair):
                keys = slope[every, heads(1, pair)]
                values = slope[every, heads(2, pair)]
                scaled = keys * FACTOR
                queries = split_heads(slope[every, heads(0, pair)] * FACTOR)
                grads = split_heads(mix[every, heads(0, pair)])
                scores = [nt(keys, one) for one in queries]
                products = [nt(values, one) for one in grads]
                dk = jnp.zeros((reach, 2 * HEAD), wide)
                dv = jnp.zeros((reach, 2 * HEAD), wide)
                dq = []
                for head in range(2):
                    stat = stats_t[slot, pl.ds(pair * 2 + head, 1), 0:reach]
                    soft = jnp.exp(jnp.minimum(scores[head] - stat, 0.0))
                    inner = stats_t[slot, pl.ds(pair * 2 + head + INNER, 1), 0:reach]
                    grad_scores = (soft * (products[head] - inner)).astype(low)
                    dq.append(tn(scaled, grad_scores))
                    dk = dk + nn(grad_scores, queries[head])
                    dv = dv + nn(soft.astype(low), grads[head])
                dq = jnp.where(upper, dq[0], dq[1])
                slope[every, heads(0, pair)] = dq.T.astype(low)
                slope[every, heads(1, pair)] = dk.astype(low)
                slope[every, heads(2, pair)] = dv.astype(low)

        for_reach(scalars, slots, length, attend)
        for j in range(3):
            copies[4 + j].wait()
        turn_own(a_in)

        for j in range(3):
            put_out(j * own, nn(turned[...], slope[:, part(j)]).T)

        def grad(rows):
            total = nt(slope[rows, part(0)], w_out[part(0), :])
            for j in range(1, 3):
                total = total + nt(slope[rows, part(j)], w_out[part(j), :])
            return total

        add_back(grad)

    @pl.when(op == 1)
    def _():
        copies = conv_copies()
        for copy in copies:
            copy.wait()
        turn_own(mix)
        put_point(nn(turned[...], du[...]).T)

        def back(slot, start, rows):
            mix[rows, :] = nt(du[rows, :], w_out[part(0), :]).astype(low)

        def clear(rows):
            mix[rows, :] = jnp.zeros((TILE, width), low)

        each_tile(back, clear)
        fill_padded(padded, a_in, slots, length)

        def depth_terms(slot, start, rows):
            near = window(padded, slot, start)
            grads = mix[rows, :].astype(wide)
            for offset in range(TAPS):
                at = PAD + offset - TAPS // 2
                term = jnp.sum(near[at : at + TILE] * grads, axis=0, keepdims=True)
                small[offset : offset + 1, :] += term * used_tap(scalars, slots, b, offset)

        each_tile(depth_terms, None)
        fill_padded(padded, mix, slots, length)

        def spread(slot, start, rows):
            near = window(padded, slot, start)
            running = gn[rows, :]
            for offset in range(TAPS):
                at = PAD - offset + TAPS // 2
                tap = depth[offset, b : b + 1, :] * used_tap(scalars, slots, b, offset)
                running = running + near[at : at + TILE] * tap
            gn[rows, :] = running

        each_tile(spread, None)
        add_back(lambda rows: 0.0)

    @pl.when(op == 2)
    def _():
        copies = ffn_copies()
        copies[0].wait()
        copies[1].wait()

        def back(slot, start, rows):
            upstream = du[rows, :]
            for j in range(chunks):
                df = nt(upstream, w_out[part(j), :]).astype(low).astype(wide)
                slope[rows, part(j)] = (df * slope[rows, part(j)].astype(wide)).astype(low)

        def clear(rows):
            slope[rows, :] = jnp.zeros((TILE, hidden), low)

        each_tile(back, clear)
        copies[2].wait()
        if first:
            copies[3].wait()
            put_out(0, nn(du[...].T, act[...]))
        turn_own(a_in)
        for d in range(groups):
            piece = slope[:, d * hidden_cols : (d + 1) * hidden_cols]
            put_in(d, nn(turned[...], piece).astype(low))
        add_back(lambda rows: nt(slope[rows, :], w_in[...]))

    for d in range(groups):
        payload[d, small_at : small_at + EXTRA, :] = small[...].astype(low)
    order = sorted(range(groups), key=lambda key: key < groups // 2)
    leaving = [
        pltpu.make_async_copy(
            payload.at[key], sent[0].at[key] if first else sent[key], p_sem.at[key]
        )
        for key in order
    ]
    for copy in leaving:
        copy.start()
    for copy in leaving:
        copy.wait()


def backward_call(b, slots, length, peers, groups, scalars, pieces, kept, weights, depth, gain):
    width = gain.shape[-1]
    hidden = weights[2].shape[2]
    rows = slots * length
    first = b == BLOCKS - 1
    last = b == 0
    count = payload_rows(width, groups, last)[2]
    shapes = [
        ((slots, length // peers, width) if last else (rows, width), wide),
    ] + ([((groups, count, width), low)] if first else [((count, width), low)] * groups)
    return pl.pallas_call(
        functools.partial(backward_kernel, b, slots, length, peers, groups, first, last),
        out_shape=[jax.ShapeDtypeStruct(*s) for s in shapes],
        in_specs=[pl.BlockSpec(memory_space=pltpu.SMEM)]
        + ([vmem_spec()] * peers if first else [any_spec(), any_spec(), vmem_spec()])
        + [any_spec()] * 12
        + [vmem_spec()] * 2,
        out_specs=[vmem_spec()] + [any_spec()] * (len(shapes) - 1),
        scratch_shapes=[
            pltpu.VMEM((groups, count, width), low),
            pltpu.VMEM((rows, width), wide),
            pltpu.VMEM((rows, width), low),
            pltpu.VMEM((rows, width), low),
            pltpu.VMEM((rows, width), low),
            pltpu.VMEM((rows, 2 * HEAD), wide),
            pltpu.VMEM((width, hidden), low),
            pltpu.VMEM((hidden, width), low),
            pltpu.VMEM((rows, width), low),
            pltpu.VMEM((rows, hidden // peers), low),
            pltpu.VMEM((rows, hidden), low),
            pltpu.VMEM((slots, length + 2 * PAD, width), wide),
            pltpu.VMEM((slots, 2 * HEAD, length), wide),
            pltpu.VMEM((width // peers, rows), low),
            pltpu.VMEM((EXTRA, width), wide),
            pltpu.SemaphoreType.DMA((4,)),
            pltpu.SemaphoreType.DMA((4,)),
            pltpu.SemaphoreType.DMA((2 * slots + 2,)),
            pltpu.SemaphoreType.DMA((groups,)),
        ],
        compiler_params=pltpu.CompilerParams(vmem_limit_bytes=VMEM_LIMIT),
        name="backward_block",
    )(scalars, *pieces, *kept, *weights, depth, gain)


def add_pieces(pieces, small, groups, peers, split):
    width = small.shape[2]
    cols = width // groups
    inner_at, small_at, _ = payload_rows(width, groups, split)
    sums = [None] * 4

    def add(index, value):
        sums[index] = value if sums[index] is None else sums[index] + value

    for at, piece in pieces:
        terms = piece[small_at : small_at + EXTRA, :].astype(wide)
        op = terms[TAPS + 2 : TAPS + 3, :]
        matrix = piece[0:cols, :].astype(wide)
        add(0, jnp.where(op == 0.0, matrix, 0.0))
        if not split:
            add(1, jnp.where(op == 2.0, matrix, 0.0))
        inner = piece[inner_at : inner_at + cols, :].astype(wide)
        add(2, jnp.where(op == 2.0, inner, 0.0))
        add(3, jnp.where(op == 1.0, piece[0 : cols // peers, :].astype(wide), 0.0))
        row = lax.broadcasted_iota(jnp.int32, terms.shape, 0)
        terms = jnp.where((row < TAPS) & (op != 1.0), 0.0, terms)
        for index in range(3):
            terms = jnp.where(row == TAPS + 2 + index, (op == index).astype(wide), terms)
        terms = jnp.where(row < TAPS + 5, terms, 0.0)
        small[at] = terms
    total = small[0]
    for index in range(1, len(pieces)):
        total = total + small[index]
    return sums, total


def placed(pieces, me):
    return [(jnp.bitwise_xor(me, key) % len(pieces), piece) for key, piece in enumerate(pieces)]


def early_kernel(index, *refs):
    pieces, total = refs[:-1], refs[-1]
    value = pieces[0][index].astype(wide)
    for piece in pieces[1:]:
        value = value + piece[index].astype(wide)
    total[...] = value.astype(low)


def early_call(pieces):
    return pl.pallas_call(
        functools.partial(early_kernel, 0),
        out_shape=jax.ShapeDtypeStruct(pieces[0].shape[1:], low),
        in_specs=[vmem_spec()] * len(pieces),
        out_specs=vmem_spec(),
        compiler_params=pltpu.CompilerParams(vmem_limit_bytes=VMEM_LIMIT),
        name="early_sum",
    )(*pieces)


def relay_kernel(groups, peers, slots, scalars, *refs):
    pieces, (dense, small) = refs[:-2], refs[-2:]
    width = dense.shape[1]
    cols = width // groups
    inner_at, point_at, small_at, _ = dense_rows(width, groups, peers)
    sums, total = add_pieces(placed(pieces, scalars[slots + 1]), small, groups, peers, True)
    dense[0:cols, :] = sums[0].astype(low)
    dense[inner_at : inner_at + cols, :] = sums[2].astype(low)
    dense[point_at : point_at + cols // peers, :] = sums[3].astype(low)
    dense[small_at : small_at + EXTRA, :] = total.astype(low)


def relay_call(groups, peers, slots, scalars, pieces):
    width = pieces[0].shape[1]
    count = dense_rows(width, groups, peers)[3]
    return pl.pallas_call(
        functools.partial(relay_kernel, groups, peers, slots),
        out_shape=jax.ShapeDtypeStruct((count, width), low),
        in_specs=[pl.BlockSpec(memory_space=pltpu.SMEM)] + [vmem_spec()] * len(pieces),
        out_specs=vmem_spec(),
        scratch_shapes=[pltpu.VMEM((len(pieces), EXTRA, width), wide)],
        compiler_params=pltpu.CompilerParams(vmem_limit_bytes=VMEM_LIMIT),
        name="relay_sum",
    )(scalars, *pieces)


def write_block(outs, at, sums, points, total, groups, peers):
    (proj, out, f_in, f_out, point, depth, gain, shift) = outs
    width = total.shape[1]
    cols = width // groups
    own = width // peers
    hidden_cols = f_in.shape[2]
    share = [1.0 / total[TAPS + 2 + op : TAPS + 3 + op, :] for op in range(3)]
    attn = sums[0] * share[0]
    for j in range(3):
        proj[at, j] = attn[:, j * own : (j + 1) * own].T
    out[at] = attn[:, 3 * own :].T
    f_out[at] = sums[1] * share[2]
    inner = sums[2] * share[2]
    for p in range(own // cols):
        f_in[at, p * cols : (p + 1) * cols, :] = inner[:, p * hidden_cols : (p + 1) * hidden_cols]
    points = points * share[1]
    points = jnp.concatenate([points[:, p * own : (p + 1) * own] for p in range(peers)], axis=0)
    point[at] = points.T
    depth[:, at, :] = total[0:TAPS] * share[1]
    gain[at : at + 1, :] = total[TAPS : TAPS + 1] * (1.0 / groups)
    shift[at : at + 1, :] = total[TAPS + 1 : TAPS + 2] * (1.0 / groups)


def direct_kernel(groups, peers, every, *refs):
    outs, small = refs[:-1], refs[-1]
    pieces = [(d, every.at[d]) for d in range(groups)]
    sums, total = add_pieces(pieces, small, groups, peers, False)
    write_block(outs, 0, sums, sums[3], total, groups, peers)


def final_kernel(groups, peers, slots, scalars, *refs):
    half = groups // 2
    near, early, (early_dense, dense) = refs[:half], refs[half : 2 * half], refs[2 * half : 2 * half + 2]
    done = refs[2 * half + 2 : 2 * half + 10]
    outs, small = refs[2 * half + 10 : -1], refs[-1]
    width = dense.shape[1]
    cols = width // groups
    inner_at, point_at, small_at, _ = dense_rows(width, groups, peers)
    sums, total = add_pieces(placed(near, scalars[slots + 1]), small, groups, peers, True)
    total = total.astype(low).astype(wide)
    total = total + dense[small_at : small_at + EXTRA, :].astype(wide)
    sums[0] = sums[0] + dense[0:cols, :].astype(wide)
    sums[1] = early_dense[0:cols, :].astype(wide)
    for piece in early:
        sums[1] = sums[1] + piece[1, 0:cols, :].astype(wide)
    sums[2] = sums[2] + dense[inner_at : inner_at + cols, :].astype(wide)
    points = sums[3] + dense[point_at : point_at + cols // peers, :].astype(wide)
    write_block(outs, 0, sums, points, total, groups, peers)
    for index, (source, target) in enumerate(zip(done, outs)):
        if index < 5:
            target[1] = source[0]
        elif index == 5:
            target[:, 1, :] = source[:, 0, :]
        else:
            target[1:2, :] = source[...]


def out_shapes(blocks, width, hidden, groups, peers):
    rows, cols = width // peers, width // groups
    shapes = [
        (blocks, 3, rows, cols),
        (blocks, rows, cols),
        (blocks, rows, hidden // groups),
        (blocks, cols, hidden // peers),
        (blocks, rows, cols),
        (TAPS, blocks, width),
        (blocks, width),
        (blocks, width),
    ]
    return [jax.ShapeDtypeStruct(s, wide) for s in shapes]


def direct_call(groups, peers, hidden, every):
    width = every.shape[-1]
    shapes = out_shapes(1, width, hidden, groups, peers)
    return pl.pallas_call(
        functools.partial(direct_kernel, groups, peers),
        out_shape=shapes,
        in_specs=[vmem_spec()],
        out_specs=[vmem_spec()] * len(shapes),
        scratch_shapes=[pltpu.VMEM((groups, EXTRA, width), wide)],
        compiler_params=pltpu.CompilerParams(vmem_limit_bytes=VMEM_LIMIT),
        name="direct_sum",
    )(every)


def final_call(groups, peers, slots, hidden, scalars, inputs):
    width = inputs[0].shape[-1]
    shapes = out_shapes(BLOCKS, width, hidden, groups, peers)
    return pl.pallas_call(
        functools.partial(final_kernel, groups, peers, slots),
        out_shape=shapes,
        in_specs=[pl.BlockSpec(memory_space=pltpu.SMEM)] + [vmem_spec()] * len(inputs),
        out_specs=[vmem_spec()] * len(shapes),
        scratch_shapes=[pltpu.VMEM((groups // 2, EXTRA, width), wide)],
        compiler_params=pltpu.CompilerParams(vmem_limit_bytes=VMEM_LIMIT),
        name="final_sum",
    )(scalars, *inputs)


def across(piece, axis, key):
    return lax.ppermute(piece, axis, [(i, i ^ key) for i in range(lax.axis_size(axis))])


def local(
    layer_in,
    lengths,
    op_ids,
    kernel_ids,
    attn_proj,
    attn_out,
    ffn_in,
    ffn_out,
    point_weights,
    depth_weights,
    norm_gains,
    norm_shifts,
    cotangent,
):
    slots, span, width = layer_in.shape
    peers = lax.axis_size("seq")
    groups = lax.axis_size("dp")
    place = lax.axis_index("seq").astype(jnp.int32)
    length = span * peers
    weights = (attn_proj, attn_out, ffn_in, ffn_out, point_weights)

    me = lax.axis_index("dp").astype(jnp.int32)
    half = groups // 2

    chosen = jnp.stack([op_ids[0], kernel_ids[0]], axis=1).reshape(-1)
    scalars = jnp.concatenate([lengths, jnp.stack([place, me]), chosen])
    depth_weights = jnp.swapaxes(depth_weights, 0, 1)

    later = cotangent.astype(low)
    parts = {0: layer_in.astype(low)}
    reach = peers // 2
    while reach:
        moved = {key ^ reach: across(part, "seq", reach) for key, part in parts.items()}
        if reach == peers // 2:
            moved, later, scalars = lax.optimization_barrier((moved, later, scalars))
        parts.update(moved)
        reach //= 2
    x_parts = [parts[key] for key in range(peers)]
    later, x_parts = lax.optimization_barrier((later, x_parts))
    cot_parts = [later] + [across(later, "seq", key) for key in range(1, peers)]
    layer_out, *saved = forward_call(
        slots, length, peers, scalars, x_parts, weights, depth_weights, norm_gains, norm_shifts
    )

    g, payload = backward_call(
        1, slots, length, peers, groups, scalars, cot_parts, saved, weights, depth_weights, norm_gains
    )
    every = lax.all_to_all(payload, "dp", 0, 0, tiled=True)
    grad, rounded, small, *early = norm_call(
        slots, length, peers, groups, scalars, g, saved, norm_gains
    )
    early = [early[0]] + [across(early[key], "dp", key) for key in range(1, half)]
    g, *sent = backward_call(
        0, slots, length, peers, groups, scalars, [grad, rounded, small], saved, weights,
        depth_weights, norm_gains,
    )
    early, g = lax.optimization_barrier((early, g))
    early_sum = early_call(early)
    early_dense = across(early_sum, "dp", half)
    far = [sent[half]] + [across(sent[half + key], "dp", key) for key in range(1, half)]
    done = direct_call(groups, peers, ffn_in.shape[2], every)
    far, _, done = lax.optimization_barrier((far, early_sum, done))
    partial = relay_call(groups, peers, slots, scalars, far)
    rest, partial = lax.optimization_barrier((sent[:half], partial))
    dense = across(partial, "dp", half)
    near = [rest[0]] + [across(rest[key], "dp", key) for key in range(1, half)]
    proj, out, f_in, f_out, point, depth, gain, shift = final_call(
        groups, peers, slots, ffn_in.shape[2], scalars, near + early + [early_dense, dense] + list(done)
    )
    f_out = jnp.swapaxes(f_out, 1, 2)
    depth = jnp.swapaxes(depth, 0, 1)
    return (layer_out, g, proj, out, f_in, f_out, point, depth, gain, shift)


def solution(mesh):
    placed = (
        P("dp", "seq", None),
        P("dp"),
        P("dp", None),
        P("dp", None),
        P(),
        P(),
        P(),
        P(),
        P(),
        P(),
        P(),
        P(),
        P("dp", "seq", None),
    )
    return jax.shard_map(
        local,
        mesh=mesh,
        in_specs=placed,
        out_specs=(
            P("dp", "seq", None),
            P("dp", "seq", None),
            P(None, None, "seq", "dp"),
            P(None, "seq", "dp"),
            P(None, "seq", "dp"),
            P(None, "seq", "dp"),
            P(None, "seq", "dp"),
            P(),
            P(),
            P(),
        ),
        check_vma=False,
    )
```

```python
import functools

import jax
import jax.numpy as jnp
from jax import lax
from jax.experimental import pallas as pl
from jax.experimental.pallas import tpu as pltpu
from jax.sharding import PartitionSpec as P

HEADS = 12
HEAD = 64
TAPS = 7
BLOCKS = 2
EXTRA = 16
PAD = 8
norm_eps = 1e-05
low = jnp.bfloat16
wide = jnp.float32
VMEM_LIMIT = 60 * 1024 * 1024


def nn(left, right):
    return lax.dot_general(left, right, (((1,), (0,)), ((), ())), preferred_element_type=wide)


def nt(left, right):
    return lax.dot_general(left, right, (((1,), (1,)), ((), ())), preferred_element_type=wide)


def tn(left, right):
    return lax.dot_general(left, right, (((0,), (0,)), ((), ())), preferred_element_type=wide)


def live_of(scalars, slot, start, count, width):
    at = lax.broadcasted_iota(jnp.int32, (count, width), 0) + start
    return at < scalars[slot]


def used_tap(scalars, slots, b, offset):
    return (abs(offset - TAPS // 2) <= scalars[slots + 3 + 2 * b] + 1).astype(wide)


def live_tiles(scalars, slot, size):
    return (scalars[slot] + size - 1) // size


def for_reach(scalars, slots, length, body):
    @pl.loop(0, slots)
    def _(slot):
        @pl.when(scalars[slot] <= length // 2)
        def _():
            body(slot, length // 2)

        @pl.when(scalars[slot] > length // 2)
        def _():
            body(slot, length)


def tiles_of(scalars, slots, length, body, rest):
    @pl.loop(0, slots)
    def _(slot):
        count = live_tiles(scalars, slot, TILE)

        @pl.loop(0, count)
        def _(t):
            start = pl.multiple_of(t * TILE, TILE)
            body(slot, start, pl.ds(pl.multiple_of(slot * length + start, TILE), TILE))

        if rest is not None:

            @pl.loop(count, length // TILE)
            def _(t):
                rest(pl.ds(pl.multiple_of(slot * length + t * TILE, TILE), TILE))


def fill_padded(padded, source, slots, length):
    width = padded.shape[2]

    @pl.loop(0, slots)
    def _(slot):
        padded[slot, 0:PAD, :] = jnp.zeros((PAD, width), wide)
        padded[slot, PAD + length : PAD + length + PAD, :] = jnp.zeros((PAD, width), wide)

        @pl.loop(0, length // 128)
        def _(t):
            rows = pl.ds(pl.multiple_of(slot * length + t * 128, 128), 128)
            at = pl.ds(pl.multiple_of(PAD + t * 128, PAD), 128)
            padded[slot, at, :] = source[rows, :].astype(wide)


def window(padded, slot, start):
    return padded[slot, pl.ds(pl.multiple_of(start, TILE), TILE + 2 * PAD), :]


TILE = 256
INNER = 16
FACTOR = HEAD**-0.5


def split_heads(tensor):
    lane = lax.broadcasted_iota(jnp.int32, tensor.shape, 1)
    none = jnp.zeros((), tensor.dtype)
    return [jnp.where(lane < HEAD, tensor, none), jnp.where(lane < HEAD, none, tensor)]


def pair_rows(tensor):
    return jnp.concatenate(split_heads(tensor), axis=0)


def forward_kernel(slots, length, peers, lengths_of, *refs):
    pieces = refs[:peers]
    (proj_h, out_h, fin_h, fout_h, point_h, depth, gain, shift) = refs[peers : peers + 8]
    refs = refs[peers + 8 :]
    layer_out = refs[0]
    saved = refs[1:8]
    (x_now, update, a_now, unit, stats, weights, mix, active, mine_active, slope, padded) = refs[8:19]
    w_sem, s_sem = refs[19:]
    scalars = lengths_of
    width = a_now.shape[1]
    hidden = slope.shape[1]
    share = mine_active.shape[1]
    span = length // peers
    chunks = hidden // width
    tiles = length // TILE
    place = scalars[slots]

    def part(j):
        return pl.ds(pl.multiple_of(j * width, width), width)

    def heads(j, pair):
        return pl.ds(pl.multiple_of(j * width + pair * 2 * HEAD, 2 * HEAD), 2 * HEAD)

    def op_of(b):
        return scalars[slots + 2 + 2 * b]

    def loads(b, op):
        w = weights.at[b]
        if op == 0:
            pairs = [(proj_h.at[b, j], j) for j in range(3)] + [(out_h.at[b], 3)]
        elif op == 1:
            pairs = [(point_h.at[b], 0)]
        else:
            pairs = [(fin_h.at[b, :, part(j)], j) for j in range(chunks)]
            pairs += [(fout_h.at[b, part(j)], chunks + j) for j in range(chunks)]
        return [pltpu.make_async_copy(source, w.at[j], w_sem.at[b, j]) for source, j in pairs]

    def saves(b, op):
        (a_h, unit_h, stats_h, qkv_h, mix_h, act_h, slope_h) = [ref.at[b] for ref in saved]
        if op == 0:
            pairs = [(slope.at[:, part(j)], qkv_h.at[j]) for j in range(3)] + [(mix, mix_h)]
        elif op == 1:
            pairs = [(mix, mix_h)]
        else:
            pairs = [(mine_active, act_h), (slope, slope_h)]
        return [
            pltpu.make_async_copy(source, target, s_sem.at[b, j])
            for j, (source, target) in enumerate(pairs)
        ]

    def common_saves(b):
        (a_h, unit_h, stats_h) = [ref.at[b] for ref in saved[:3]]
        pairs = [(a_now, a_h), (unit, unit_h), (stats, stats_h)]
        return [
            pltpu.make_async_copy(source, target, s_sem.at[b, 4 + j])
            for j, (source, target) in enumerate(pairs)
        ]

    def by_op(b, action):
        for op in range(3):

            @pl.when(op_of(b) == op)
            def _():
                action(op)

    def each_tile(body, rest):
        tiles_of(scalars, slots, length, body, rest)

    for b in range(BLOCKS):

        def start_all(op):
            for copy in loads(b, op):
                copy.start()

        by_op(b, start_all)

    for key, piece in enumerate(pieces):
        origin = jnp.bitwise_xor(place, key) * span

        @pl.loop(0, slots)
        def _(slot):
            rows = pl.ds(pl.multiple_of(slot * length + origin, span), span)
            keep = live_of(scalars, slot, origin, span, width)
            value = jnp.where(keep, piece[slot].astype(wide), 0.0)
            x_now[rows, :] = value
            a_now[rows, :] = value.astype(low)

    def attention(b):
        w = weights.at[b]

        @pl.loop(0, 3)
        def _(j):
            pltpu.make_async_copy(proj_h.at[b, j], w.at[j], w_sem.at[b, j]).wait()

            def project(slot, start, rows):
                slope[rows, part(j)] = nn(a_now[rows, :], w[j]).astype(low)

            def clear(rows):
                slope[rows, part(j)] = jnp.zeros((TILE, width), low)

            each_tile(project, clear)
            pltpu.make_async_copy(slope.at[:, part(j)], saved[3].at[b, j], s_sem.at[b, j]).start()

        def clear_mix(rows):
            mix[rows, :] = jnp.zeros((TILE, width), low)

        each_tile(lambda slot, start, rows: None, clear_mix)

        def attend(slot, reach):
            base = pl.multiple_of(slot * length, length)
            key_at = lax.broadcasted_iota(jnp.int32, (1, reach), 1)
            bias = jnp.where(key_at < scalars[slot], 0.0, -1000000000.0).astype(wide)
            lane = lax.broadcasted_iota(jnp.int32, (TILE, 2 * HEAD), 1)

            @pl.loop(0, HEADS // 2, unroll=3)
            def _(pair):
                keys = slope[pl.ds(base, reach), heads(1, pair)]
                values = slope[pl.ds(base, reach), heads(2, pair)]
                for t in range(reach // TILE):
                    rows = pl.ds(pl.multiple_of(base + t * TILE, TILE), TILE)
                    scores = nt(pair_rows(slope[rows, heads(0, pair)] * FACTOR), keys) + bias
                    top = jnp.max(scores, axis=-1, keepdims=True)
                    exponent = jnp.exp(scores - top)
                    total = jnp.sum(exponent, axis=-1, keepdims=True)
                    mixed = nn(exponent.astype(low), values) * (1.0 / total)
                    stat = top + jnp.log(total)
                    kept = jnp.where(lane == pair * 2, stat[:TILE], stats[rows, :])
                    stats[rows, :] = jnp.where(lane == pair * 2 + 1, stat[TILE:], kept)
                    both = jnp.where(lane < HEAD, mixed[:TILE], mixed[TILE:])
                    mix[rows, heads(0, pair)] = both.astype(low)

        for_reach(scalars, slots, length, attend)
        saves(b, 0)[3].start()
        loads(b, 0)[3].wait()

        def out(slot, start, rows):
            update[rows, :] = nn(mix[rows, :], w[3])

        each_tile(out, None)

    def convolution(b):
        fill_padded(padded, a_now, slots, length)
        loads(b, 1)[0].wait()

        def run(slot, start, rows):
            near = window(padded, slot, start)
            running = jnp.zeros((TILE, width), wide)
            for offset in range(TAPS):
                at = PAD + offset - TAPS // 2
                tap = depth[offset, pl.ds(b, 1), :] * used_tap(scalars, slots, b, offset)
                running = running + near[at : at + TILE] * tap
            mix[rows, :] = running.astype(low)
            update[rows, :] = nn(running.astype(low), weights[b, 0])

        def clear(rows):
            mix[rows, :] = jnp.zeros((TILE, width), low)

        each_tile(run, clear)
        saves(b, 1)[0].start()

    def feed_forward(b):
        w = weights.at[b]
        mine = pl.ds(pl.multiple_of(place * share, 128), share)

        for copy in loads(b, 2):
            copy.wait()

        def run(slot, start, rows):
            update[rows, :] = jnp.zeros((TILE, width), wide)

            @pl.loop(0, chunks, unroll=4)
            def _(j):
                h = nn(a_now[rows, :], w[j])
                cdf = 0.5 * (1.0 + lax.erf(h * (0.5**0.5)))
                density = jnp.exp(-0.5 * h * h) * 0.3989422804014327
                value = (h * cdf).astype(low)
                active[:, part(j)] = value
                slope[rows, part(j)] = (cdf + h * density).astype(low)
                update[rows, :] += nn(value, w[chunks + j])

            mine_active[rows, :] = active[:, mine]

        def clear(rows):
            mine_active[rows, :] = jnp.zeros((TILE, share), low)

        each_tile(run, clear)
        for save in saves(b, 2):
            save.start()

    @pl.loop(0, BLOCKS)
    def _(b):
        common_saves(b)[0].start()

        @pl.when(b > 0)
        def _():
            def wait_saves(op):
                for save in saves(b - 1, op):
                    save.wait()

            by_op(b - 1, wait_saves)
            for save in common_saves(b - 1)[1:]:
                save.wait()

        for op, branch in enumerate((attention, convolution, feed_forward)):

            @pl.when(op_of(b) == op)
            def _():
                branch(b)

        common_saves(b)[0].wait()

        def norm(slot, start, rows):
            z = x_now[rows, :] + update[rows, :]
            center = z - jnp.mean(z, axis=-1, keepdims=True)
            scale = lax.rsqrt(jnp.mean(center * center, axis=-1, keepdims=True) + norm_eps)
            value = center * scale
            unit[rows, :] = value.astype(low)
            lane = lax.broadcasted_iota(jnp.int32, (TILE, 2 * HEAD), 1)
            stats[rows, :] = jnp.where(lane == HEADS, scale, stats[rows, :])
            keep = live_of(scalars, slot, start, TILE, width)
            value = jnp.where(keep, value * gain[pl.ds(b, 1), :] + shift[pl.ds(b, 1), :], 0.0)
            x_now[rows, :] = value
            a_now[rows, :] = value.astype(low)

        def clear(rows):
            x_now[rows, :] = jnp.zeros((TILE, width), wide)
            a_now[rows, :] = jnp.zeros((TILE, width), low)

        each_tile(norm, clear)
        for save in common_saves(b)[1:]:
            save.start()

    for slot in range(slots):
        rows = pl.ds(pl.multiple_of(slot * length + place * span, span), span)
        layer_out[slot] = x_now[rows, :]

    def wait_last(op):
        for save in saves(BLOCKS - 1, op):
            save.wait()

    by_op(BLOCKS - 1, wait_last)
    for save in common_saves(BLOCKS - 1)[1:]:
        save.wait()


def any_spec():
    return pl.BlockSpec(memory_space=pl.ANY)


def vmem_spec():
    return pl.BlockSpec(memory_space=pltpu.VMEM)


def forward_call(slots, length, peers, scalars, pieces, weights, depth, gain, shift):
    width = gain.shape[-1]
    hidden = weights[2].shape[2]
    rows = slots * length
    shapes = [((slots, length // peers, width), wide)]
    shapes += [
        ((BLOCKS, rows, width), low),
        ((BLOCKS, rows, width), low),
        ((BLOCKS, rows, 2 * HEAD), wide),
        ((BLOCKS, 3, rows, width), low),
        ((BLOCKS, rows, width), low),
        ((BLOCKS, rows, hidden // peers), low),
        ((BLOCKS, rows, hidden), low),
    ]
    return pl.pallas_call(
        functools.partial(forward_kernel, slots, length, peers),
        out_shape=[jax.ShapeDtypeStruct(*s) for s in shapes],
        in_specs=[pl.BlockSpec(memory_space=pltpu.SMEM)]
        + [vmem_spec()] * len(pieces)
        + [any_spec()] * 5
        + [vmem_spec()] * 3,
        out_specs=[vmem_spec()] + [any_spec()] * (len(shapes) - 1),
        scratch_shapes=[
            pltpu.VMEM((rows, width), wide),
            pltpu.VMEM((rows, width), wide),
            pltpu.VMEM((rows, width), low),
            pltpu.VMEM((rows, width), low),
            pltpu.VMEM((rows, 2 * HEAD), wide),
            pltpu.VMEM((BLOCKS, 8, width, width), low),
            pltpu.VMEM((rows, width), low),
            pltpu.VMEM((TILE, hidden), low),
            pltpu.VMEM((rows, hidden // peers), low),
            pltpu.VMEM((rows, hidden), low),
            pltpu.VMEM((slots, length + 2 * PAD, width), wide),
            pltpu.SemaphoreType.DMA((BLOCKS, 8)),
            pltpu.SemaphoreType.DMA((BLOCKS, 8)),
        ],
        compiler_params=pltpu.CompilerParams(vmem_limit_bytes=VMEM_LIMIT),
        name="forward_blocks",
    )(scalars, *pieces, *weights, depth, gain, shift)


def up16(count):
    return -(-count // 16) * 16


def payload_rows(width, groups, split):
    pitch = up16(width // groups)
    inner = 0 if split else pitch
    return inner, inner + pitch, inner + pitch + EXTRA


def dense_rows(width, groups, peers):
    pitch = up16(width // groups)
    tail = up16(width // groups // peers)
    return pitch, 2 * pitch, 2 * pitch + tail, 2 * pitch + tail + EXTRA


def norm_back(b, scalars, gain, slot, start, rows, unit, stats, gn, du, small):
    span, width = rows.size, gn.shape[1]
    keep = live_of(scalars, slot, start, span, width)
    g = jnp.where(keep, gn[rows, :], 0.0)
    value = unit[rows, :].astype(wide)
    gu = g * value
    gy = g * gain[b : b + 1, :]
    one = jnp.mean(gy, axis=-1, keepdims=True)
    two = jnp.mean(gu * gain[b : b + 1, :], axis=-1, keepdims=True)
    dz = stats[rows, HEADS : HEADS + 1] * (gy - one - value * two)
    gn[rows, :] = dz
    du[rows, :] = dz.astype(low)
    small[TAPS : TAPS + 1, :] += jnp.sum(gu, axis=0, keepdims=True)
    small[TAPS + 1 : TAPS + 2, :] += jnp.sum(g, axis=0, keepdims=True)


def pair_place(me, d, half):
    key = jnp.bitwise_xor(me, d)
    return 2 * (key % half) + (key < half).astype(jnp.int32)


def norm_kernel(slots, length, peers, groups, scalars, g_h, unit_h, stats_h, act_h, gain, *refs):
    (gn_out, du_out, small) = refs[:3]
    half = groups // 2
    sent = refs[3 : 3 + half]
    (gn, du, unit, stats, act, payload, c_sem, p_sem) = refs[3 + half :]
    b = 0
    width = gn.shape[1]
    cols = width // groups
    span = length // peers
    op = scalars[slots + 2]
    me = scalars[slots + 1]

    def slot_copies(slot):
        rows = pl.ds(pl.multiple_of(slot * length, length), length)
        pairs = [(g_h, gn), (unit_h.at[b], unit), (stats_h.at[b], stats)]
        return [
            pltpu.make_async_copy(source.at[rows], target.at[rows], c_sem.at[3 * slot + j])
            for j, (source, target) in enumerate(pairs)
        ]

    def act_copy():
        return pltpu.make_async_copy(act_h.at[b], act, c_sem.at[3 * slots])

    for slot in range(slots):
        for copy in slot_copies(slot):
            copy.start()

    @pl.when(op == 2)
    def _():
        act_copy().start()

    small[...] = jnp.zeros(small.shape, wide)
    small[TAPS + 2 : TAPS + 3, :] = jnp.full((1, width), op.astype(wide), wide)

    @pl.loop(0, slots)
    def _(slot):
        for copy in slot_copies(slot):
            copy.wait()

        @pl.loop(0, peers)
        def _(j):
            start = pl.multiple_of(j * span, span)
            rows = pl.ds(pl.multiple_of(slot * length + start, span), span)

            @pl.when(start < scalars[slot])
            def _():
                norm_back(b, scalars, gain, slot, start, rows, unit, stats, gn, du, small)

            @pl.when(start >= scalars[slot])
            def _():
                gn[rows, :] = jnp.zeros((span, width), wide)
                du[rows, :] = jnp.zeros((span, width), low)

    saves = [
        pltpu.make_async_copy(gn, gn_out, p_sem.at[half]),
        pltpu.make_async_copy(du, du_out, p_sem.at[half + 1]),
    ]
    for save in saves:
        save.start()

    @pl.when(op == 2)
    def _():
        act_copy().wait()
        values = nn(du[...].T, act[...]).astype(low)
        for d in range(groups):
            payload[pair_place(me, d, half), 0:cols, :] = values[d * cols : (d + 1) * cols]

    @pl.when(op != 2)
    def _():
        for d in range(groups):
            payload[d] = jnp.zeros(payload.shape[1:], low)

    leaving = [
        pltpu.make_async_copy(payload.at[pl.ds(2 * key, 2)], sent[key], p_sem.at[key])
        for key in range(half)
    ]
    for copy in leaving:
        copy.start()
    for copy in leaving + saves:
        copy.wait()


def norm_call(slots, length, peers, groups, scalars, g, kept, gain):
    rows, width = g.shape
    (_, unit, stats, _, _, act, _) = kept
    half = groups // 2
    pitch = up16(width // groups)
    shapes = [((rows, width), wide), ((rows, width), low), ((EXTRA, width), wide)]
    shapes += [((2, pitch, width), low)] * half
    return pl.pallas_call(
        functools.partial(norm_kernel, slots, length, peers, groups),
        out_shape=[jax.ShapeDtypeStruct(*s) for s in shapes],
        in_specs=[pl.BlockSpec(memory_space=pltpu.SMEM)] + [any_spec()] * 4 + [vmem_spec()],
        out_specs=[any_spec(), any_spec(), vmem_spec()] + [any_spec()] * half,
        scratch_shapes=[
            pltpu.VMEM((rows, width), wide),
            pltpu.VMEM((rows, width), low),
            pltpu.VMEM((rows, width), low),
            pltpu.VMEM((rows, 2 * HEAD), wide),
            pltpu.VMEM((rows, act.shape[2]), low),
            pltpu.VMEM((groups, pitch, width), low),
            pltpu.SemaphoreType.DMA((3 * slots + 1,)),
            pltpu.SemaphoreType.DMA((half + 2,)),
        ],
        compiler_params=pltpu.CompilerParams(vmem_limit_bytes=VMEM_LIMIT),
        name="norm_backward",
    )(scalars, g, unit, stats, act, gain)


def backward_kernel(b, slots, length, peers, groups, first, last, scalars, *refs):
    pieces = refs[: (peers if first else 3)]
    refs = refs[len(pieces) :]
    (a_h, unit_h, stats_h, qkv_h, mix_h, act_h, slope_h) = [ref.at[b] for ref in refs[:7]]
    (proj_h, out_h, fin_h, fout_h, point_h, depth, gain) = refs[7:14]
    g_out = refs[14]
    outputs = 1 if first else groups
    sent = refs[15 : 15 + outputs]
    (payload, gn, du, a_in, unit, stats, w_in, w_out, mix, act, slope, padded, stats_t, turned, small) = refs[
        15 + outputs : 30 + outputs
    ]
    (w_sem, s_sem, c_sem, p_sem) = refs[30 + outputs :]
    width = a_in.shape[1]
    hidden = w_in.shape[1]
    chunks = hidden // width
    tiles = length // TILE
    own = width // peers
    cols = width // groups
    hidden_cols = hidden // groups
    place = scalars[slots]
    me = scalars[slots + 1]
    op = scalars[slots + 2 + 2 * b]
    span = length // peers
    inner_at, small_at, _ = payload_rows(width, groups, last)

    def key_of(d):
        return d if first else jnp.bitwise_xor(me, d)

    def part(j):
        return pl.ds(j * width, width)

    def heads(j, pair):
        return pl.ds(pl.multiple_of(j * width + pair * 2 * HEAD, 2 * HEAD), 2 * HEAD)

    def slot_copies(slot):
        rows = pl.ds(pl.multiple_of(slot * length, length), length)
        if first:
            pairs = [(unit_h, unit)]
        else:
            pairs = [(pieces[0], gn), (pieces[1], du)]
        return [
            pltpu.make_async_copy(source.at[rows], target.at[rows], c_sem.at[2 * slot + j])
            for j, (source, target) in enumerate(pairs)
        ]

    def stats_copy():
        return pltpu.make_async_copy(stats_h, stats, c_sem.at[2 * slots])

    def input_copy():
        return pltpu.make_async_copy(a_h, a_in, c_sem.at[2 * slots + 1])

    def attn_copies():
        return (
            [
                pltpu.make_async_copy(qkv_h.at[j], slope.at[:, part(j)], s_sem.at[j])
                for j in range(3)
            ]
            + [pltpu.make_async_copy(mix_h, mix, s_sem.at[3])]
            + [
                pltpu.make_async_copy(proj_h.at[b, j], w_out.at[part(j)], w_sem.at[j])
                for j in range(3)
            ]
            + [pltpu.make_async_copy(out_h.at[b], w_out.at[part(3)], w_sem.at[3])]
        )

    def conv_copies():
        return [
            pltpu.make_async_copy(mix_h, mix, s_sem.at[0]),
            pltpu.make_async_copy(point_h.at[b], w_out.at[part(0)], w_sem.at[0]),
        ]

    def ffn_copies():
        return [
            pltpu.make_async_copy(fout_h.at[b], w_out, w_sem.at[0]),
            pltpu.make_async_copy(slope_h, slope, s_sem.at[0]),
            pltpu.make_async_copy(fin_h.at[b], w_in, w_sem.at[1]),
        ] + ([pltpu.make_async_copy(act_h, act, s_sem.at[1])] if first else [])

    stats_copy().start()
    for slot in range(slots):
        for copy in slot_copies(slot):
            copy.start()
    for index, copies in enumerate((attn_copies, conv_copies, ffn_copies)):

        @pl.when(op == index)
        def _():
            for copy in copies():
                copy.start()

    input_copy().start()

    def each_tile(body, rest):
        tiles_of(scalars, slots, length, body, rest)

    stats_copy().wait()
    if first:
        small[...] = jnp.zeros(small.shape, wide)
        small[TAPS + 2 : TAPS + 3, :] = jnp.full((1, width), op.astype(wide), wide)

        @pl.loop(0, slots)
        def _(slot):
            for copy in slot_copies(slot):
                copy.wait()

            @pl.loop(0, peers)
            def _(j):
                start = pl.multiple_of(j * span, span)
                rows = pl.ds(pl.multiple_of(slot * length + start, span), span)

                @pl.when(start < scalars[slot])
                def _():
                    if first:
                        for key in range(peers):

                            @pl.when(jnp.bitwise_xor(place, key) == j)
                            def _():
                                gn[rows, :] = pieces[key][slot].astype(wide)

                    norm_back(b, scalars, gain, slot, start, rows, unit, stats, gn, du, small)

                @pl.when(start >= scalars[slot])
                def _():
                    gn[rows, :] = jnp.zeros((span, width), wide)
                    du[rows, :] = jnp.zeros((span, width), low)

    else:
        small[...] = pieces[2][...]
        for slot in range(slots):
            for copy in slot_copies(slot):
                copy.wait()
    input_copy().wait()

    def turn_own(source):
        for s in range(peers):

            @pl.when(place == s)
            def _():
                turned[...] = source[:, s * own : (s + 1) * own].T

    def put_out(start, values):
        for d in range(groups):
            piece = values[d * cols : (d + 1) * cols].astype(low)
            payload[key_of(d), 0:cols, start : start + values.shape[1]] = piece

    def put_point(values):
        count = cols // peers
        for d in range(groups):
            for p in range(peers):
                piece = values[d * cols + p * count : d * cols + (p + 1) * count].astype(low)
                payload[key_of(d), 0:count, p * own : (p + 1) * own] = piece

    def put_in(d, values):
        for p in range(own // cols):
            at = slice(p * hidden_cols, (p + 1) * hidden_cols)
            payload[key_of(d), inner_at : inner_at + cols, at] = values[p * cols : (p + 1) * cols]

    def add_back(grad):
        if last:
            @pl.loop(0, slots)
            def _(slot):
                rows = pl.ds(pl.multiple_of(slot * length + place * span, span), span)
                keep = live_of(scalars, slot, place * span, span, width)

                @pl.when(place * span < scalars[slot])
                def _():
                    g_out[slot] = jnp.where(keep, gn[rows, :] + grad(rows), 0.0)

                @pl.when(place * span >= scalars[slot])
                def _():
                    g_out[slot] = jnp.zeros((span, width), wide)

        else:

            def add(slot, start, rows):
                g_out[rows, :] = gn[rows, :] + grad(rows)

            each_tile(add, None)

    @pl.when(op == 0)
    def _():
        copies = attn_copies()
        copies[7].wait()
        for copy in copies[:4]:
            copy.wait()
        turn_own(mix)
        put_out(3 * own, nn(turned[...], du[...]).T)

        feature = lax.broadcasted_iota(jnp.int32, (width, 2 * HEAD), 0)
        column = (lax.broadcasted_iota(jnp.int32, (width, 2 * HEAD), 1) - INNER) * HEAD
        of_head = ((feature >= column) & (feature < column + HEAD)).astype(wide).astype(low)

        def back(slot, start, rows):
            grads = nt(du[rows, :], w_out[part(3), :]).astype(low)
            both = grads.astype(wide) * mix[rows, :].astype(wide)
            high = both.astype(low)
            rest = (both - high.astype(wide)).astype(low)
            lane = lax.broadcasted_iota(jnp.int32, (TILE, 2 * HEAD), 1)
            inner = nn(high, of_head) + nn(rest, of_head)
            stats[rows, :] = jnp.where(lane < INNER, stats[rows, :], inner)
            mix[rows, :] = grads

        def clear(rows):
            for j in range(3):
                slope[rows, part(j)] = jnp.zeros((TILE, width), low)

        each_tile(back, clear)

        @pl.loop(0, slots)
        def _(slot):
            stats_t[slot] = stats[pl.ds(pl.multiple_of(slot * length, length), length), :].T

        def attend(slot, reach):
            every = pl.ds(pl.multiple_of(slot * length, length), reach)
            upper = lax.broadcasted_iota(jnp.int32, (2 * HEAD, reach), 0) < HEAD

            @pl.loop(0, HEADS // 2)
            def _(pair):
                keys = slope[every, heads(1, pair)]
                values = slope[every, heads(2, pair)]
                scaled = keys * FACTOR
                queries = split_heads(slope[every, heads(0, pair)] * FACTOR)
                grads = split_heads(mix[every, heads(0, pair)])
                scores = [nt(keys, one) for one in queries]
                products = [nt(values, one) for one in grads]
                dk = jnp.zeros((reach, 2 * HEAD), wide)
                dv = jnp.zeros((reach, 2 * HEAD), wide)
                dq = []
                for head in range(2):
                    stat = stats_t[slot, pl.ds(pair * 2 + head, 1), 0:reach]
                    soft = jnp.exp(jnp.minimum(scores[head] - stat, 0.0))
                    inner = stats_t[slot, pl.ds(pair * 2 + head + INNER, 1), 0:reach]
                    grad_scores = (soft * (products[head] - inner)).astype(low)
                    dq.append(tn(scaled, grad_scores))
                    dk = dk + nn(grad_scores, queries[head])
                    dv = dv + nn(soft.astype(low), grads[head])
                dq = jnp.where(upper, dq[0], dq[1])
                slope[every, heads(0, pair)] = dq.T.astype(low)
                slope[every, heads(1, pair)] = dk.astype(low)
                slope[every, heads(2, pair)] = dv.astype(low)

        for_reach(scalars, slots, length, attend)
        for j in range(3):
            copies[4 + j].wait()
        turn_own(a_in)

        for j in range(3):
            put_out(j * own, nn(turned[...], slope[:, part(j)]).T)

        def grad(rows):
            total = nt(slope[rows, part(0)], w_out[part(0), :])
            for j in range(1, 3):
                total = total + nt(slope[rows, part(j)], w_out[part(j), :])
            return total

        add_back(grad)

    @pl.when(op == 1)
    def _():
        copies = conv_copies()
        for copy in copies:
            copy.wait()
        turn_own(mix)
        put_point(nn(turned[...], du[...]).T)

        def back(slot, start, rows):
            mix[rows, :] = nt(du[rows, :], w_out[part(0), :]).astype(low)

        def clear(rows):
            mix[rows, :] = jnp.zeros((TILE, width), low)

        each_tile(back, clear)
        fill_padded(padded, a_in, slots, length)

        def depth_terms(slot, start, rows):
            near = window(padded, slot, start)
            grads = mix[rows, :].astype(wide)
            for offset in range(TAPS):
                at = PAD + offset - TAPS // 2
                term = jnp.sum(near[at : at + TILE] * grads, axis=0, keepdims=True)
                small[offset : offset + 1, :] += term * used_tap(scalars, slots, b, offset)

        each_tile(depth_terms, None)
        fill_padded(padded, mix, slots, length)

        def spread(slot, start, rows):
            near = window(padded, slot, start)
            running = gn[rows, :]
            for offset in range(TAPS):
                at = PAD - offset + TAPS // 2
                tap = depth[offset, b : b + 1, :] * used_tap(scalars, slots, b, offset)
                running = running + near[at : at + TILE] * tap
            gn[rows, :] = running

        each_tile(spread, None)
        add_back(lambda rows: 0.0)

    @pl.when(op == 2)
    def _():
        copies = ffn_copies()
        copies[0].wait()
        copies[1].wait()

        def back(slot, start, rows):
            upstream = du[rows, :]
            for j in range(chunks):
                df = nt(upstream, w_out[part(j), :]).astype(low).astype(wide)
                slope[rows, part(j)] = (df * slope[rows, part(j)].astype(wide)).astype(low)

        def clear(rows):
            slope[rows, :] = jnp.zeros((TILE, hidden), low)

        each_tile(back, clear)
        copies[2].wait()
        if first:
            copies[3].wait()
            put_out(0, nn(du[...].T, act[...]))
        turn_own(a_in)
        for d in range(groups):
            piece = slope[:, d * hidden_cols : (d + 1) * hidden_cols]
            put_in(d, nn(turned[...], piece).astype(low))
        add_back(lambda rows: nt(slope[rows, :], w_in[...]))

    for d in range(groups):
        payload[d, small_at : small_at + EXTRA, :] = small[...].astype(low)
    order = sorted(range(groups), key=lambda key: key < groups // 2)
    leaving = [
        pltpu.make_async_copy(
            payload.at[key], sent[0].at[key] if first else sent[key], p_sem.at[key]
        )
        for key in order
    ]
    for copy in leaving:
        copy.start()
    for copy in leaving:
        copy.wait()


def backward_call(b, slots, length, peers, groups, scalars, pieces, kept, weights, depth, gain):
    width = gain.shape[-1]
    hidden = weights[2].shape[2]
    rows = slots * length
    first = b == BLOCKS - 1
    last = b == 0
    count = payload_rows(width, groups, last)[2]
    shapes = [
        ((slots, length // peers, width) if last else (rows, width), wide),
    ] + ([((groups, count, width), low)] if first else [((count, width), low)] * groups)
    return pl.pallas_call(
        functools.partial(backward_kernel, b, slots, length, peers, groups, first, last),
        out_shape=[jax.ShapeDtypeStruct(*s) for s in shapes],
        in_specs=[pl.BlockSpec(memory_space=pltpu.SMEM)]
        + ([vmem_spec()] * peers if first else [any_spec(), any_spec(), vmem_spec()])
        + [any_spec()] * 12
        + [vmem_spec()] * 2,
        out_specs=[vmem_spec()] + [any_spec()] * (len(shapes) - 1),
        scratch_shapes=[
            pltpu.VMEM((groups, count, width), low),
            pltpu.VMEM((rows, width), wide),
            pltpu.VMEM((rows, width), low),
            pltpu.VMEM((rows, width), low),
            pltpu.VMEM((rows, width), low),
            pltpu.VMEM((rows, 2 * HEAD), wide),
            pltpu.VMEM((width, hidden), low),
            pltpu.VMEM((hidden, width), low),
            pltpu.VMEM((rows, width), low),
            pltpu.VMEM((rows, hidden // peers), low),
            pltpu.VMEM((rows, hidden), low),
            pltpu.VMEM((slots, length + 2 * PAD, width), wide),
            pltpu.VMEM((slots, 2 * HEAD, length), wide),
            pltpu.VMEM((width // peers, rows), low),
            pltpu.VMEM((EXTRA, width), wide),
            pltpu.SemaphoreType.DMA((4,)),
            pltpu.SemaphoreType.DMA((4,)),
            pltpu.SemaphoreType.DMA((2 * slots + 2,)),
            pltpu.SemaphoreType.DMA((groups,)),
        ],
        compiler_params=pltpu.CompilerParams(vmem_limit_bytes=VMEM_LIMIT),
        name="backward_block",
    )(scalars, *pieces, *kept, *weights, depth, gain)


def add_pieces(pieces, small, groups, peers, split):
    width = small.shape[2]
    cols = width // groups
    inner_at, small_at, _ = payload_rows(width, groups, split)
    sums = [None] * 4

    def add(index, value):
        sums[index] = value if sums[index] is None else sums[index] + value

    for at, piece in pieces:
        terms = piece[small_at : small_at + EXTRA, :].astype(wide)
        op = terms[TAPS + 2 : TAPS + 3, :]
        matrix = piece[0:cols, :].astype(wide)
        add(0, jnp.where(op == 0.0, matrix, 0.0))
        if not split:
            add(1, jnp.where(op == 2.0, matrix, 0.0))
        inner = piece[inner_at : inner_at + cols, :].astype(wide)
        add(2, jnp.where(op == 2.0, inner, 0.0))
        add(3, jnp.where(op == 1.0, piece[0 : cols // peers, :].astype(wide), 0.0))
        row = lax.broadcasted_iota(jnp.int32, terms.shape, 0)
        terms = jnp.where((row < TAPS) & (op != 1.0), 0.0, terms)
        for index in range(3):
            terms = jnp.where(row == TAPS + 2 + index, (op == index).astype(wide), terms)
        terms = jnp.where(row < TAPS + 5, terms, 0.0)
        small[at] = terms
    total = small[0]
    for index in range(1, len(pieces)):
        total = total + small[index]
    return sums, total


def placed(pieces, me):
    return [(jnp.bitwise_xor(me, key) % len(pieces), piece) for key, piece in enumerate(pieces)]


def early_kernel(index, *refs):
    pieces, total = refs[:-1], refs[-1]
    value = pieces[0][index].astype(wide)
    for piece in pieces[1:]:
        value = value + piece[index].astype(wide)
    total[...] = value.astype(low)


def early_call(pieces):
    return pl.pallas_call(
        functools.partial(early_kernel, 0),
        out_shape=jax.ShapeDtypeStruct(pieces[0].shape[1:], low),
        in_specs=[vmem_spec()] * len(pieces),
        out_specs=vmem_spec(),
        compiler_params=pltpu.CompilerParams(vmem_limit_bytes=VMEM_LIMIT),
        name="early_sum",
    )(*pieces)


def relay_kernel(groups, peers, slots, scalars, *refs):
    pieces, (dense, small) = refs[:-2], refs[-2:]
    width = dense.shape[1]
    cols = width // groups
    inner_at, point_at, small_at, _ = dense_rows(width, groups, peers)
    sums, total = add_pieces(placed(pieces, scalars[slots + 1]), small, groups, peers, True)
    dense[0:cols, :] = sums[0].astype(low)
    dense[inner_at : inner_at + cols, :] = sums[2].astype(low)
    dense[point_at : point_at + cols // peers, :] = sums[3].astype(low)
    dense[small_at : small_at + EXTRA, :] = total.astype(low)


def relay_call(groups, peers, slots, scalars, pieces):
    width = pieces[0].shape[1]
    count = dense_rows(width, groups, peers)[3]
    return pl.pallas_call(
        functools.partial(relay_kernel, groups, peers, slots),
        out_shape=jax.ShapeDtypeStruct((count, width), low),
        in_specs=[pl.BlockSpec(memory_space=pltpu.SMEM)] + [vmem_spec()] * len(pieces),
        out_specs=vmem_spec(),
        scratch_shapes=[pltpu.VMEM((len(pieces), EXTRA, width), wide)],
        compiler_params=pltpu.CompilerParams(vmem_limit_bytes=VMEM_LIMIT),
        name="relay_sum",
    )(scalars, *pieces)


def write_block(outs, at, sums, points, total, groups, peers):
    (proj, out, f_in, f_out, point, depth, gain, shift) = outs
    width = total.shape[1]
    cols = width // groups
    own = width // peers
    hidden_cols = f_in.shape[2]
    share = [1.0 / total[TAPS + 2 + op : TAPS + 3 + op, :] for op in range(3)]
    attn = sums[0] * share[0]
    for j in range(3):
        proj[at, j] = attn[:, j * own : (j + 1) * own].T
    out[at] = attn[:, 3 * own :].T
    f_out[at] = sums[1] * share[2]
    inner = sums[2] * share[2]
    for p in range(own // cols):
        f_in[at, p * cols : (p + 1) * cols, :] = inner[:, p * hidden_cols : (p + 1) * hidden_cols]
    points = points * share[1]
    points = jnp.concatenate([points[:, p * own : (p + 1) * own] for p in range(peers)], axis=0)
    point[at] = points.T
    depth[:, at, :] = total[0:TAPS] * share[1]
    gain[at : at + 1, :] = total[TAPS : TAPS + 1] * (1.0 / groups)
    shift[at : at + 1, :] = total[TAPS + 1 : TAPS + 2] * (1.0 / groups)


def direct_kernel(groups, peers, every, *refs):
    outs, small = refs[:-1], refs[-1]
    pieces = [(d, every.at[d]) for d in range(groups)]
    sums, total = add_pieces(pieces, small, groups, peers, False)
    write_block(outs, 0, sums, sums[3], total, groups, peers)


def final_kernel(groups, peers, slots, scalars, *refs):
    half = groups // 2
    near, early, (early_dense, dense) = refs[:half], refs[half : 2 * half], refs[2 * half : 2 * half + 2]
    done = refs[2 * half + 2 : 2 * half + 10]
    outs, small = refs[2 * half + 10 : -1], refs[-1]
    width = dense.shape[1]
    cols = width // groups
    inner_at, point_at, small_at, _ = dense_rows(width, groups, peers)
    sums, total = add_pieces(placed(near, scalars[slots + 1]), small, groups, peers, True)
    total = total.astype(low).astype(wide)
    total = total + dense[small_at : small_at + EXTRA, :].astype(wide)
    sums[0] = sums[0] + dense[0:cols, :].astype(wide)
    sums[1] = early_dense[0:cols, :].astype(wide)
    for piece in early:
        sums[1] = sums[1] + piece[1, 0:cols, :].astype(wide)
    sums[2] = sums[2] + dense[inner_at : inner_at + cols, :].astype(wide)
    points = sums[3] + dense[point_at : point_at + cols // peers, :].astype(wide)
    write_block(outs, 0, sums, points, total, groups, peers)
    for index, (source, target) in enumerate(zip(done, outs)):
        if index < 5:
            target[1] = source[0]
        elif index == 5:
            target[:, 1, :] = source[:, 0, :]
        else:
            target[1:2, :] = source[...]


def out_shapes(blocks, width, hidden, groups, peers):
    rows, cols = width // peers, width // groups
    shapes = [
        (blocks, 3, rows, cols),
        (blocks, rows, cols),
        (blocks, rows, hidden // groups),
        (blocks, cols, hidden // peers),
        (blocks, rows, cols),
        (TAPS, blocks, width),
        (blocks, width),
        (blocks, width),
    ]
    return [jax.ShapeDtypeStruct(s, wide) for s in shapes]


def direct_call(groups, peers, hidden, every):
    width = every.shape[-1]
    shapes = out_shapes(1, width, hidden, groups, peers)
    return pl.pallas_call(
        functools.partial(direct_kernel, groups, peers),
        out_shape=shapes,
        in_specs=[vmem_spec()],
        out_specs=[vmem_spec()] * len(shapes),
        scratch_shapes=[pltpu.VMEM((groups, EXTRA, width), wide)],
        compiler_params=pltpu.CompilerParams(vmem_limit_bytes=VMEM_LIMIT),
        name="direct_sum",
    )(every)


def final_call(groups, peers, slots, hidden, scalars, inputs):
    width = inputs[0].shape[-1]
    shapes = out_shapes(BLOCKS, width, hidden, groups, peers)
    return pl.pallas_call(
        functools.partial(final_kernel, groups, peers, slots),
        out_shape=shapes,
        in_specs=[pl.BlockSpec(memory_space=pltpu.SMEM)] + [vmem_spec()] * len(inputs),
        out_specs=[vmem_spec()] * len(shapes),
        scratch_shapes=[pltpu.VMEM((groups // 2, EXTRA, width), wide)],
        compiler_params=pltpu.CompilerParams(vmem_limit_bytes=VMEM_LIMIT),
        name="final_sum",
    )(scalars, *inputs)


def across(piece, axis, key):
    return lax.ppermute(piece, axis, [(i, i ^ key) for i in range(lax.axis_size(axis))])


def local(
    layer_in,
    lengths,
    op_ids,
    kernel_ids,
    attn_proj,
    attn_out,
    ffn_in,
    ffn_out,
    point_weights,
    depth_weights,
    norm_gains,
    norm_shifts,
    cotangent,
):
    slots, span, width = layer_in.shape
    peers = lax.axis_size("seq")
    groups = lax.axis_size("dp")
    place = lax.axis_index("seq").astype(jnp.int32)
    length = span * peers
    weights = (attn_proj, attn_out, ffn_in, ffn_out, point_weights)

    me = lax.axis_index("dp").astype(jnp.int32)
    half = groups // 2

    chosen = jnp.stack([op_ids[0], kernel_ids[0]], axis=1).reshape(-1)
    scalars = jnp.concatenate([lengths, jnp.stack([place, me]), chosen])
    depth_weights = jnp.swapaxes(depth_weights, 0, 1)

    later = cotangent.astype(low)
    parts = {0: layer_in.astype(low)}
    reach = peers // 2
    while reach:
        moved = {key ^ reach: across(part, "seq", reach) for key, part in parts.items()}
        if reach == peers // 2:
            moved, later, scalars = lax.optimization_barrier((moved, later, scalars))
        parts.update(moved)
        reach //= 2
    x_parts = [parts[key] for key in range(peers)]
    later, x_parts = lax.optimization_barrier((later, x_parts))
    cot_parts = [later] + [across(later, "seq", key) for key in range(1, peers)]
    layer_out, *saved = forward_call(
        slots, length, peers, scalars, x_parts, weights, depth_weights, norm_gains, norm_shifts
    )

    g, payload = backward_call(
        1, slots, length, peers, groups, scalars, cot_parts, saved, weights, depth_weights, norm_gains
    )
    every = lax.all_to_all(payload, "dp", 0, 0, tiled=True)
    grad, rounded, small, *early = norm_call(
        slots, length, peers, groups, scalars, g, saved, norm_gains
    )
    early = [early[0]] + [across(early[key], "dp", key) for key in range(1, half)]
    g, *sent = backward_call(
        0, slots, length, peers, groups, scalars, [grad, rounded, small], saved, weights,
        depth_weights, norm_gains,
    )
    early, g = lax.optimization_barrier((early, g))
    early_sum = early_call(early)
    early_dense = across(early_sum, "dp", half)
    far = [sent[half]] + [across(sent[half + key], "dp", key) for key in range(1, half)]
    far, _ = lax.optimization_barrier((far, early_sum))
    partial = relay_call(groups, peers, slots, scalars, far)
    rest, partial = lax.optimization_barrier((sent[:half], partial))
    dense = across(partial, "dp", half)
    near = [rest[0]] + [across(rest[key], "dp", key) for key in range(1, half)]
    every, _ = lax.optimization_barrier((every, partial))
    done = direct_call(groups, peers, ffn_in.shape[2], every)
    proj, out, f_in, f_out, point, depth, gain, shift = final_call(
        groups, peers, slots, ffn_in.shape[2], scalars, near + early + [early_dense, dense] + list(done)
    )
    f_out = jnp.swapaxes(f_out, 1, 2)
    depth = jnp.swapaxes(depth, 0, 1)
    return (layer_out, g, proj, out, f_in, f_out, point, depth, gain, shift)


def solution(mesh):
    placed = (
        P("dp", "seq", None),
        P("dp"),
        P("dp", None),
        P("dp", None),
        P(),
        P(),
        P(),
        P(),
        P(),
        P(),
        P(),
        P(),
        P("dp", "seq", None),
    )
    return jax.shard_map(
        local,
        mesh=mesh,
        in_specs=placed,
        out_specs=(
            P("dp", "seq", None),
            P("dp", "seq", None),
            P(None, None, "seq", "dp"),
            P(None, "seq", "dp"),
            P(None, "seq", "dp"),
            P(None, "seq", "dp"),
            P(None, "seq", "dp"),
            P(),
            P(),
            P(),
        ),
        check_vma=False,
    )
```
